128 devices in a mesh: dp: 16 (over y, z_lo, core), branch: 8 (over x, z_hi).
Axes of the slice: x: 4, y: 4, z: 4 (z_hi: 2, z_lo: 2; z = z_hi * 2 + z_lo), core: 2. Of those that a mesh axis runs over, the one named last changes fastest.
Arguments:
- image_hidden: bfloat16 [16384, 1024], P('dp', 'branch'), may hold values from -8 to 8
- text_hidden: bfloat16 [16384, 768], P('dp', 'branch'), may hold values from -8 to 8
- image_proj: bfloat16 [1024, 768], replicated, may hold values from -0.1875 to 0.1875
- text_proj: bfloat16 [768, 768], replicated, may hold values from -0.21650635 to 0.21650635
- log_inverse_sharpness: float32 [1], replicated, may hold values from 4 to 5.9
- partner: int32 [16384], replicated, may hold values from 0 to 16383, each once
Outputs:
- loss: float32 [1], replicated
- grad_log_scale: float32 [1], replicated
- grad_image_hidden: bfloat16 [16384, 1024], P('dp', 'branch')
- grad_text_hidden: bfloat16 [16384, 768], P('dp', 'branch')
- grad_image_proj: float32 [1024, 768], P('branch')
- grad_text_proj: float32 [768, 768], P('branch')
The draws below stay inside these ranges and needn't reach their ends.
Inputs may be any that keep to these rules, and one draw needn't show every extreme that they name: `partner`: each text index appears exactly once.
All inputs are finite; a program needn't handle non-finite values.
Results may differ from the reference program's by a relative error of at most 0.0029.
The reference program's roundings to bfloat16 on the way count: a program that leaves them out, or rounds other values in their place, can miss the bound.
Values may be sent and summed in bfloat16 or wider, within the bound.
No kernel may reach another device: no remote copies, remote signals or barrier semaphores. Data moves between devices by JAX's collectives and lax.ppermute only.
A program may use at most 64 MiB of HBM per device.

```python
import jax
import jax.numpy as jnp
from jax import lax

IMG_WIDTH = 1024
TXT_WIDTH = 768
EMBED = 768
PAIRS = 16384
N_DP = 16


def joint_draw(key):
    streams = jax.random.split(jax.random.fold_in(key, 7), 4)
    image_proj = jax.random.truncated_normal(streams[0], -6.0, 6.0, (IMG_WIDTH, EMBED), jnp.float32) * IMG_WIDTH ** (-0.5)
    text_proj = jax.random.truncated_normal(streams[1], -6.0, 6.0, (TXT_WIDTH, EMBED), jnp.float32) * TXT_WIDTH ** (-0.5)
    image_hidden = jax.random.truncated_normal(streams[2], -6.0, 6.0, (PAIRS, IMG_WIDTH), jnp.float32)
    text_hidden = jax.random.truncated_normal(streams[3], -6.0, 6.0, (PAIRS, TXT_WIDTH), jnp.float32)
    image_hidden = jnp.clip(image_hidden, -8.0, 8.0)
    text_hidden = jnp.clip(text_hidden, -8.0, 8.0)
    return (image_hidden, text_hidden, image_proj, text_proj)


def draw_image_hidden(key, part):
    return joint_draw(key)[0].astype(jnp.bfloat16)


def draw_text_hidden(key, part):
    return joint_draw(key)[1].astype(jnp.bfloat16)


def draw_image_proj(key, part):
    return joint_draw(key)[2].astype(jnp.bfloat16)


def draw_text_proj(key, part):
    return joint_draw(key)[3].astype(jnp.bfloat16)


def draw_log_inverse_sharpness(key, part):
    stream = jax.random.fold_in(key, 11)
    return jax.random.uniform(stream, (1,), jnp.float32, 4.0, 5.9)


def setup_inputs(seed: int = 0) -> dict:
    keys = jax.random.split(jax.random.key(seed), 7)
    image_hidden = draw_image_hidden(jax.random.fold_in(keys[6], 71), 0)
    text_hidden = draw_text_hidden(jax.random.fold_in(keys[6], 71), 0)
    image_proj = draw_image_proj(jax.random.fold_in(keys[6], 71), 0)
    text_proj = draw_text_proj(jax.random.fold_in(keys[6], 71), 0)
    log_inverse_sharpness = draw_log_inverse_sharpness(jax.random.fold_in(keys[6], 71), 0)
    partner = jax.random.permutation(keys[5], PAIRS).astype(jnp.int32)
    return dict(image_hidden=image_hidden, text_hidden=text_hidden, image_proj=image_proj, text_proj=text_proj, log_inverse_sharpness=log_inverse_sharpness, partner=partner)


NORM_EPSILON = 1e-06

def normalize(raw_rows):
    lengths = jnp.sqrt(lax.optimization_barrier(jnp.sum(raw_rows * raw_rows, axis=1, keepdims=True)) + NORM_EPSILON)
    unit_rows = raw_rows / lengths
    return (unit_rows, lengths, unit_rows.astype(jnp.bfloat16))

def unnormalize(upstream, unit_rows, lengths):
    radial = lax.optimization_barrier(jnp.sum(upstream * unit_rows, axis=1, keepdims=True))
    return ((upstream - unit_rows * radial) / lengths).astype(jnp.bfloat16)

def reference(image_hidden, text_hidden, image_proj, text_proj, log_inverse_sharpness, partner):
    total_pairs = image_hidden.shape[0]
    image_raw = jnp.dot(image_hidden.astype(jnp.float32), image_proj.astype(jnp.float32), preferred_element_type=jnp.float32)
    text_raw = jnp.dot(text_hidden.astype(jnp.float32), text_proj.astype(jnp.float32), preferred_element_type=jnp.float32)
    image_unit, image_length, image_emb = normalize(image_raw)
    text_unit, text_length, caption_feature_entries = normalize(text_raw)
    normalized_exponent_divisor = jnp.exp(log_inverse_sharpness[0])
    block_rows = total_pairs // N_DP
    image_blocks = image_emb.reshape(N_DP, block_rows, -1)
    partner_blocks = partner.reshape(N_DP, block_rows)
    column_ids = jnp.arange(total_pairs, dtype=jnp.int32)
    denominator = 2.0 * total_pairs

    def block_logits(sample_feature_entries):
        return normalized_exponent_divisor * lax.dot_general(sample_feature_entries.astype(jnp.float32), caption_feature_entries.astype(jnp.float32), (((1,), (1,)), ((), ())), preferred_element_type=jnp.float32)

    def forward(carried, item):
        column_peak, column_mass = carried
        sample_feature_entries, rows_partner = item
        matching_cosine_scores = block_logits(sample_feature_entries)
        row_peak = lax.optimization_barrier(jnp.max(matching_cosine_scores, axis=1))
        row_lse = row_peak + jnp.log(lax.optimization_barrier(jnp.sum(jnp.exp(matching_cosine_scores - row_peak[:, None]), axis=1)))
        matched = rows_partner[:, None] == column_ids[None, :]
        positive = lax.optimization_barrier(jnp.sum(jnp.where(matched, matching_cosine_scores, 0.0), axis=1))
        new_peak = jnp.maximum(column_peak, lax.optimization_barrier(jnp.max(matching_cosine_scores, axis=0)))
        column_mass = column_mass * jnp.exp(column_peak - new_peak) + lax.optimization_barrier(jnp.sum(jnp.exp(matching_cosine_scores - new_peak[None, :]), axis=0))
        return ((new_peak, column_mass), (row_lse, positive))
    start_peak = jnp.full((total_pairs,), -jnp.inf, jnp.float32)
    start_mass = jnp.zeros((total_pairs,), jnp.float32)
    (column_peak, column_mass), (row_lse, positive) = lax.scan(forward, (start_peak, start_mass), (image_blocks, partner_blocks))
    col_lse = column_peak + jnp.log(column_mass)
    loss = (jnp.sum(row_lse) + jnp.sum(col_lse) - 2.0 * jnp.sum(positive)) / denominator

    def backward(carried, item):
        caption_objective_sum, scale_total = carried
        sample_feature_entries, rows_partner, rows_lse = item
        matching_cosine_scores = block_logits(sample_feature_entries)
        matched = (rows_partner[:, None] == column_ids[None, :]).astype(jnp.float32)
        weights = (jnp.exp(matching_cosine_scores - rows_lse[:, None]) + jnp.exp(matching_cosine_scores - col_lse[None, :]) - 2.0 * matched) / denominator
        scale_total = scale_total + jnp.sum(weights * matching_cosine_scores)
        reduced_width_parameters = weights.astype(jnp.bfloat16)
        picture_projection_matrix = normalized_exponent_divisor * jnp.dot(reduced_width_parameters.astype(jnp.float32), caption_feature_entries.astype(jnp.float32), preferred_element_type=jnp.float32)
        caption_objective_sum = caption_objective_sum + normalized_exponent_divisor * lax.dot_general(reduced_width_parameters.astype(jnp.float32), sample_feature_entries.astype(jnp.float32), (((0,), (0,)), ((), ())), preferred_element_type=jnp.float32)
        return ((caption_objective_sum, scale_total), picture_projection_matrix)
    start_text = jnp.zeros((total_pairs, caption_feature_entries.shape[1]), jnp.float32)
    start_scale = jnp.zeros((), jnp.float32)
    (text_up, scale_grad), picture_projection_matrix = lax.scan(backward, (start_text, start_scale), (image_blocks, partner_blocks, row_lse))
    picture_projection_matrix = picture_projection_matrix.reshape(total_pairs, -1)
    image_down = unnormalize(picture_projection_matrix, image_unit, image_length)
    text_down = unnormalize(text_up, text_unit, text_length)
    grad_image_hidden = jnp.dot(image_down.astype(jnp.float32), image_proj.T.astype(jnp.float32), preferred_element_type=jnp.float32).astype(jnp.bfloat16)
    grad_text_hidden = jnp.dot(text_down.astype(jnp.float32), text_proj.T.astype(jnp.float32), preferred_element_type=jnp.float32).astype(jnp.bfloat16)
    grad_image_proj = jnp.dot(image_hidden.T.astype(jnp.float32), image_down.astype(jnp.float32), preferred_element_type=jnp.float32)
    grad_text_proj = jnp.dot(text_hidden.T.astype(jnp.float32), text_down.astype(jnp.float32), preferred_element_type=jnp.float32)
    return (loss.reshape(1), scale_grad.reshape(1), grad_image_hidden, grad_text_hidden, grad_image_proj, grad_text_proj)
```

```python
import jax
import jax.numpy as jnp
import numpy as np
from jax import lax
from jax.sharding import Mesh
from jax.sharding import PartitionSpec as P

SIZES = {"y": 4, "zl": 2, "c": 2, "x": 4, "zh": 2}
AXES = tuple(SIZES)
DP = ("y", "zl", "c")
PLANE = ("y", "zl")
BRANCH = ("x", "zh")

NORM_EPSILON = 1e-06
FULL_SCALE = 32000.0
BF = jnp.bfloat16
F32 = jnp.float32


def moved(value, axes, target):
    sizes = [SIZES[a] for a in axes]
    pairs = []
    for i in range(int(np.prod(sizes))):
        at = tuple(int(v) for v in np.unravel_index(i, sizes))
        pairs.append((i, int(np.ravel_multi_index(target(*at), sizes))))
    return lax.ppermute(value, axes, pairs)


def swapped(value, axis, mask=1):
    return moved(value, (axis,), lambda i: (i ^ mask,))


def rounds(rows, exponent):
    return jnp.round(rows * (FULL_SCALE * jnp.exp2(-exponent))).astype(jnp.int16)


def coded(rows, blocks):
    count, width = rows.shape
    r = count // blocks
    top = jnp.max(jnp.abs(rows), axis=1)
    exponent = jnp.maximum(jnp.ceil(jnp.log2(top)), -80.0)
    fixed = rounds(rows, exponent[:, None]).reshape(blocks, r, width)
    tail = jnp.pad(exponent.reshape(blocks, 1, r), ((0, 0), (0, 7), (0, width - r)))
    return jnp.concatenate([fixed, tail.astype(jnp.int16)], axis=1)


def decoded(blocks):
    r = blocks.shape[-2] - 8
    exponent = blocks[..., r, :r].astype(F32)
    return blocks[..., :r, :].astype(F32) * (jnp.exp2(exponent) / FULL_SCALE)[..., None]


def normalize(raw_rows):
    lengths = jnp.sqrt(jnp.sum(raw_rows * raw_rows, axis=1, keepdims=True) + NORM_EPSILON)
    unit_rows = raw_rows / lengths
    return (unit_rows, lengths, unit_rows.astype(BF))


def unnormalize(upstream, unit_rows, lengths):
    radial = jnp.sum(upstream * unit_rows, axis=1, keepdims=True)
    return ((upstream - unit_rows * radial) / lengths).astype(BF)


def per_device(image_hidden, text_hidden, image_proj, text_proj, log_inverse_sharpness, partner):
    y, zl, c, x, zh = (lax.axis_index(a) for a in AXES)
    branch_pos = x * 2 + zh
    data_pos = (y * 2 + zl) * 2 + c
    group_rows, image_slab = image_hidden.shape
    text_slab = text_hidden.shape[1]
    own_rows = group_rows // 8
    embed = image_proj.shape[1]
    total_pairs = group_rows * 16
    denominator = 2.0 * total_pairs
    scale = jnp.exp(log_inverse_sharpness[0])

    other_slab = swapped(image_hidden, "zh")
    text_local = lax.all_to_all(text_hidden, BRANCH, split_axis=0, concat_axis=1, tiled=True)
    pair = jnp.where(
        zh == 0,
        jnp.concatenate([image_hidden, other_slab], axis=1),
        jnp.concatenate([other_slab, image_hidden], axis=1),
    )
    far = [moved(pair, ("x",), lambda i, k=k: ((i + k) % 4,)) for k in (2, 1, 3)]
    text_raw = jnp.dot(text_local, text_proj, preferred_element_type=F32)
    text_unit, text_length, text_emb = normalize(text_raw)
    near_text = lax.all_to_all(
        jnp.broadcast_to(text_emb[None], (8, own_rows, embed)), PLANE, 0, 0, tiled=True
    ).reshape(8 * own_rows, embed)
    column_emb = jnp.concatenate([near_text, swapped(near_text, "c")], axis=0)

    hidden_full = jnp.zeros((group_rows, 8 * image_slab), BF)
    for k, block in ((0, pair), (2, far[0]), (1, far[1]), (3, far[2])):
        hidden_full = lax.dynamic_update_slice(
            hidden_full, block, (0, lax.rem(x + 4 - k, 4) * 2 * image_slab)
        )
    image_raw = jnp.dot(hidden_full, image_proj, preferred_element_type=F32)
    group_unit, group_length, group_emb = normalize(image_raw)
    image_unit = lax.dynamic_slice_in_dim(group_unit, branch_pos * own_rows, own_rows, 0)
    image_length = lax.dynamic_slice_in_dim(group_length, branch_pos * own_rows, own_rows, 0)

    text_columns, group_emb, column_emb = lax.optimization_barrier(
        (text_hidden.T, group_emb, column_emb)
    )
    text_full = lax.all_gather(text_columns, BRANCH, axis=0, tiled=True)

    logits = scale * lax.dot_general(
        group_emb, column_emb, (((1,), (1,)), ((), ())), preferred_element_type=F32
    )
    column_count = logits.shape[1]
    position = jnp.arange(column_count, dtype=jnp.int32)
    core = jnp.bitwise_xor(position // (8 * own_rows), c)
    block = position % (8 * own_rows) // own_rows
    column_ids = ((block * 2 + core) * 8 + branch_pos) * own_rows + position % own_rows
    row_partner = lax.dynamic_slice_in_dim(partner, data_pos * group_rows, group_rows, 0)
    matched = row_partner[:, None] == column_ids[None, :]
    positive = jnp.sum(jnp.where(matched, logits, 0.0), axis=1)
    row_peak = jnp.max(logits, axis=1)
    row_mass = jnp.sum(jnp.exp(logits - row_peak[:, None]), axis=1)
    col_peak = jnp.max(logits, axis=0)
    col_mass = jnp.sum(jnp.exp(logits - col_peak[None, :]), axis=0)

    def joined(mine, theirs):
        peak = jnp.maximum(mine[0], theirs[0])
        mass = mine[1] * jnp.exp(mine[0] - peak) + theirs[1] * jnp.exp(theirs[0] - peak)
        return jnp.stack([peak, mass, *(mine[2:] + theirs[2:])])

    row_stats = jnp.stack([row_peak, row_mass, positive])
    col_stats = jnp.stack([col_peak, col_mass])
    theirs = swapped(col_stats, "c").reshape(2, 2, -1)[:, ::-1].reshape(2, -1)
    col_stats = joined(col_stats, theirs)
    for row_step, col_step in ((("x", 1), ("y", 1)), (("x", 2), ("y", 2)), (("zh", 1), ("zl", 1))):
        row_in = swapped(row_stats, *row_step)
        col_in = swapped(col_stats, *col_step)
        row_stats, col_stats = joined(row_stats, row_in), joined(col_stats, col_in)
    row_lse = row_stats[0] + jnp.log(row_stats[1])
    positive = row_stats[2]
    col_lse = col_stats[0] + jnp.log(col_stats[1])

    weights = (
        jnp.exp(logits - row_lse[:, None])
        + jnp.exp(logits - col_lse[None, :])
        - 2.0 * matched.astype(F32)
    ) / denominator
    scale_part = jnp.sum(weights * logits)
    weights_low = weights.astype(BF)

    def text_part(half):
        return scale * lax.dot_general(
            half, group_emb, (((0,), (0,)), ((), ())), preferred_element_type=F32
        )

    half = column_count // 2
    text_other = swapped(text_part(weights_low[:, half:]), "c")
    text_sum = text_part(weights_low[:, :half]) + text_other
    text_fixed = coded(text_sum, 8)
    image_fixed = coded(
        scale * jnp.dot(weights_low, column_emb, preferred_element_type=F32), 8
    )
    text_up = lax.dynamic_slice_in_dim(text_sum, (y * 2 + zl) * own_rows, own_rows, 0)
    arrivals = []
    for dy, dz in ((2, 1), (2, 0), (1, 1), (3, 1), (1, 0), (3, 0), (0, 1)):
        index = lax.rem(y + dy, 4) * 2 + lax.rem(zl + dz, 2)
        piece = lax.dynamic_slice_in_dim(text_fixed, index, 1, 0)
        arrivals.append(
            moved(piece, PLANE, lambda i, j, a=dy, b=dz: ((i + a) % 4, (j + b) % 2))
        )
    image_blocks = lax.all_to_all(image_fixed, BRANCH, 0, 0, tiled=True)
    image_up = jnp.sum(decoded(image_blocks), axis=0)
    text_up = text_up + sum(decoded(piece[0]) for piece in arrivals)

    image_down = unnormalize(image_up, image_unit, image_length)
    text_down = unnormalize(text_up, text_unit, text_length)
    image_grad = lax.dot_general(
        image_down, image_proj, (((1,), (1,)), ((), ())), preferred_element_type=F32
    ).astype(BF)
    text_grad = lax.dot_general(
        text_down, text_proj, (((1,), (1,)), ((), ())), preferred_element_type=F32
    ).astype(BF)

    def by_column(rows):
        return jnp.swapaxes(rows.reshape(own_rows, 8, -1), 0, 1)

    sent = [by_column(a) for a in (image_grad, text_grad, image_down, text_down)]
    got = lax.all_to_all(jnp.concatenate(sent, axis=2), BRANCH, 0, 0, tiled=True)
    got = got.reshape(group_rows, -1)
    cuts = np.cumsum([a.shape[2] for a in sent])
    grad_image_hidden = got[:, : cuts[0]]
    grad_text_hidden = got[:, cuts[0] : cuts[1]]
    image_weight = lax.dot_general(
        hidden_full, got[:, cuts[1] : cuts[2]], (((0,), (0,)), ((), ())), preferred_element_type=F32
    )
    text_weight = jnp.dot(text_full, got[:, cuts[2] : cuts[3]], preferred_element_type=F32)

    own_row_terms = lax.dynamic_slice_in_dim(
        row_lse - 2.0 * positive, branch_pos * own_rows, own_rows, 0
    )
    own_col_terms = lax.dynamic_slice_in_dim(col_lse, (y * 2 + zl) * own_rows, own_rows, 0)
    loss_part = (jnp.sum(own_row_terms) + jnp.sum(own_col_terms)) / denominator
    width = image_weight.shape[1]
    scalars = jnp.pad(jnp.stack([loss_part, scale_part])[:, None], ((0, 6), (0, width - 1)))
    partial = jnp.concatenate(
        [
            image_weight.reshape(16, -1, width),
            text_weight.reshape(16, -1, width),
            jnp.broadcast_to(scalars[None], (16, 8, width)),
        ],
        axis=1,
    )
    summed = jnp.sum(lax.all_to_all(partial, DP, 0, 0, tiled=True), axis=0)
    turned = moved(summed, AXES, lambda a, b, core, d, e: (d, e, core, a, b))
    whole = lax.all_to_all(
        jnp.broadcast_to(turned[None], (16, *turned.shape)), DP, 0, 0, tiled=True
    )

    def slab(first, rows):
        part = whole[:, first : first + rows].reshape(8, 2, rows, width)
        return part.transpose(1, 2, 0, 3).reshape(2 * rows, 8 * width)

    image_rows, text_rows = image_slab // 2, text_slab // 2
    totals = jnp.sum(whole[::2, image_rows + text_rows :, 0], axis=0)
    return (
        totals[0].reshape(1),
        totals[1].reshape(1),
        grad_image_hidden,
        grad_text_hidden,
        slab(0, image_rows),
        slab(image_rows, text_rows),
    )


def solution(mesh):
    torus = Mesh(mesh.devices.reshape(tuple(SIZES.values())), AXES)
    placed = (P(DP, BRANCH), P(DP, BRANCH), P(), P(), P(), P())
    return jax.shard_map(
        per_device,
        mesh=torus,
        in_specs=placed,
        out_specs=(P(), P(), P(DP, BRANCH), P(DP, BRANCH), P(BRANCH, None), P(BRANCH, None)),
        check_vma=False,
    )
```

```python
import jax
import jax.numpy as jnp
import numpy as np
from jax import lax
from jax.sharding import Mesh
from jax.sharding import PartitionSpec as P

SIZES = {"y": 4, "zl": 2, "c": 2, "x": 4, "zh": 2}
AXES = tuple(SIZES)
DP = ("y", "zl", "c")
PLANE = ("y", "zl")
BRANCH = ("x", "zh")

NORM_EPSILON = 1e-06
FULL_SCALE = 32000.0
BF = jnp.bfloat16
F32 = jnp.float32


def moved(value, axes, target):
    sizes = [SIZES[a] for a in axes]
    pairs = []
    for i in range(int(np.prod(sizes))):
        at = tuple(int(v) for v in np.unravel_index(i, sizes))
        pairs.append((i, int(np.ravel_multi_index(target(*at), sizes))))
    return lax.ppermute(value, axes, pairs)


def swapped(value, axis, mask=1):
    return moved(value, (axis,), lambda i: (i ^ mask,))


def paired(own, other, side):
    return jnp.where(
        side == 0,
        jnp.concatenate([own, other], axis=1),
        jnp.concatenate([other, own], axis=1),
    )


def stacked(own, other, side):
    return jnp.where(side == 0, jnp.concatenate([own, other]), jnp.concatenate([other, own]))


def rounds(rows, exponent):
    return jnp.round(rows * (FULL_SCALE * jnp.exp2(-exponent))).astype(jnp.int16)


def coded(rows, blocks):
    count, width = rows.shape
    r = count // blocks
    top = jnp.max(jnp.abs(rows), axis=1)
    exponent = jnp.maximum(jnp.ceil(jnp.log2(top)), -80.0)
    fixed = rounds(rows, exponent[:, None]).reshape(blocks, r, width)
    tail = jnp.pad(exponent.reshape(blocks, 1, r), ((0, 0), (0, 7), (0, width - r)))
    return jnp.concatenate([fixed, tail.astype(jnp.int16)], axis=1)


def decoded(blocks):
    r = blocks.shape[-2] - 8
    exponent = blocks[..., r, :r].astype(F32)
    return blocks[..., :r, :].astype(F32) * (jnp.exp2(exponent) / FULL_SCALE)[..., None]


def normalize(raw_rows):
    lengths = jnp.sqrt(jnp.sum(raw_rows * raw_rows, axis=1, keepdims=True) + NORM_EPSILON)
    unit_rows = raw_rows / lengths
    return (unit_rows, lengths, unit_rows.astype(BF))


def unnormalize(upstream, unit_rows, lengths):
    radial = jnp.sum(upstream * unit_rows, axis=1, keepdims=True)
    return ((upstream - unit_rows * radial) / lengths).astype(BF)


def per_device(image_hidden, text_hidden, image_proj, text_proj, log_inverse_sharpness, partner):
    y, zl, c, x, zh = (lax.axis_index(a) for a in AXES)
    branch_pos = x * 2 + zh
    data_pos = (y * 2 + zl) * 2 + c
    group_rows, image_slab = image_hidden.shape
    text_slab = text_hidden.shape[1]
    own_rows = group_rows // 8
    embed = image_proj.shape[1]
    total_pairs = group_rows * 16
    denominator = 2.0 * total_pairs
    scale = jnp.exp(log_inverse_sharpness[0])

    image_pair = paired(image_hidden, swapped(image_hidden, "zh"), zh)
    text_pair = paired(text_hidden, swapped(text_hidden, "zh"), zh)
    text_blocks = text_pair.reshape(4, 2, own_rows, 2 * text_slab)
    text_blocks = lax.dynamic_index_in_dim(text_blocks, zh, 1, keepdims=False)

    def turned_by(rows, width):
        return lax.dynamic_slice_in_dim(jnp.concatenate([rows, rows]), x * width, 4 * width, 0)

    def from_x(send):
        arrived = [moved(send(k), ("x",), lambda i, k=k: ((i + k) % 4,)) for k in (3, 2, 1)]
        return jnp.concatenate([send(0), *arrived], axis=1)

    text_local = from_x(
        lambda k: lax.dynamic_index_in_dim(text_blocks, lax.rem(x + k, 4), 0, keepdims=False)
    )
    text_raw = jnp.dot(
        text_local, turned_by(text_proj, 2 * text_slab), preferred_element_type=F32
    )
    text_unit, text_length, text_emb = normalize(text_raw)
    near_text = lax.all_to_all(
        jnp.broadcast_to(text_emb[None], (8, own_rows, embed)), PLANE, 0, 0, tiled=True
    ).reshape(8 * own_rows, embed)
    column_emb = jnp.concatenate([near_text, swapped(near_text, "c")], axis=0)

    hidden_full = from_x(lambda k: image_pair)
    image_raw = jnp.dot(
        hidden_full, turned_by(image_proj, 2 * image_slab), preferred_element_type=F32
    )
    group_unit, group_length, group_emb = normalize(image_raw)
    image_unit = lax.dynamic_slice_in_dim(group_unit, branch_pos * own_rows, own_rows, 0)
    image_length = lax.dynamic_slice_in_dim(group_length, branch_pos * own_rows, own_rows, 0)

    text_pair, _ = lax.optimization_barrier((text_pair, hidden_full))
    text_full = from_x(lambda k: text_pair)

    logits = scale * lax.dot_general(
        group_emb, column_emb, (((1,), (1,)), ((), ())), preferred_element_type=F32
    )
    column_count = logits.shape[1]
    position = jnp.arange(column_count, dtype=jnp.int32)
    core = jnp.bitwise_xor(position // (8 * own_rows), c)
    block = position % (8 * own_rows) // own_rows
    column_ids = ((block * 2 + core) * 8 + branch_pos) * own_rows + position % own_rows
    row_partner = lax.dynamic_slice_in_dim(partner, data_pos * group_rows, group_rows, 0)
    matched = row_partner[:, None] == column_ids[None, :]
    positive_part = jnp.sum(jnp.where(matched, logits, 0.0))
    row_peak = jnp.max(logits, axis=1)
    row_mass = jnp.sum(jnp.exp(logits - row_peak[:, None]), axis=1)
    col_peak = jnp.max(logits, axis=0)
    col_mass = jnp.sum(jnp.exp(logits - col_peak[None, :]), axis=0)

    def joined(mine, theirs):
        peak = jnp.maximum(mine[0], theirs[0])
        mass = mine[1] * jnp.exp(mine[0] - peak) + theirs[1] * jnp.exp(theirs[0] - peak)
        return jnp.stack([peak, mass])

    row_stats = jnp.stack([row_peak, row_mass])
    col_stats = jnp.stack([col_peak, col_mass])
    theirs = swapped(col_stats, "c").reshape(2, 2, -1)[:, ::-1].reshape(2, -1)
    col_stats = joined(col_stats, theirs)
    for row_step, col_step in ((("x", 1), ("y", 1)), (("x", 2), ("y", 2)), (("zh", 1), ("zl", 1))):
        row_in = swapped(row_stats, *row_step)
        col_in = swapped(col_stats, *col_step)
        row_stats, col_stats = joined(row_stats, row_in), joined(col_stats, col_in)
    row_lse = row_stats[0] + jnp.log(row_stats[1])
    col_lse = col_stats[0] + jnp.log(col_stats[1])

    weights = (
        jnp.exp(logits - row_lse[:, None])
        + jnp.exp(logits - col_lse[None, :])
        - 2.0 * matched.astype(F32)
    ) / denominator
    scale_part = jnp.sum(weights * logits)
    weights_low = weights.astype(BF)

    def text_part(half):
        return scale * lax.dot_general(
            half, group_emb, (((0,), (0,)), ((), ())), preferred_element_type=F32
        )

    half = column_count // 2
    text_other = swapped(text_part(weights_low[:, half:]), "c")
    text_sum = text_part(weights_low[:, :half]) + text_other
    text_fixed = coded(text_sum, 8)
    image_fixed = coded(
        scale * jnp.dot(weights_low, column_emb, preferred_element_type=F32), 8
    )
    text_fixed, image_fixed = lax.optimization_barrier((text_fixed, image_fixed))
    text_up = lax.dynamic_slice_in_dim(text_sum, (y * 2 + zl) * own_rows, own_rows, 0)
    arrivals = []
    for dy, dz in ((2, 1), (2, 0), (1, 1), (3, 1), (1, 0), (3, 0), (0, 1)):
        index = lax.rem(y + dy, 4) * 2 + lax.rem(zl + dz, 2)
        piece = lax.dynamic_slice_in_dim(text_fixed, index, 1, 0)
        arrivals.append(
            moved(piece, PLANE, lambda i, j, a=dy, b=dz: ((i + a) % 4, (j + b) % 2))
        )
    image_blocks = lax.all_to_all(image_fixed, BRANCH, 0, 0, tiled=True)
    image_up = jnp.sum(decoded(image_blocks), axis=0)
    text_up = text_up + sum(decoded(piece[0]) for piece in arrivals)

    image_down = unnormalize(image_up, image_unit, image_length)
    text_down = unnormalize(text_up, text_unit, text_length)
    image_grad = lax.dot_general(
        image_down, image_proj, (((1,), (1,)), ((), ())), preferred_element_type=F32
    ).astype(BF)
    text_grad = lax.dot_general(
        text_down, text_proj, (((1,), (1,)), ((), ())), preferred_element_type=F32
    ).astype(BF)

    def by_column(rows):
        return jnp.swapaxes(rows.reshape(own_rows, 8, -1), 0, 1)

    sent = [by_column(a) for a in (image_grad, text_grad, image_down, text_down)]
    got = lax.all_to_all(jnp.concatenate(sent, axis=2), BRANCH, 0, 0, tiled=True)
    got = got.reshape(group_rows, -1)
    cuts = np.cumsum([a.shape[2] for a in sent])
    grad_image_hidden = got[:, : cuts[0]]
    grad_text_hidden = got[:, cuts[0] : cuts[1]]

    def weight(features, downs, width):
        rolled = lax.dot_general(
            features, downs, (((0,), (0,)), ((), ())), preferred_element_type=F32
        )
        return lax.dynamic_slice_in_dim(
            jnp.concatenate([rolled, rolled]), lax.rem(4 - x, 4) * width, 4 * width, 0
        )

    image_weight = weight(hidden_full, got[:, cuts[1] : cuts[2]], 2 * image_slab)
    text_weight = weight(text_full, got[:, cuts[2] : cuts[3]], 2 * text_slab)

    own_row_terms = lax.dynamic_slice_in_dim(row_lse, branch_pos * own_rows, own_rows, 0)
    own_col_terms = lax.dynamic_slice_in_dim(col_lse, (y * 2 + zl) * own_rows, own_rows, 0)
    loss_part = jnp.sum(own_row_terms) + jnp.sum(own_col_terms) - 2.0 * positive_part
    loss_part = loss_part / denominator
    width = image_weight.shape[1]
    scalars = jnp.pad(jnp.stack([loss_part, scale_part])[:, None], ((0, 6), (0, width - 1)))
    partial = jnp.concatenate(
        [
            image_weight.reshape(16, -1, width),
            text_weight.reshape(16, -1, width),
            jnp.broadcast_to(scalars[None], (16, 8, width)),
        ],
        axis=1,
    )
    summed = jnp.sum(lax.all_to_all(partial, DP, 0, 0, tiled=True), axis=0)
    turned = moved(summed, AXES, lambda a, b, core, d, e: (d, e, core, a, b))
    line = stacked(turned[None], swapped(turned, "zl")[None], zl)
    lines = jnp.stack(
        [line] + [moved(line, ("y",), lambda i, k=k: ((i + k) % 4,)) for k in (3, 2, 1)]
    )
    lines = lax.dynamic_slice_in_dim(jnp.concatenate([lines, lines]), lax.rem(4 - y, 4), 4, 0)
    whole = stacked(lines[None], swapped(lines, "c")[None], c).reshape(2, 8, *turned.shape)

    def slab(first, rows):
        part = whole[:, :, first : first + rows]
        return part.transpose(0, 2, 1, 3).reshape(2 * rows, 8 * width)

    image_rows, text_rows = image_slab // 2, text_slab // 2
    totals = jnp.sum(whole[0, :, image_rows + text_rows :, 0], axis=0)
    return (
        totals[0].reshape(1),
        totals[1].reshape(1),
        grad_image_hidden,
        grad_text_hidden,
        slab(0, image_rows),
        slab(image_rows, text_rows),
    )


def solution(mesh):
    torus = Mesh(mesh.devices.reshape(tuple(SIZES.values())), AXES)
    placed = (P(DP, BRANCH), P(DP, BRANCH), P(), P(), P(), P())
    return jax.shard_map(
        per_device,
        mesh=torus,
        in_specs=placed,
        out_specs=(P(), P(), P(DP, BRANCH), P(DP, BRANCH), P(BRANCH, None), P(BRANCH, None)),
        check_vma=False,
    )
```

```python
import jax
import jax.numpy as jnp
import numpy as np
from jax import lax
from jax.sharding import Mesh
from jax.sharding import PartitionSpec as P

SIZES = {"y": 4, "zl": 2, "c": 2, "x": 4, "zh": 2}
AXES = tuple(SIZES)
DP = ("y", "zl", "c")
PLANE = ("y", "zl")
BRANCH = ("x", "zh")

NORM_EPSILON = 1e-06
FULL_SCALE = 32000.0
BF = jnp.bfloat16
F32 = jnp.float32


def moved(value, axes, target):
    sizes = [SIZES[a] for a in axes]
    pairs = []
    for i in range(int(np.prod(sizes))):
        at = tuple(int(v) for v in np.unravel_index(i, sizes))
        pairs.append((i, int(np.ravel_multi_index(target(*at), sizes))))
    return lax.ppermute(value, axes, pairs)


def swapped(value, axis, mask=1):
    return moved(value, (axis,), lambda i: (i ^ mask,))


def paired(own, other, side):
    return jnp.where(
        side == 0,
        jnp.concatenate([own, other], axis=1),
        jnp.concatenate([other, own], axis=1),
    )


def stacked(own, other, side):
    return jnp.where(side == 0, jnp.concatenate([own, other]), jnp.concatenate([other, own]))


def rounds(rows, exponent):
    return jnp.round(rows * (FULL_SCALE * jnp.exp2(-exponent))).astype(jnp.int16)


def coded(rows, blocks):
    count, width = rows.shape
    r = count // blocks
    top = jnp.max(jnp.abs(rows), axis=1)
    exponent = jnp.maximum(jnp.ceil(jnp.log2(top)), -80.0)
    fixed = rounds(rows, exponent[:, None]).reshape(blocks, r, width)
    tail = jnp.pad(exponent.reshape(blocks, 1, r), ((0, 0), (0, 7), (0, width - r)))
    return jnp.concatenate([fixed, tail.astype(jnp.int16)], axis=1)


def decoded(blocks):
    r = blocks.shape[-2] - 8
    exponent = blocks[..., r, :r].astype(F32)
    return blocks[..., :r, :].astype(F32) * (jnp.exp2(exponent) / FULL_SCALE)[..., None]


def normalize(raw_rows):
    lengths = jnp.sqrt(jnp.sum(raw_rows * raw_rows, axis=1, keepdims=True) + NORM_EPSILON)
    unit_rows = raw_rows / lengths
    return (unit_rows, lengths, unit_rows.astype(BF))


def unnormalize(upstream, unit_rows, lengths):
    radial = jnp.sum(upstream * unit_rows, axis=1, keepdims=True)
    return ((upstream - unit_rows * radial) / lengths).astype(BF)


def per_device(image_hidden, text_hidden, image_proj, text_proj, log_inverse_sharpness, partner):
    y, zl, c, x, zh = (lax.axis_index(a) for a in AXES)
    branch_pos = x * 2 + zh
    data_pos = (y * 2 + zl) * 2 + c
    group_rows, image_slab = image_hidden.shape
    text_slab = text_hidden.shape[1]
    own_rows = group_rows // 8
    embed = image_proj.shape[1]
    total_pairs = group_rows * 16
    denominator = 2.0 * total_pairs
    scale = jnp.exp(log_inverse_sharpness[0])

    image_other, text_other = lax.optimization_barrier(
        (swapped(image_hidden, "zh"), swapped(text_hidden, "zh"))
    )
    image_pair = paired(image_hidden, image_other, zh)
    text_pair = paired(text_hidden, text_other, zh)
    text_blocks = text_pair.reshape(4, 2, own_rows, 2 * text_slab)
    text_blocks = lax.dynamic_index_in_dim(text_blocks, zh, 1, keepdims=False)

    def turned_by(rows, width):
        return lax.dynamic_slice_in_dim(jnp.concatenate([rows, rows]), x * width, 4 * width, 0)

    def from_x(send):
        return [send(0)] + [moved(send(k), ("x",), lambda i, k=k: ((i + k) % 4,)) for k in (3, 2, 1)]

    text_local = jnp.concatenate(
        from_x(
            lambda k: lax.dynamic_index_in_dim(text_blocks, lax.rem(x + k, 4), 0, keepdims=False)
        ),
        axis=1,
    )
    text_raw = jnp.dot(
        text_local, turned_by(text_proj, 2 * text_slab), preferred_element_type=F32
    )
    text_unit, text_length, text_emb = normalize(text_raw)
    near_text = lax.all_to_all(
        jnp.broadcast_to(text_emb[None], (8, own_rows, embed)), PLANE, 0, 0, tiled=True
    ).reshape(8 * own_rows, embed)
    image_parts, near_text = lax.optimization_barrier((from_x(lambda k: image_pair), near_text))
    column_emb = jnp.concatenate([near_text, swapped(near_text, "c")], axis=0)

    hidden_full = jnp.concatenate(image_parts, axis=1)
    image_raw = jnp.dot(
        hidden_full, turned_by(image_proj, 2 * image_slab), preferred_element_type=F32
    )
    group_unit, group_length, group_emb = normalize(image_raw)
    image_unit = lax.dynamic_slice_in_dim(group_unit, branch_pos * own_rows, own_rows, 0)
    image_length = lax.dynamic_slice_in_dim(group_length, branch_pos * own_rows, own_rows, 0)

    text_pair, _ = lax.optimization_barrier((text_pair, image_parts))
    text_parts = from_x(lambda k: text_pair)

    logits = scale * lax.dot_general(
        group_emb, column_emb, (((1,), (1,)), ((), ())), preferred_element_type=F32
    )
    column_count = logits.shape[1]
    position = jnp.arange(column_count, dtype=jnp.int32)
    core = jnp.bitwise_xor(position // (8 * own_rows), c)
    block = position % (8 * own_rows) // own_rows
    column_ids = ((block * 2 + core) * 8 + branch_pos) * own_rows + position % own_rows
    row_partner = lax.dynamic_slice_in_dim(partner, data_pos * group_rows, group_rows, 0)
    matched = row_partner[:, None] == column_ids[None, :]
    positive_part = jnp.sum(jnp.where(matched, logits, 0.0))
    row_peak = jnp.max(logits, axis=1)
    row_mass = jnp.sum(jnp.exp(logits - row_peak[:, None]), axis=1)
    col_peak = jnp.max(logits, axis=0)
    col_mass = jnp.sum(jnp.exp(logits - col_peak[None, :]), axis=0)

    def joined(mine, theirs):
        peak = jnp.maximum(mine[0], theirs[0])
        mass = mine[1] * jnp.exp(mine[0] - peak) + theirs[1] * jnp.exp(theirs[0] - peak)
        return jnp.stack([peak, mass])

    row_stats = jnp.stack([row_peak, row_mass])
    col_stats = jnp.stack([col_peak, col_mass])
    theirs = swapped(col_stats, "c").reshape(2, 2, -1)[:, ::-1].reshape(2, -1)
    col_stats = joined(col_stats, theirs)
    for row_step, col_step in ((("x", 1), ("y", 1)), (("x", 2), ("y", 2)), (("zh", 1), ("zl", 1))):
        row_in = swapped(row_stats, *row_step)
        col_in = swapped(col_stats, *col_step)
        row_stats, col_stats = joined(row_stats, row_in), joined(col_stats, col_in)
    row_stats, col_stats, text_parts = lax.optimization_barrier((row_stats, col_stats, text_parts))
    text_full = jnp.concatenate(text_parts, axis=1)
    row_lse = row_stats[0] + jnp.log(row_stats[1])
    col_lse = col_stats[0] + jnp.log(col_stats[1])

    weights = (
        jnp.exp(logits - row_lse[:, None])
        + jnp.exp(logits - col_lse[None, :])
        - 2.0 * matched.astype(F32)
    ) / denominator
    scale_part = jnp.sum(weights * logits)
    weights_low = weights.astype(BF)

    def text_part(half):
        return scale * lax.dot_general(
            half, group_emb, (((0,), (0,)), ((), ())), preferred_element_type=F32
        )

    half = column_count // 2
    text_other = swapped(text_part(weights_low[:, half:]), "c")
    image_fixed = coded(scale * jnp.dot(weights_low, column_emb, preferred_element_type=F32), 8)
    image_fixed = image_fixed.reshape(4, 2, own_rows + 8, embed)
    image_ring = from_x(
        lambda k: lax.dynamic_index_in_dim(image_fixed, lax.rem(x + k, 4), 0, keepdims=False)
    )
    text_fixed = coded(text_part(weights_low[:, :half]) + text_other, 8)
    text_blocks = lax.all_to_all(text_fixed, PLANE, 0, 0, tiled=True)
    image_pairs = sum(decoded(part) for part in image_ring)
    image_own = lax.dynamic_index_in_dim(image_pairs, zh, 0, keepdims=False)
    image_other = lax.dynamic_index_in_dim(image_pairs, 1 - zh, 0, keepdims=False)
    image_other = swapped(coded(image_other, 1), "zh")
    image_up = image_own + decoded(image_other)[0]
    text_up = jnp.sum(decoded(text_blocks), axis=0)

    image_down = unnormalize(image_up, image_unit, image_length)
    text_down = unnormalize(text_up, text_unit, text_length)
    image_grad = lax.dot_general(
        image_down, image_proj, (((1,), (1,)), ((), ())), preferred_element_type=F32
    ).astype(BF)
    text_grad = lax.dot_general(
        text_down, text_proj, (((1,), (1,)), ((), ())), preferred_element_type=F32
    ).astype(BF)

    def by_column(rows):
        return jnp.swapaxes(rows.reshape(own_rows, 8, -1), 0, 1)

    def redistributed(parts):
        sent = [by_column(a) for a in parts]
        got = lax.all_to_all(jnp.concatenate(sent, axis=2), BRANCH, 0, 0, tiled=True)
        got = got.reshape(group_rows, -1)
        cut = sent[0].shape[2]
        return got[:, :cut], got[:, cut:]

    image_columns, text_columns = redistributed((image_down, text_down))
    grad_image_hidden, grad_text_hidden = redistributed((image_grad, text_grad))

    def weight(features, downs, width):
        rolled = lax.dot_general(
            features, downs, (((0,), (0,)), ((), ())), preferred_element_type=F32
        )
        return lax.dynamic_slice_in_dim(
            jnp.concatenate([rolled, rolled]), lax.rem(4 - x, 4) * width, 4 * width, 0
        )

    image_weight = weight(hidden_full, image_columns, 2 * image_slab)
    text_weight = weight(text_full, text_columns, 2 * text_slab)

    own_row_terms = lax.dynamic_slice_in_dim(row_lse, branch_pos * own_rows, own_rows, 0)
    own_col_terms = lax.dynamic_slice_in_dim(col_lse, (y * 2 + zl) * own_rows, own_rows, 0)
    loss_part = jnp.sum(own_row_terms) + jnp.sum(own_col_terms) - 2.0 * positive_part
    loss_part = loss_part / denominator
    width = image_weight.shape[1]
    scalars = jnp.pad(jnp.stack([loss_part, scale_part])[:, None], ((0, 6), (0, width - 1)))
    partial = jnp.concatenate(
        [
            image_weight.reshape(16, -1, width),
            text_weight.reshape(16, -1, width),
            jnp.broadcast_to(scalars[None], (16, 8, width)),
        ],
        axis=1,
    )
    summed = jnp.sum(lax.all_to_all(partial, DP, 0, 0, tiled=True), axis=0)
    turned = moved(summed, AXES, lambda a, b, core, d, e: (d, e, core, a, b))
    line = stacked(turned[None], swapped(turned, "zl")[None], zl)
    lines = jnp.stack(
        [line] + [moved(line, ("y",), lambda i, k=k: ((i + k) % 4,)) for k in (3, 2, 1)]
    )
    lines = lax.dynamic_slice_in_dim(jnp.concatenate([lines, lines]), lax.rem(4 - y, 4), 4, 0)
    whole = stacked(lines[None], swapped(lines, "c")[None], c).reshape(2, 8, *turned.shape)

    def slab(first, rows):
        part = whole[:, :, first : first + rows]
        return part.transpose(0, 2, 1, 3).reshape(2 * rows, 8 * width)

    image_rows, text_rows = image_slab // 2, text_slab // 2
    totals = jnp.sum(whole[0, :, image_rows + text_rows :, 0], axis=0)
    return (
        totals[0].reshape(1),
        totals[1].reshape(1),
        grad_image_hidden,
        grad_text_hidden,
        slab(0, image_rows),
        slab(image_rows, text_rows),
    )


def solution(mesh):
    torus = Mesh(mesh.devices.reshape(tuple(SIZES.values())), AXES)
    placed = (P(DP, BRANCH), P(DP, BRANCH), P(), P(), P(), P())
    return jax.shard_map(
        per_device,
        mesh=torus,
        in_specs=placed,
        out_specs=(P(), P(), P(DP, BRANCH), P(DP, BRANCH), P(BRANCH, None), P(BRANCH, None)),
        check_vma=False,
    )
```

```python
import jax
import jax.numpy as jnp
import numpy as np
from jax import lax
from jax.experimental import pallas as pl
from jax.experimental.pallas import tpu as pltpu
from jax.sharding import Mesh
from jax.sharding import PartitionSpec as P

SIZES = {"y": 4, "zl": 2, "c": 2, "x": 4, "zh": 2}
AXES = tuple(SIZES)
DP = ("y", "zl", "c")
PLANE = ("y", "zl")
BRANCH = ("x", "zh")

NORM_EPSILON = 1e-06
FULL_SCALE = 32000.0
DENOMINATOR = 32768.0
LOW = -1e30
LANES = 128
TAIL = 16
RUN = 2048
BF = jnp.bfloat16
F32 = jnp.float32


def moved(value, axes, target):
    sizes = [SIZES[a] for a in axes]
    pairs = []
    for i in range(int(np.prod(sizes))):
        at = tuple(int(v) for v in np.unravel_index(i, sizes))
        pairs.append((i, int(np.ravel_multi_index(target(*at), sizes))))
    return lax.ppermute(value, axes, pairs)


def swapped(value, axis, mask=1):
    return moved(value, (axis,), lambda i: (i ^ mask,))


def paired(own, other, side):
    return jnp.where(
        side == 0,
        jnp.concatenate([own, other], axis=1),
        jnp.concatenate([other, own], axis=1),
    )


def stacked(own, other, side):
    return jnp.where(side == 0, jnp.concatenate([own, other]), jnp.concatenate([other, own]))


def normalize(raw_rows):
    lengths = jnp.sqrt(jnp.sum(raw_rows * raw_rows, axis=1, keepdims=True) + NORM_EPSILON)
    unit_rows = raw_rows / lengths
    return (unit_rows, lengths, unit_rows.astype(BF))


def eye():
    row = lax.broadcasted_iota(jnp.int32, (LANES, LANES), 0)
    return row == lax.broadcasted_iota(jnp.int32, (LANES, LANES), 1)


def as_row(column):
    return jnp.sum(jnp.where(eye(), column, 0.0), axis=0, keepdims=True)


def as_column(row):
    return jnp.sum(jnp.where(eye(), row, 0.0), axis=1, keepdims=True)


def exponent_of(top):
    return jnp.maximum(jnp.ceil(jnp.log2(top)), -80.0)


def to_fixed(values, exponent):
    return jnp.round(values * (FULL_SCALE * jnp.exp2(-exponent))).astype(jnp.int32).astype(jnp.int16)


def from_fixed(fixed, exponent):
    return fixed.astype(jnp.int32).astype(F32) * (jnp.exp2(exponent) / FULL_SCALE)


def tail(row):
    return jnp.broadcast_to(row, (TAIL, row.shape[1])).astype(jnp.int32).astype(jnp.int16)


def code_rows(values):
    exponent = exponent_of(jnp.max(jnp.abs(values), axis=1, keepdims=True))
    return to_fixed(values, exponent), tail(as_row(exponent))


def decode_rows(fixed, exponents):
    row = exponents.astype(jnp.int32).astype(F32)[:1]
    return from_fixed(fixed, as_column(row))


def kernel_call(body, name, out_shape, grid=(), in_specs=None, out_specs=None, scratch=(), prefetch=0, flops=0, moved_bytes=0):
    spec = pltpu.PrefetchScalarGridSpec(
        num_scalar_prefetch=prefetch,
        grid=grid,
        in_specs=in_specs,
        out_specs=out_specs,
        scratch_shapes=scratch,
    )
    return pl.pallas_call(
        body,
        out_shape=out_shape,
        grid_spec=spec,
        name=name,
        compiler_params=pltpu.CompilerParams(vmem_limit_bytes=40 * 2**20),
        cost_estimate=pl.CostEstimate(flops=flops, bytes_accessed=moved_bytes, transcendentals=0),
    )


def whole(shape):
    return pl.BlockSpec(shape, lambda *_: (0,) * len(shape))


def shaped(shape, dtype):
    return jax.ShapeDtypeStruct(shape, dtype)


def project_group(place, parts, proj):
    rows, width = parts[0].shape
    embed = proj.shape[1]
    step = 256

    def body(place_ref, a, b, c, d, proj_ref, emb_ref, unit_ref, length_ref):
        i = pl.program_id(0)
        raw = None
        for k, part in enumerate((a, b, c, d)):
            first = pl.multiple_of(lax.rem(place_ref[0] + k, 4) * width, width)
            term = jnp.dot(
                part[...], proj_ref[pl.ds(first, width), :], preferred_element_type=F32
            )
            raw = term if raw is None else raw + term
        length = jnp.sqrt(jnp.sum(raw * raw, axis=1, keepdims=True) + NORM_EPSILON)
        unit = raw / length
        emb_ref[...] = unit.astype(BF)
        for h in range(step // LANES):

            @pl.when(place_ref[1] == i * (step // LANES) + h)
            def _():
                unit_ref[...] = unit[h * LANES : (h + 1) * LANES]
                length_ref[...] = jnp.broadcast_to(
                    length[h * LANES : (h + 1) * LANES], (LANES, LANES)
                )

    return kernel_call(
        body,
        "project_group",
        (
            shaped((rows, embed), BF),
            shaped((LANES, embed), F32),
            shaped((LANES, LANES), F32),
        ),
        grid=(rows // step,),
        in_specs=[pl.BlockSpec((step, width), lambda i, *_: (i, 0))] * 4 + [whole(proj.shape)],
        out_specs=[
            pl.BlockSpec((step, embed), lambda i, *_: (i, 0)),
            whole((LANES, embed)),
            whole((LANES, LANES)),
        ],
        prefetch=1,
        flops=2 * rows * 4 * width * embed,
        moved_bytes=6 * 2**20,
    )(place, *parts, proj)


def half_logits(scale, image_emb, text_emb):
    rows, embed = image_emb.shape
    columns = text_emb.shape[0]
    width, step = 512, 256

    def body(scale_ref, image_ref, text_ref, logits_ref, rows_ref, cols_ref, peak_ref, mass_ref):
        j = pl.program_id(0)

        @pl.when(j == 0)
        def _():
            peak_ref[...] = jnp.full(peak_ref.shape, LOW, F32)
            mass_ref[...] = jnp.zeros(mass_ref.shape, F32)

        col_peak = jnp.full((1, width), LOW, F32)
        col_mass = jnp.zeros((1, width), F32)
        for r in range(rows // step):
            at = slice(r * step, (r + 1) * step)
            value = scale_ref[0] * lax.dot_general(
                image_ref[at], text_ref[...], (((1,), (1,)), ((), ())), preferred_element_type=F32
            )
            logits_ref[at] = value
            tiles = [value[:, t : t + LANES] for t in range(0, width, LANES)]
            old = peak_ref[at]
            peak = old
            for tile in tiles:
                peak = jnp.maximum(peak, tile)
            mass = mass_ref[at] * jnp.exp(old - peak)
            for tile in tiles:
                mass = mass + jnp.exp(tile - peak)
            peak_ref[at] = peak
            mass_ref[at] = mass
            top = jnp.maximum(col_peak, jnp.max(value, axis=0, keepdims=True))
            col_mass = col_mass * jnp.exp(col_peak - top) + jnp.sum(
                jnp.exp(value - top), axis=0, keepdims=True
            )
            col_peak = top
        cols_ref[0:1] = col_peak
        cols_ref[1:2] = col_mass

        @pl.when(j == pl.num_programs(0) - 1)
        def _():
            for r in range(rows // LANES):
                at = slice(r * LANES, (r + 1) * LANES)
                peak = jnp.max(peak_ref[at], axis=1, keepdims=True)
                mass = jnp.sum(
                    mass_ref[at] * jnp.exp(peak_ref[at] - peak), axis=1, keepdims=True
                )
                rows_ref[r : r + 1] = as_row(peak)
                rows_ref[8 + r : 9 + r] = as_row(mass)

    return kernel_call(
        body,
        "half_logits",
        (shaped((rows, columns), F32), shaped((16, LANES), F32), shaped((2, columns), F32)),
        grid=(columns // width,),
        in_specs=[
            pl.BlockSpec(memory_space=pltpu.SMEM),
            whole(image_emb.shape),
            pl.BlockSpec((width, embed), lambda j: (j, 0)),
        ],
        out_specs=[
            pl.BlockSpec((rows, width), lambda j: (0, j)),
            whole((16, LANES)),
            pl.BlockSpec((2, width), lambda j: (0, j)),
        ],
        scratch=[pltpu.VMEM((rows, LANES), F32)] * 2,
        flops=2 * rows * columns * embed,
        moved_bytes=8 * 2**20,
    )(scale, image_emb, text_emb)


def weigh(logits, row_lse, col_lse, partner, first_id):
    rows, columns = logits.shape
    lane = lax.broadcasted_iota(jnp.int32, (1, LANES), 1)
    weights = []
    for t in range(columns // LANES):
        at = slice(t * LANES, (t + 1) * LANES)
        value = logits[:, at]
        matched = partner == lane + first_id(t)
        weight = jnp.exp(value - row_lse) + jnp.exp(value - col_lse[:, at])
        weight = (weight - jnp.where(matched, 2.0, 0.0)) * (1.0 / DENOMINATOR)
        scale_term = jnp.sum(weight * value, axis=0, keepdims=True)
        positive = jnp.sum(jnp.where(matched, value, 0.0), axis=0, keepdims=True)
        weights.append((weight.astype(BF), scale_term, positive))
    return weights


def columns_of(rows_ref, first, count):
    return jnp.concatenate(
        [as_column(rows_ref[first + r : first + r + 1]) for r in range(count)], axis=0
    )


def far_weights(place, scale, logits, row_lse, col_lse, partner, image_turned):
    rows, columns = logits.shape
    embed = image_turned.shape[0]
    width = 256

    def body(place_ref, scale_ref, logits_ref, row_ref, col_ref, partner_ref, turned_ref, low_ref, text_ref, terms_ref):
        j = pl.program_id(0)
        sums = [jnp.zeros((1, LANES), F32)] * 2
        for r in range(0, rows, 256):
            at = slice(r, r + 256)
            row = columns_of(row_ref, r // LANES, 2)
            part = columns_of(partner_ref, r // LANES, 2).astype(jnp.int32)
            made = weigh(
                logits_ref[at], row, col_ref[...], part, lambda t: place_ref[0] + (2 * j + t) * RUN
            )
            for t, (low, scale_term, positive) in enumerate(made):
                low_ref[at, t * LANES : (t + 1) * LANES] = low
                sums = [sums[0] + scale_term, sums[1] + positive]
        text_ref[...] = scale_ref[0] * jnp.dot(
            turned_ref[...], low_ref[...], preferred_element_type=F32
        )

        @pl.when(j == 0)
        def _():
            terms_ref[...] = jnp.zeros(terms_ref.shape, F32)

        terms_ref[0:1] += sums[0]
        terms_ref[1:2] += sums[1]

    return kernel_call(
        body,
        "far_weights",
        (
            shaped((rows, columns), BF),
            shaped((embed, columns), F32),
            shaped((8, LANES), F32),
        ),
        grid=(columns // width,),
        in_specs=[
            pl.BlockSpec(memory_space=pltpu.SMEM),
            pl.BlockSpec((rows, width), lambda j, *_: (0, j)),
            whole(row_lse.shape),
            pl.BlockSpec((1, width), lambda j, *_: (0, j)),
            whole(partner.shape),
            whole(image_turned.shape),
        ],
        out_specs=[
            pl.BlockSpec((rows, width), lambda j, *_: (0, j)),
            pl.BlockSpec((embed, width), lambda j, *_: (0, j)),
            whole((8, LANES)),
        ],
        prefetch=1,
        flops=2 * rows * columns * embed,
        moved_bytes=8 * 2**20,
    )(place, scale, logits, row_lse, col_lse, partner, image_turned)


def near_weights(place, scale, logits, row_lse, col_lse, partner, far_low, near_emb, far_emb):
    rows, columns = logits.shape
    embed = near_emb.shape[1]
    step = 256

    def body(place_ref, scale_ref, logits_ref, row_ref, col_ref, partner_ref, far_ref, near_emb_ref, far_emb_ref, *outs):
        low_ref, terms_ref, *coded_refs = outs
        k = pl.program_id(0)
        row = columns_of(row_ref, 0, 2)
        part = columns_of(partner_ref, 0, 2).astype(jnp.int32)
        made = weigh(logits_ref[...], row, col_ref[...], part, lambda t: place_ref[1] + t * RUN)
        sums = [jnp.zeros((1, LANES), F32)] * 2
        for t, (low, scale_term, positive) in enumerate(made):
            low_ref[:, t * LANES : (t + 1) * LANES] = low
            sums = [sums[0] + scale_term, sums[1] + positive]

        @pl.when(k == 0)
        def _():
            terms_ref[...] = jnp.zeros(terms_ref.shape, F32)

        terms_ref[0:1] += sums[0]
        terms_ref[1:2] += sums[1]
        image = jnp.dot(low_ref[...], near_emb_ref[...], preferred_element_type=F32)
        image = image + jnp.dot(far_ref[...], far_emb_ref[...], preferred_element_type=F32)
        image = scale_ref[0] * image
        coded = [code_rows(image[:LANES]), code_rows(image[LANES:])]
        for i in range(4):

            @pl.when(k == i)
            def _():
                for h in range(2):
                    fixed, exponents = coded[h]
                    coded_refs[i][h, :LANES] = fixed
                    coded_refs[i][h, LANES:] = jnp.zeros((TAIL, embed), jnp.int16)
                    coded_refs[i][h, LANES:, :LANES] = exponents

    def rows_at(k, place_ref):
        return lax.rem(place_ref[2] + k, 4)

    piece = (2, LANES + TAIL, embed)
    return kernel_call(
        body,
        "near_weights",
        (
            shaped((rows, columns), BF),
            shaped((8, LANES), F32),
            *[shaped(piece, jnp.int16)] * 4,
        ),
        grid=(4,),
        in_specs=[
            pl.BlockSpec(memory_space=pltpu.SMEM),
            pl.BlockSpec((step, columns), lambda k, p: (rows_at(k, p), 0)),
            pl.BlockSpec((None, 2, LANES), lambda k, p: (rows_at(k, p), 0, 0)),
            whole(col_lse.shape),
            pl.BlockSpec((None, 2, LANES), lambda k, p: (rows_at(k, p), 0, 0)),
            pl.BlockSpec((step, columns), lambda k, p: (rows_at(k, p), 0)),
            whole(near_emb.shape),
            whole(far_emb.shape),
        ],
        out_specs=[
            pl.BlockSpec((step, columns), lambda k, p: (rows_at(k, p), 0)),
            whole((8, LANES)),
            *[whole(piece)] * 4,
        ],
        prefetch=1,
        flops=4 * rows * columns * embed,
        moved_bytes=10 * 2**20,
    )(place, scale, logits, row_lse.reshape(4, 2, LANES), col_lse, partner.reshape(4, 2, LANES), far_low, near_emb, far_emb)


def near_text_sum(scale, low, image_turned, arrived):
    embed, columns = arrived.shape
    rows = low.shape[0]
    width = 256

    def body(scale_ref, low_ref, turned_ref, arrived_ref, out_ref):
        text = scale_ref[0] * jnp.dot(turned_ref[...], low_ref[...], preferred_element_type=F32)
        text = text + arrived_ref[...]
        exponent = exponent_of(jnp.max(jnp.abs(text), axis=0, keepdims=True))
        fixed = to_fixed(text, exponent)
        last = tail(exponent)
        for h in range(width // LANES):
            at = slice(h * LANES, (h + 1) * LANES)
            out_ref[h, :embed] = fixed[:, at]
            out_ref[h, embed:] = last[:, at]

    return kernel_call(
        body,
        "near_text_sum",
        shaped((columns // LANES, embed + TAIL, LANES), jnp.int16),
        grid=(columns // width,),
        in_specs=[
            pl.BlockSpec(memory_space=pltpu.SMEM),
            pl.BlockSpec((rows, width), lambda j: (0, j)),
            whole(image_turned.shape),
            pl.BlockSpec((embed, width), lambda j: (0, j)),
        ],
        out_specs=pl.BlockSpec((width // LANES, embed + TAIL, LANES), lambda j: (j, 0, 0)),
        flops=2 * rows * columns * embed,
        moved_bytes=8 * 2**20,
    )(scale, low, image_turned, arrived)


def pair_sums(place, pieces):
    embed = pieces[0].shape[-1]

    def body(place_ref, a, b, c, d, own_ref, other_ref):
        def total(h):
            parts = [decode_rows(p[h, :LANES], p[h, LANES:, :LANES]) for p in (a, b, c, d)]
            return (parts[0] + parts[1]) + (parts[2] + parts[3])

        own_ref[...] = total(place_ref[3])
        fixed, exponents = code_rows(total(1 - place_ref[3]))
        other_ref[:LANES] = fixed
        other_ref[LANES:] = jnp.zeros((TAIL, embed), jnp.int16)
        other_ref[LANES:, :LANES] = exponents

    return kernel_call(
        body,
        "pair_sums",
        (shaped((LANES, embed), F32), shaped((LANES + TAIL, embed), jnp.int16)),
        grid=(1,),
        in_specs=[whole(pieces[0].shape)] * 4,
        out_specs=[whole((LANES, embed)), whole((LANES + TAIL, embed))],
        prefetch=1,
        flops=10**7,
        moved_bytes=3 * 2**20,
    )(place, *pieces)


def lowered(upstream, unit, length):
    radial = jnp.sum(upstream * unit, axis=1, keepdims=True)
    return ((upstream - unit * radial) / length).astype(BF)


def image_down_of(own, other, unit, length):
    def body(own_ref, other_ref, unit_ref, length_ref, out_ref):
        up = own_ref[...] + decode_rows(other_ref[:LANES], other_ref[LANES:, :LANES])
        out_ref[...] = lowered(up, unit_ref[...], length_ref[:, :1])

    return kernel_call(
        body,
        "image_down",
        shaped(own.shape, BF),
        grid=(1,),
        in_specs=[whole(a.shape) for a in (own, other, unit, length)],
        out_specs=whole(own.shape),
        flops=10**7,
        moved_bytes=2 * 2**20,
    )(own, other, unit, length)


def text_down_of(pieces, unit, length):
    embed = unit.shape[1]

    def body(pieces_ref, unit_ref, length_ref, out_ref):
        up = jnp.zeros((embed, LANES), F32)
        for n in range(pieces.shape[0]):
            row = pieces_ref[n, embed:].astype(jnp.int32).astype(F32)[:1]
            up = up + from_fixed(pieces_ref[n, :embed], row)
        out_ref[...] = lowered(up.T, unit_ref[...], length_ref[:, :1])

    return kernel_call(
        body,
        "text_down",
        shaped(unit.shape, BF),
        grid=(1,),
        in_specs=[whole(a.shape) for a in (pieces, unit, length)],
        out_specs=whole(unit.shape),
        flops=10**7,
        moved_bytes=2 * 2**20,
    )(pieces, unit, length)


def weight_sums(place, image_parts, text_parts, downs, scalars):
    width = downs.shape[1] // 2
    image_run, text_run = image_parts[0].shape[1] // 4, text_parts[0].shape[1] // 4

    def body(place_ref, *refs):
        image_refs, text_refs, (downs_ref, scalars_ref, out_ref) = refs[:4], refs[4:8], refs[8:]
        for k in range(4):
            runs = pl.ds(4 * lax.rem(place_ref[2] + k, 4), 4)
            for part, first, run, cut in (
                (image_refs[k], 0, image_run, slice(0, width)),
                (text_refs[k], image_run, text_run, slice(width, 2 * width)),
            ):
                value = lax.dot_general(
                    part[...], downs_ref[...], (((0,), (0,)), ((), ())), preferred_element_type=F32
                )
                out_ref[runs, first : first + run, :] = value[:, cut].reshape(4, run, width)
        out_ref[:, image_run + text_run :, :] = jnp.broadcast_to(scalars_ref[...][None], (16, 8, width))

    shape = (16, image_run + text_run + 8, width)
    args = (*image_parts, *text_parts, downs, scalars)
    return kernel_call(
        body,
        "weight_sums",
        shaped(shape, F32),
        grid=(1,),
        in_specs=[whole(a.shape) for a in args],
        out_specs=whole(shape),
        prefetch=1,
        flops=10**9,
        moved_bytes=6 * 2**20,
    )(place, *args)


def per_device(image_hidden, text_hidden, image_proj, text_proj, log_inverse_sharpness, partner):
    y, zl, c, x, zh = (lax.axis_index(a) for a in AXES)
    branch_pos = x * 2 + zh
    data_pos = (y * 2 + zl) * 2 + c
    group_rows, image_slab = image_hidden.shape
    text_slab = text_hidden.shape[1]
    own_rows = group_rows // 8
    embed = image_proj.shape[1]
    scale = jnp.exp(log_inverse_sharpness)
    first = branch_pos * own_rows
    place = jnp.stack([(1 - c) * group_rows + first, c * group_rows + first, x, zh])

    image_other, text_other = lax.optimization_barrier(
        (swapped(image_hidden, "zh"), swapped(text_hidden, "zh"))
    )
    image_pair = paired(image_hidden, image_other, zh)
    text_pair = paired(text_hidden, text_other, zh)
    text_blocks = text_pair.reshape(4, 2, own_rows, 2 * text_slab)
    text_blocks = lax.dynamic_index_in_dim(text_blocks, zh, 1, keepdims=False)

    def turned_by(rows, width):
        return lax.dynamic_slice_in_dim(jnp.concatenate([rows, rows]), x * width, 4 * width, 0)

    def from_x(send):
        return [send(0)] + [moved(send(k), ("x",), lambda i, k=k: ((i + k) % 4,)) for k in (3, 2, 1)]

    text_local = jnp.concatenate(
        from_x(
            lambda k: lax.dynamic_index_in_dim(text_blocks, lax.rem(x + k, 4), 0, keepdims=False)
        ),
        axis=1,
    )
    text_raw = jnp.dot(
        text_local, turned_by(text_proj, 2 * text_slab), preferred_element_type=F32
    )
    text_unit, text_length, text_emb = normalize(text_raw)
    near_text = lax.all_to_all(
        jnp.broadcast_to(text_emb[None], (8, own_rows, embed)), PLANE, 0, 0, tiled=True
    ).reshape(8 * own_rows, embed)
    image_parts, near_text = lax.optimization_barrier((from_x(lambda k: image_pair), near_text))
    far_text = swapped(near_text, "c")
    group_emb, image_unit, image_length = project_group(
        jnp.stack([x, branch_pos]), image_parts, image_proj
    )

    text_pair, _ = lax.optimization_barrier((text_pair, image_parts))
    text_parts = from_x(lambda k: text_pair)

    near_logits, near_rows, near_cols = half_logits(scale, group_emb, near_text)
    far_logits, far_rows, far_cols = half_logits(scale, group_emb, far_text)
    image_turned = group_emb.T

    def joined(mine, theirs):
        peak = jnp.maximum(mine[0], theirs[0])
        mass = mine[1] * jnp.exp(mine[0] - peak) + theirs[1] * jnp.exp(theirs[0] - peak)
        return jnp.stack([peak, mass])

    row_stats = joined(near_rows.reshape(2, 8, LANES), far_rows.reshape(2, 8, LANES))
    col_stats = jnp.concatenate([near_cols, far_cols], axis=1)
    col_in = swapped(jnp.concatenate([far_cols, near_cols], axis=1), "c")
    col_stats = joined(col_stats, col_in)
    for row_step, col_step in ((("x", 1), ("y", 1)), (("x", 2), ("y", 2)), (("zh", 1), ("zl", 1))):
        row_in = swapped(row_stats, *row_step)
        col_in = swapped(col_stats, *col_step)
        row_stats, col_stats = joined(row_stats, row_in), joined(col_stats, col_in)
    row_stats, col_stats, text_parts = lax.optimization_barrier((row_stats, col_stats, text_parts))
    row_lse = row_stats[0] + jnp.log(row_stats[1])
    col_lse = col_stats[0] + jnp.log(col_stats[1])

    row_partner = lax.dynamic_slice_in_dim(partner, data_pos * group_rows, group_rows, 0)
    row_partner = row_partner.astype(F32).reshape(8, LANES)
    near_lse, far_lse = col_lse[None, :group_rows], col_lse[None, group_rows:]
    far_low, far_part, far_terms = far_weights(
        place, scale, far_logits, row_lse, far_lse, row_partner, image_turned
    )
    text_arrived = swapped(far_part, "c")
    near_low, near_terms, *image_coded = near_weights(
        place, scale, near_logits, row_lse, near_lse, row_partner, far_low, near_text, far_text
    )
    image_ring = from_x(lambda k: image_coded[k])
    text_coded = near_text_sum(scale, near_low, image_turned, text_arrived)
    text_pieces = lax.all_to_all(text_coded, PLANE, 0, 0, tiled=True)
    image_own, image_other = pair_sums(place, image_ring)
    image_down = image_down_of(image_own, swapped(image_other, "zh"), image_unit, image_length)
    text_down = text_down_of(text_pieces, text_unit, text_length)
    image_grad = lax.dot_general(
        image_down, image_proj, (((1,), (1,)), ((), ())), preferred_element_type=F32
    ).astype(BF)
    text_grad = lax.dot_general(
        text_down, text_proj, (((1,), (1,)), ((), ())), preferred_element_type=F32
    ).astype(BF)

    def by_column(rows):
        return jnp.swapaxes(rows.reshape(own_rows, 8, -1), 0, 1)

    def redistributed(parts):
        sent = [by_column(a) for a in parts]
        got = lax.all_to_all(jnp.concatenate(sent, axis=2), BRANCH, 0, 0, tiled=True)
        return got.reshape(group_rows, -1)

    downs = redistributed((image_down, text_down))
    grads = redistributed((image_grad, text_grad))
    grad_image_hidden, grad_text_hidden = grads[:, :image_slab], grads[:, image_slab:]

    terms = jnp.sum(far_terms + near_terms, axis=1)
    own_row_terms = lax.dynamic_index_in_dim(row_lse, branch_pos, 0)
    own_col_terms = lax.dynamic_slice_in_dim(col_lse, (y * 2 + zl) * own_rows, own_rows, 0)
    loss_part = jnp.sum(own_row_terms) + jnp.sum(own_col_terms) - 2.0 * terms[1]
    width = embed // 8
    scalars = jnp.stack([loss_part / DENOMINATOR, terms[0]])
    scalars = jnp.pad(scalars[:, None], ((0, 6), (0, width - 1)))
    partial = weight_sums(place, image_parts, text_parts, downs, scalars)
    summed = jnp.sum(lax.all_to_all(partial, DP, 0, 0, tiled=True), axis=0)
    turned = moved(summed, AXES, lambda a, b, core, d, e: (d, e, core, a, b))
    line = stacked(turned[None], swapped(turned, "zl")[None], zl)
    lines = jnp.stack(
        [line] + [moved(line, ("y",), lambda i, k=k: ((i + k) % 4,)) for k in (3, 2, 1)]
    )
    lines = lax.dynamic_slice_in_dim(jnp.concatenate([lines, lines]), lax.rem(4 - y, 4), 4, 0)
    whole = stacked(lines[None], swapped(lines, "c")[None], c).reshape(2, 8, *turned.shape)

    def slab(first, rows):
        part = whole[:, :, first : first + rows]
        return part.transpose(0, 2, 1, 3).reshape(2 * rows, 8 * width)

    image_rows, text_rows = image_slab // 2, text_slab // 2
    totals = jnp.sum(whole[0, :, image_rows + text_rows :, 0], axis=0)
    return (
        totals[0].reshape(1),
        totals[1].reshape(1),
        grad_image_hidden,
        grad_text_hidden,
        slab(0, image_rows),
        slab(image_rows, text_rows),
    )


def solution(mesh):
    torus = Mesh(mesh.devices.reshape(tuple(SIZES.values())), AXES)
    placed = (P(DP, BRANCH), P(DP, BRANCH), P(), P(), P(), P())
    return jax.shard_map(
        per_device,
        mesh=torus,
        in_specs=placed,
        out_specs=(P(), P(), P(DP, BRANCH), P(DP, BRANCH), P(BRANCH, None), P(BRANCH, None)),
        check_vma=False,
    )
```

```python
import jax
import jax.numpy as jnp
import numpy as np
from jax import lax
from jax.experimental import pallas as pl
from jax.experimental.pallas import tpu as pltpu
from jax.sharding import Mesh
from jax.sharding import PartitionSpec as P

SIZES = {"y": 4, "zl": 2, "c": 2, "x": 4, "zh": 2}
AXES = tuple(SIZES)
DP = ("y", "zl", "c")
PLANE = ("y", "zl")
BRANCH = ("x", "zh")

NORM_EPSILON = 1e-06
FULL_SCALE = 32000.0
DENOMINATOR = 32768.0
LOW = -1e30
LANES = 128
TAIL = 16
RUN = 2048
BF = jnp.bfloat16
F32 = jnp.float32


def moved(value, axes, target):
    sizes = [SIZES[a] for a in axes]
    pairs = []
    for i in range(int(np.prod(sizes))):
        at = tuple(int(v) for v in np.unravel_index(i, sizes))
        pairs.append((i, int(np.ravel_multi_index(target(*at), sizes))))
    return lax.ppermute(value, axes, pairs)


def swapped(value, axis, mask=1):
    return moved(value, (axis,), lambda i: (i ^ mask,))


def paired(own, other, side):
    return jnp.where(
        side == 0,
        jnp.concatenate([own, other], axis=1),
        jnp.concatenate([other, own], axis=1),
    )


def stacked(own, other, side):
    return jnp.where(side == 0, jnp.concatenate([own, other]), jnp.concatenate([other, own]))


def normalize(raw_rows):
    lengths = jnp.sqrt(jnp.sum(raw_rows * raw_rows, axis=1, keepdims=True) + NORM_EPSILON)
    unit_rows = raw_rows / lengths
    return (unit_rows, lengths, unit_rows.astype(BF))


def eye():
    row = lax.broadcasted_iota(jnp.int32, (LANES, LANES), 0)
    return row == lax.broadcasted_iota(jnp.int32, (LANES, LANES), 1)


def as_row(column):
    return jnp.sum(jnp.where(eye(), column, 0.0), axis=0, keepdims=True)


def as_column(row):
    return jnp.sum(jnp.where(eye(), row, 0.0), axis=1, keepdims=True)


def exponent_of(top):
    return jnp.maximum(jnp.ceil(jnp.log2(top)), -80.0)


def to_fixed(values, exponent):
    return jnp.round(values * (FULL_SCALE * jnp.exp2(-exponent))).astype(jnp.int32).astype(jnp.int16)


def from_fixed(fixed, exponent):
    return fixed.astype(jnp.int32).astype(F32) * (jnp.exp2(exponent) / FULL_SCALE)


def tail(row):
    return jnp.broadcast_to(row, (TAIL, row.shape[1])).astype(jnp.int32).astype(jnp.int16)


def code_rows(values):
    exponent = exponent_of(jnp.max(jnp.abs(values), axis=1, keepdims=True))
    return to_fixed(values, exponent), tail(as_row(exponent))


def decode_rows(fixed, exponents):
    row = exponents.astype(jnp.int32).astype(F32)[:1]
    return from_fixed(fixed, as_column(row))


def kernel_call(body, name, out_shape, grid=(), in_specs=None, out_specs=None, scratch=(), prefetch=0, flops=0, moved_bytes=0):
    spec = pltpu.PrefetchScalarGridSpec(
        num_scalar_prefetch=prefetch,
        grid=grid,
        in_specs=in_specs,
        out_specs=out_specs,
        scratch_shapes=scratch,
    )
    return pl.pallas_call(
        body,
        out_shape=out_shape,
        grid_spec=spec,
        name=name,
        compiler_params=pltpu.CompilerParams(vmem_limit_bytes=18 * 2**20),
        cost_estimate=pl.CostEstimate(flops=flops, bytes_accessed=moved_bytes, transcendentals=0),
    )


def whole(shape):
    return pl.BlockSpec(shape, lambda *_: (0,) * len(shape))


def shaped(shape, dtype):
    return jax.ShapeDtypeStruct(shape, dtype)


def project_group(place, parts, proj):
    rows, width = parts[0].shape
    embed = proj.shape[1]
    step = 256

    def body(place_ref, a, b, c, d, proj_ref, emb_ref, turned_ref, hidden_ref, unit_ref, length_ref):
        i = pl.program_id(0)
        raw = None
        for k, part in enumerate((a, b, c, d)):
            first = pl.multiple_of(lax.rem(place_ref[0] + k, 4) * width, width)
            term = jnp.dot(
                part[...], proj_ref[pl.ds(first, width), :], preferred_element_type=F32
            )
            raw = term if raw is None else raw + term
            hidden_ref[:, k * width : (k + 1) * width] = part[...]
        length = jnp.sqrt(jnp.sum(raw * raw, axis=1, keepdims=True) + NORM_EPSILON)
        unit = raw / length
        emb_ref[...] = unit.astype(BF)
        turned_ref[...] = unit.T.astype(BF)
        for h in range(step // LANES):

            @pl.when(place_ref[1] == i * (step // LANES) + h)
            def _():
                unit_ref[...] = unit[h * LANES : (h + 1) * LANES]
                length_ref[...] = jnp.broadcast_to(
                    length[h * LANES : (h + 1) * LANES], (LANES, LANES)
                )

    return kernel_call(
        body,
        "project_group",
        (
            shaped((rows, embed), BF),
            shaped((embed, rows), BF),
            pltpu.HBM((rows, 4 * width), BF),
            pltpu.HBM((LANES, embed), F32),
            pltpu.HBM((LANES, LANES), F32),
        ),
        grid=(rows // step,),
        in_specs=[pl.BlockSpec((step, width), lambda i, *_: (i, 0))] * 4 + [whole(proj.shape)],
        out_specs=[
            pl.BlockSpec((step, embed), lambda i, *_: (i, 0)),
            pl.BlockSpec((embed, step), lambda i, *_: (0, i)),
            pl.BlockSpec((step, 4 * width), lambda i, *_: (i, 0)),
            whole((LANES, embed)),
            whole((LANES, LANES)),
        ],
        prefetch=1,
        flops=2 * rows * 4 * width * embed,
        moved_bytes=6 * 2**20,
    )(place, *parts, proj)


def half_logits(scale, image_emb, text_emb):
    rows, embed = image_emb.shape
    columns = text_emb.shape[0]
    width, step = 512, 256

    def body(scale_ref, image_ref, text_ref, logits_ref, rows_ref, cols_ref, peak_ref, mass_ref):
        j = pl.program_id(0)

        @pl.when(j == 0)
        def _():
            peak_ref[...] = jnp.full(peak_ref.shape, LOW, F32)
            mass_ref[...] = jnp.zeros(mass_ref.shape, F32)

        col_peak = jnp.full((1, width), LOW, F32)
        col_mass = jnp.zeros((1, width), F32)
        for r in range(rows // step):
            at = slice(r * step, (r + 1) * step)
            value = scale_ref[0] * lax.dot_general(
                image_ref[at], text_ref[...], (((1,), (1,)), ((), ())), preferred_element_type=F32
            )
            logits_ref[at] = value
            tiles = [value[:, t : t + LANES] for t in range(0, width, LANES)]
            old = peak_ref[at]
            peak = old
            for tile in tiles:
                peak = jnp.maximum(peak, tile)
            mass = mass_ref[at] * jnp.exp(old - peak)
            for tile in tiles:
                mass = mass + jnp.exp(tile - peak)
            peak_ref[at] = peak
            mass_ref[at] = mass
            top = jnp.maximum(col_peak, jnp.max(value, axis=0, keepdims=True))
            col_mass = col_mass * jnp.exp(col_peak - top) + jnp.sum(
                jnp.exp(value - top), axis=0, keepdims=True
            )
            col_peak = top
        cols_ref[0:1] = col_peak
        cols_ref[1:2] = col_mass

        @pl.when(j == pl.num_programs(0) - 1)
        def _():
            for r in range(rows // LANES):
                at = slice(r * LANES, (r + 1) * LANES)
                peak = jnp.max(peak_ref[at], axis=1, keepdims=True)
                mass = jnp.sum(
                    mass_ref[at] * jnp.exp(peak_ref[at] - peak), axis=1, keepdims=True
                )
                rows_ref[r : r + 1] = as_row(peak)
                rows_ref[8 + r : 9 + r] = as_row(mass)

    return kernel_call(
        body,
        "half_logits",
        (shaped((rows, columns), F32), shaped((16, LANES), F32), shaped((2, columns), F32)),
        grid=(columns // width,),
        in_specs=[
            pl.BlockSpec(memory_space=pltpu.SMEM),
            whole(image_emb.shape),
            pl.BlockSpec((width, embed), lambda j: (j, 0)),
        ],
        out_specs=[
            pl.BlockSpec((rows, width), lambda j: (0, j)),
            whole((16, LANES)),
            pl.BlockSpec((2, width), lambda j: (0, j)),
        ],
        scratch=[pltpu.VMEM((rows, LANES), F32)] * 2,
        flops=2 * rows * columns * embed,
        moved_bytes=8 * 2**20,
    )(scale, image_emb, text_emb)


def weigh(logits, row_lse, col_lse, partner, first_id):
    rows, columns = logits.shape
    lane = lax.broadcasted_iota(jnp.int32, (1, LANES), 1)
    weights = []
    for t in range(columns // LANES):
        at = slice(t * LANES, (t + 1) * LANES)
        value = logits[:, at]
        matched = partner == lane + first_id(t)
        weight = jnp.exp(value - row_lse) + jnp.exp(value - col_lse[:, at])
        weight = (weight - jnp.where(matched, 2.0, 0.0)) * (1.0 / DENOMINATOR)
        scale_term = jnp.sum(weight * value, axis=0, keepdims=True)
        positive = jnp.sum(jnp.where(matched, value, 0.0), axis=0, keepdims=True)
        weights.append((weight.astype(BF), scale_term, positive))
    return weights


def columns_of(rows_ref, first, count):
    return jnp.concatenate(
        [as_column(rows_ref[first + r : first + r + 1]) for r in range(count)], axis=0
    )


def far_weights(place, scale, logits, row_lse, col_lse, partner, image_turned):
    rows, columns = logits.shape
    embed = image_turned.shape[0]
    width = 256

    def body(place_ref, scale_ref, logits_ref, row_ref, col_ref, partner_ref, turned_ref, low_ref, text_ref, terms_ref):
        j = pl.program_id(0)
        sums = [jnp.zeros((1, LANES), F32)] * 2
        for r in range(0, rows, 256):
            at = slice(r, r + 256)
            row = columns_of(row_ref, r // LANES, 2)
            part = columns_of(partner_ref, r // LANES, 2).astype(jnp.int32)
            made = weigh(
                logits_ref[at], row, col_ref[...], part, lambda t: place_ref[0] + (2 * j + t) * RUN
            )
            for t, (low, scale_term, positive) in enumerate(made):
                low_ref[at, t * LANES : (t + 1) * LANES] = low
                sums = [sums[0] + scale_term, sums[1] + positive]
        text_ref[...] = scale_ref[0] * jnp.dot(
            turned_ref[...], low_ref[...], preferred_element_type=F32
        )

        @pl.when(j == 0)
        def _():
            terms_ref[...] = jnp.zeros(terms_ref.shape, F32)

        terms_ref[0:1] += sums[0]
        terms_ref[1:2] += sums[1]

    return kernel_call(
        body,
        "far_weights",
        (
            shaped((rows, columns), BF),
            shaped((embed, columns), F32),
            shaped((8, LANES), F32),
        ),
        grid=(columns // width,),
        in_specs=[
            pl.BlockSpec(memory_space=pltpu.SMEM),
            pl.BlockSpec((rows, width), lambda j, *_: (0, j)),
            whole(row_lse.shape),
            pl.BlockSpec((1, width), lambda j, *_: (0, j)),
            whole(partner.shape),
            whole(image_turned.shape),
        ],
        out_specs=[
            pl.BlockSpec((rows, width), lambda j, *_: (0, j)),
            pl.BlockSpec((embed, width), lambda j, *_: (0, j)),
            whole((8, LANES)),
        ],
        prefetch=1,
        flops=2 * rows * columns * embed,
        moved_bytes=8 * 2**20,
    )(place, scale, logits, row_lse, col_lse, partner, image_turned)


def near_weights(place, scale, logits, row_lse, col_lse, partner, far_low, near_emb, far_emb):
    rows, columns = logits.shape
    embed = near_emb.shape[1]
    step = 256

    def body(place_ref, scale_ref, logits_ref, row_ref, col_ref, partner_ref, far_ref, near_emb_ref, far_emb_ref, *outs):
        low_ref, terms_ref, coded_ref = outs
        k = pl.program_id(0)
        row = columns_of(row_ref, 0, 2)
        part = columns_of(partner_ref, 0, 2).astype(jnp.int32)
        made = weigh(logits_ref[...], row, col_ref[...], part, lambda t: place_ref[1] + t * RUN)
        sums = [jnp.zeros((1, LANES), F32)] * 2
        for t, (low, scale_term, positive) in enumerate(made):
            low_ref[:, t * LANES : (t + 1) * LANES] = low
            sums = [sums[0] + scale_term, sums[1] + positive]

        @pl.when(k == 0)
        def _():
            terms_ref[...] = jnp.zeros(terms_ref.shape, F32)

        terms_ref[0:1] += sums[0]
        terms_ref[1:2] += sums[1]
        image = jnp.dot(low_ref[...], near_emb_ref[...], preferred_element_type=F32)
        image = image + jnp.dot(far_ref[...], far_emb_ref[...], preferred_element_type=F32)
        image = scale_ref[0] * image
        for h in range(2):
            fixed, exponents = code_rows(image[h * LANES : (h + 1) * LANES])
            coded_ref[h, :LANES] = fixed
            coded_ref[h, LANES:] = jnp.zeros((TAIL, embed), jnp.int16)
            coded_ref[h, LANES:, :LANES] = exponents

    def rows_at(k, place_ref):
        return k

    piece = (2, LANES + TAIL, embed)
    return kernel_call(
        body,
        "near_weights",
        (
            shaped((rows, columns), BF),
            shaped((8, LANES), F32),
            shaped((4, *piece), jnp.int16),
        ),
        grid=(4,),
        in_specs=[
            pl.BlockSpec(memory_space=pltpu.SMEM),
            pl.BlockSpec((step, columns), lambda k, p: (rows_at(k, p), 0)),
            pl.BlockSpec((None, 2, LANES), lambda k, p: (rows_at(k, p), 0, 0)),
            whole(col_lse.shape),
            pl.BlockSpec((None, 2, LANES), lambda k, p: (rows_at(k, p), 0, 0)),
            pl.BlockSpec((step, columns), lambda k, p: (rows_at(k, p), 0)),
            whole(near_emb.shape),
            whole(far_emb.shape),
        ],
        out_specs=[
            pl.BlockSpec((step, columns), lambda k, p: (rows_at(k, p), 0)),
            whole((8, LANES)),
            pl.BlockSpec((None, *piece), lambda k, p: (k, 0, 0, 0)),
        ],
        prefetch=1,
        flops=4 * rows * columns * embed,
        moved_bytes=10 * 2**20,
    )(place, scale, logits, row_lse.reshape(4, 2, LANES), col_lse, partner.reshape(4, 2, LANES), far_low, near_emb, far_emb)


def near_text_sum(place, scale, low, image_turned, arrived):
    embed, columns = arrived.shape
    rows = low.shape[0]
    width = 2 * LANES

    def body(place_ref, scale_ref, low_ref, turned_ref, arrived_ref, *out_refs):
        text = scale_ref[0] * jnp.dot(turned_ref[...], low_ref[...], preferred_element_type=F32)
        text = text + arrived_ref[...]
        exponent = exponent_of(jnp.max(jnp.abs(text), axis=0, keepdims=True))
        fixed = to_fixed(text, exponent)
        last = tail(exponent)
        for k in range(4):
            for h in range(2):
                for z in range(2):

                    @pl.when((pl.program_id(0) == k) & (place_ref[5] == z))
                    def _():
                        at = slice((z ^ h) * LANES, ((z ^ h) + 1) * LANES)
                        out_refs[2 * k + h][:embed] = fixed[:, at]
                        out_refs[2 * k + h][embed:] = last[:, at]

    def block(k, place_ref):
        return lax.rem(place_ref[4] + k, 4)

    piece = (embed + TAIL, LANES)
    return kernel_call(
        body,
        "near_text_sum",
        (shaped(piece, jnp.int16),) * 8,
        grid=(columns // width,),
        in_specs=[
            pl.BlockSpec(memory_space=pltpu.SMEM),
            pl.BlockSpec((rows, width), lambda k, p: (0, block(k, p))),
            whole(image_turned.shape),
            pl.BlockSpec((embed, width), lambda k, p: (0, block(k, p))),
        ],
        out_specs=[whole(piece)] * 8,
        prefetch=1,
        flops=2 * rows * columns * embed,
        moved_bytes=8 * 2**20,
    )(place, scale, low, image_turned, arrived)


def pair_sums(place, pieces):
    embed = pieces.shape[-1]

    def body(place_ref, pieces_ref, own_ref, other_ref):
        def total(h):
            parts = [
                decode_rows(pieces_ref[n, h, :LANES], pieces_ref[n, h, LANES:, :LANES])
                for n in range(4)
            ]
            return (parts[0] + parts[1]) + (parts[2] + parts[3])

        own_ref[...] = total(place_ref[3])
        fixed, exponents = code_rows(total(1 - place_ref[3]))
        other_ref[:LANES] = fixed
        other_ref[LANES:] = jnp.zeros((TAIL, embed), jnp.int16)
        other_ref[LANES:, :LANES] = exponents

    return kernel_call(
        body,
        "pair_sums",
        (shaped((LANES, embed), F32), shaped((LANES + TAIL, embed), jnp.int16)),
        grid=(1,),
        in_specs=[whole(pieces.shape)],
        out_specs=[whole((LANES, embed)), whole((LANES + TAIL, embed))],
        prefetch=1,
        flops=10**7,
        moved_bytes=3 * 2**20,
    )(place, pieces)


def lowered(upstream, unit, length):
    radial = jnp.sum(upstream * unit, axis=1, keepdims=True)
    return ((upstream - unit * radial) / length).astype(BF)


def image_down_of(own, other, unit, length):
    def body(own_ref, other_ref, unit_ref, length_ref, out_ref):
        up = own_ref[...] + decode_rows(other_ref[:LANES], other_ref[LANES:, :LANES])
        out_ref[...] = lowered(up, unit_ref[...], length_ref[:, :1])

    return kernel_call(
        body,
        "image_down",
        shaped(own.shape, BF),
        grid=(1,),
        in_specs=[whole(a.shape) for a in (own, other, unit, length)],
        out_specs=whole(own.shape),
        flops=10**7,
        moved_bytes=2 * 2**20,
    )(own, other, unit, length)


def text_down_of(pieces, unit, length):
    embed = unit.shape[1]

    def body(*refs):
        piece_refs, (unit_ref, length_ref, out_ref) = refs[:8], refs[8:]
        up = jnp.zeros((embed, LANES), F32)
        for piece in piece_refs:
            row = piece[embed:].astype(jnp.int32).astype(F32)[:1]
            up = up + from_fixed(piece[:embed], row)
        out_ref[...] = lowered(up.T, unit_ref[...], length_ref[:, :1])

    args = (*pieces, unit, length)
    return kernel_call(
        body,
        "text_down",
        shaped(unit.shape, BF),
        grid=(1,),
        in_specs=[whole(a.shape) for a in args],
        out_specs=whole(unit.shape),
        flops=10**7,
        moved_bytes=2 * 2**20,
    )(*args)


def weight_sums(place, hidden, text_parts, downs, scalars):
    width = downs.shape[1] // 2
    image_run, text_run = hidden.shape[1] // 16, text_parts[0].shape[1] // 4

    def body(place_ref, hidden_ref, *refs):
        text_refs, (downs_ref, scalars_ref, kept_ref, sent_ref) = refs[:4], refs[4:]
        even = place_ref[6] == 0
        for k in range(4):
            runs = pl.ds(2 * lax.rem(place_ref[2] + k, 4), 2)
            image = hidden_ref[:, k * 4 * image_run : (k + 1) * 4 * image_run]
            for part, first, run, cut in (
                (image, 0, image_run, slice(0, width)),
                (text_refs[k][...], image_run, text_run, slice(width, 2 * width)),
            ):
                value = lax.dot_general(
                    part, downs_ref[...], (((0,), (0,)), ((), ())), preferred_element_type=F32
                )
                value = value[:, cut].reshape(2, 2, run, width)
                kept_ref[runs, first : first + run, :] = jnp.where(even, value[:, 0], value[:, 1])
                sent_ref[runs, first : first + run, :] = jnp.where(even, value[:, 1], value[:, 0])
        for ref in (kept_ref, sent_ref):
            ref[:, image_run + text_run :, :] = jnp.broadcast_to(scalars_ref[...][None], (8, 8, width))

    shape = (8, image_run + text_run + 8, width)
    args = (hidden, *text_parts, downs, scalars)
    return kernel_call(
        body,
        "weight_sums",
        (shaped(shape, F32),) * 2,
        grid=(1,),
        in_specs=[whole(a.shape) for a in args],
        out_specs=[whole(shape)] * 2,
        prefetch=1,
        flops=10**9,
        moved_bytes=6 * 2**20,
    )(place, *args)


def per_device(image_hidden, text_hidden, image_proj, text_proj, log_inverse_sharpness, partner):
    y, zl, c, x, zh = (lax.axis_index(a) for a in AXES)
    branch_pos = x * 2 + zh
    data_pos = (y * 2 + zl) * 2 + c
    group_rows, image_slab = image_hidden.shape
    text_slab = text_hidden.shape[1]
    own_rows = group_rows // 8
    embed = image_proj.shape[1]
    scale = jnp.exp(log_inverse_sharpness)
    first = branch_pos * own_rows
    place = jnp.stack([(1 - c) * group_rows + first, c * group_rows + first, x, zh, y, zl, c])

    image_other, text_local = lax.optimization_barrier(
        (
            swapped(image_hidden, "zh"),
            lax.all_to_all(text_hidden, BRANCH, split_axis=0, concat_axis=1, tiled=True),
        )
    )
    image_pair = paired(image_hidden, image_other, zh)

    def from_x(send):
        return [send(0)] + [moved(send(k), ("x",), lambda i, k=k: ((i + k) % 4,)) for k in (3, 2, 1)]

    text_raw = jnp.dot(text_local, text_proj, preferred_element_type=F32)
    text_unit, text_length, text_emb = normalize(text_raw)
    near_text = lax.all_to_all(
        jnp.broadcast_to(text_emb[None], (8, own_rows, embed)), PLANE, 0, 0, tiled=True
    ).reshape(8 * own_rows, embed)
    text_own, _ = lax.optimization_barrier((text_hidden, text_local))
    image_parts, near_text, text_other = lax.optimization_barrier(
        (from_x(lambda k: image_pair), near_text, swapped(text_own, "zh"))
    )
    far_text = swapped(near_text, "c")
    group_emb, image_turned, hidden, image_unit, image_length = project_group(
        jnp.stack([x, branch_pos]), image_parts, image_proj
    )

    text_pair = paired(text_hidden, text_other, zh)
    text_parts = from_x(lambda k: text_pair)

    near_logits, near_rows, near_cols = half_logits(scale, group_emb, near_text)
    far_logits, far_rows, far_cols = half_logits(scale, group_emb, far_text)
    near_rows, far_rows, near_cols, far_cols, text_parts = lax.optimization_barrier(
        (near_rows, far_rows, near_cols, far_cols, text_parts)
    )

    def joined(mine, theirs):
        peak = jnp.maximum(mine[0], theirs[0])
        mass = mine[1] * jnp.exp(mine[0] - peak) + theirs[1] * jnp.exp(theirs[0] - peak)
        return jnp.stack([peak, mass])

    row_stats = joined(near_rows.reshape(2, 8, LANES), far_rows.reshape(2, 8, LANES))
    col_stats = jnp.concatenate([near_cols, far_cols], axis=1)
    col_in = swapped(jnp.concatenate([far_cols, near_cols], axis=1), "c")
    col_stats = joined(col_stats, col_in)

    def along(stats, axis):
        return [moved(stats, (axis,), lambda i, k=k: ((i + k) % 4,)) for k in (1, 3, 2)]

    def joined_four(own, others):
        return joined(joined(own, others[2]), joined(others[0], others[1]))

    row_in, col_in = along(row_stats, "x"), along(col_stats, "y")
    row_stats, col_stats = joined_four(row_stats, row_in), joined_four(col_stats, col_in)
    row_in, col_in = swapped(row_stats, "zh"), swapped(col_stats, "zl")
    row_stats, col_stats = joined(row_stats, row_in), joined(col_stats, col_in)
    row_lse = row_stats[0] + jnp.log(row_stats[1])
    col_lse = col_stats[0] + jnp.log(col_stats[1])

    row_partner = lax.dynamic_slice_in_dim(partner, data_pos * group_rows, group_rows, 0)
    row_partner = row_partner.astype(F32).reshape(8, LANES)
    near_lse, far_lse = col_lse[None, :group_rows], col_lse[None, group_rows:]
    far_low, far_part, far_terms = far_weights(
        place, scale, far_logits, row_lse, far_lse, row_partner, image_turned
    )
    text_arrived = swapped(far_part, "c")
    near_low, near_terms, image_coded = near_weights(
        place, scale, near_logits, row_lse, near_lse, row_partner, far_low, near_text, far_text
    )
    image_pieces = lax.all_to_all(image_coded, "x", 0, 0, tiled=True)
    text_coded = near_text_sum(place, scale, near_low, image_turned, text_arrived)
    text_pieces = [text_coded[0]] + [
        moved(
            text_coded[2 * k + h], PLANE, lambda i, j, k=k, h=h: ((i + k) % 4, j ^ h)
        )
        for k, h in ((2, 1), (2, 0), (1, 1), (3, 1), (1, 0), (3, 0), (0, 1))
    ]
    image_own, image_other = pair_sums(place, image_pieces)
    image_down = image_down_of(image_own, swapped(image_other, "zh"), image_unit, image_length)
    text_down = text_down_of(text_pieces, text_unit, text_length)
    image_grad = lax.dot_general(
        image_down, image_proj, (((1,), (1,)), ((), ())), preferred_element_type=F32
    ).astype(BF)
    text_grad = lax.dot_general(
        text_down, text_proj, (((1,), (1,)), ((), ())), preferred_element_type=F32
    ).astype(BF)

    def by_column(rows):
        return jnp.swapaxes(rows.reshape(own_rows, 8, -1), 0, 1)

    def redistributed(parts):
        sent = [by_column(a) for a in parts]
        got = lax.all_to_all(jnp.concatenate(sent, axis=2), BRANCH, 0, 0, tiled=True)
        return got.reshape(group_rows, -1)

    downs = redistributed((image_down, text_down))
    grads = redistributed((image_grad, text_grad))
    grad_image_hidden, grad_text_hidden = grads[:, :image_slab], grads[:, image_slab:]

    terms = jnp.sum(far_terms + near_terms, axis=1)
    own_row_terms = lax.dynamic_index_in_dim(row_lse, branch_pos, 0)
    own_col_terms = lax.dynamic_slice_in_dim(col_lse, (y * 2 + zl) * own_rows, own_rows, 0)
    loss_part = jnp.sum(own_row_terms) + jnp.sum(own_col_terms) - 2.0 * terms[1]
    width = embed // 8
    scalars = jnp.stack([loss_part / DENOMINATOR, terms[0]])
    scalars = jnp.pad(scalars[:, None], ((0, 6), (0, width - 1)))
    kept, sent = weight_sums(place, hidden, text_parts, downs, scalars)
    partial = kept + swapped(sent, "c")
    summed = jnp.sum(lax.all_to_all(partial, PLANE, 0, 0, tiled=True), axis=0)
    own, other = (
        moved(summed, AXES, lambda a, b, core, d, e, h=h: (d, e ^ h, core, a, b)) for h in (0, 1)
    )
    line = stacked(own[None], other[None], zl)
    lines = jnp.stack(
        [line] + [moved(line, ("y",), lambda i, k=k: ((i + k) % 4,)) for k in (3, 2, 1)]
    )
    lines = lax.dynamic_slice_in_dim(jnp.concatenate([lines, lines]), lax.rem(4 - y, 4), 4, 0)
    whole = stacked(lines[None], swapped(lines, "c")[None], c).reshape(2, 8, *summed.shape)

    def slab(first, rows):
        part = whole[:, :, first : first + rows]
        return part.transpose(0, 2, 1, 3).reshape(2 * rows, 8 * width)

    image_rows, text_rows = image_slab // 2, text_slab // 2
    totals = jnp.sum(whole[0, :, image_rows + text_rows :, 0], axis=0)
    return (
        totals[0].reshape(1),
        totals[1].reshape(1),
        grad_image_hidden,
        grad_text_hidden,
        slab(0, image_rows),
        slab(image_rows, text_rows),
    )


def solution(mesh):
    torus = Mesh(mesh.devices.reshape(tuple(SIZES.values())), AXES)
    placed = (P(DP, BRANCH), P(DP, BRANCH), P(), P(), P(), P())
    return jax.shard_map(
        per_device,
        mesh=torus,
        in_specs=placed,
        out_specs=(P(), P(), P(DP, BRANCH), P(DP, BRANCH), P(BRANCH, None), P(BRANCH, None)),
        check_vma=False,
    )
```

```python
import jax
import jax.numpy as jnp
import numpy as np
from jax import lax
from jax.experimental import pallas as pl
from jax.experimental.pallas import tpu as pltpu
from jax.sharding import Mesh
from jax.sharding import PartitionSpec as P

SIZES = {"y": 4, "zl": 2, "c": 2, "x": 4, "zh": 2}
AXES = tuple(SIZES)
DP = ("y", "zl", "c")
PLANE = ("y", "zl")
BRANCH = ("x", "zh")

NORM_EPSILON = 1e-06
FULL_SCALE = 32000.0
DENOMINATOR = 32768.0
LOW = -1e30
LANES = 128
TAIL = 16
RUN = 2048
BF = jnp.bfloat16
F32 = jnp.float32


def moved(value, axes, target):
    sizes = [SIZES[a] for a in axes]
    pairs = []
    for i in range(int(np.prod(sizes))):
        at = tuple(int(v) for v in np.unravel_index(i, sizes))
        pairs.append((i, int(np.ravel_multi_index(target(*at), sizes))))
    return lax.ppermute(value, axes, pairs)


def swapped(value, axis, mask=1):
    return moved(value, (axis,), lambda i: (i ^ mask,))


def paired(own, other, side):
    return jnp.where(
        side == 0,
        jnp.concatenate([own, other], axis=1),
        jnp.concatenate([other, own], axis=1),
    )


def stacked(own, other, side):
    return jnp.where(side == 0, jnp.concatenate([own, other]), jnp.concatenate([other, own]))


def normalize(raw_rows):
    lengths = jnp.sqrt(jnp.sum(raw_rows * raw_rows, axis=1, keepdims=True) + NORM_EPSILON)
    unit_rows = raw_rows / lengths
    return (unit_rows, lengths, unit_rows.astype(BF))


def eye():
    row = lax.broadcasted_iota(jnp.int32, (LANES, LANES), 0)
    return row == lax.broadcasted_iota(jnp.int32, (LANES, LANES), 1)


def as_row(column):
    return jnp.sum(jnp.where(eye(), column, 0.0), axis=0, keepdims=True)


def as_column(row):
    return jnp.sum(jnp.where(eye(), row, 0.0), axis=1, keepdims=True)


def exponent_of(top):
    return jnp.maximum(jnp.ceil(jnp.log2(top)), -80.0)


def to_fixed(values, exponent):
    return jnp.round(values * (FULL_SCALE * jnp.exp2(-exponent))).astype(jnp.int32).astype(jnp.int16)


def from_fixed(fixed, exponent):
    return fixed.astype(jnp.int32).astype(F32) * (jnp.exp2(exponent) / FULL_SCALE)


def tail(row):
    return jnp.broadcast_to(row, (TAIL, row.shape[1])).astype(jnp.int32).astype(jnp.int16)


def code_rows(values):
    exponent = exponent_of(jnp.max(jnp.abs(values), axis=1, keepdims=True))
    return to_fixed(values, exponent), tail(as_row(exponent))


def decode_rows(fixed, exponents):
    row = exponents.astype(jnp.int32).astype(F32)[:1]
    return from_fixed(fixed, as_column(row))


def kernel_call(body, name, out_shape, grid=(), in_specs=None, out_specs=None, scratch=(), prefetch=0, flops=0, moved_bytes=0):
    spec = pltpu.PrefetchScalarGridSpec(
        num_scalar_prefetch=prefetch,
        grid=grid,
        in_specs=in_specs,
        out_specs=out_specs,
        scratch_shapes=scratch,
    )
    return pl.pallas_call(
        body,
        out_shape=out_shape,
        grid_spec=spec,
        name=name,
        compiler_params=pltpu.CompilerParams(vmem_limit_bytes=18 * 2**20),
        cost_estimate=pl.CostEstimate(flops=flops, bytes_accessed=moved_bytes, transcendentals=0),
    )


def whole(shape):
    return pl.BlockSpec(shape, lambda *_: (0,) * len(shape))


def shaped(shape, dtype):
    return jax.ShapeDtypeStruct(shape, dtype)


def project_group(place, parts, proj):
    rows, width = parts[0].shape
    embed = proj.shape[1]
    step = 256

    def body(place_ref, a, b, c, d, proj_ref, emb_ref, turned_ref, hidden_ref, unit_ref, length_ref):
        i = pl.program_id(0)
        raw = None
        for k, part in enumerate((a, b, c, d)):
            first = pl.multiple_of(lax.rem(place_ref[0] + k, 4) * width, width)
            term = jnp.dot(
                part[...], proj_ref[pl.ds(first, width), :], preferred_element_type=F32
            )
            raw = term if raw is None else raw + term
            hidden_ref[:, k * width : (k + 1) * width] = part[...]
        length = jnp.sqrt(jnp.sum(raw * raw, axis=1, keepdims=True) + NORM_EPSILON)
        unit = raw / length
        emb_ref[...] = unit.astype(BF)
        turned_ref[...] = unit.T.astype(BF)
        for h in range(step // LANES):

            @pl.when(place_ref[1] == i * (step // LANES) + h)
            def _():
                unit_ref[...] = unit[h * LANES : (h + 1) * LANES]
                length_ref[...] = jnp.broadcast_to(
                    length[h * LANES : (h + 1) * LANES], (LANES, LANES)
                )

    return kernel_call(
        body,
        "project_group",
        (
            shaped((rows, embed), BF),
            shaped((embed, rows), BF),
            pltpu.HBM((rows, 4 * width), BF),
            pltpu.HBM((LANES, embed), F32),
            pltpu.HBM((LANES, LANES), F32),
        ),
        grid=(rows // step,),
        in_specs=[pl.BlockSpec((step, width), lambda i, *_: (i, 0))] * 4 + [whole(proj.shape)],
        out_specs=[
            pl.BlockSpec((step, embed), lambda i, *_: (i, 0)),
            pl.BlockSpec((embed, step), lambda i, *_: (0, i)),
            pl.BlockSpec((step, 4 * width), lambda i, *_: (i, 0)),
            whole((LANES, embed)),
            whole((LANES, LANES)),
        ],
        prefetch=1,
        flops=4 * 10**10,
        moved_bytes=6 * 2**20,
    )(place, *parts, proj)


def half_logits(scale, image_emb, text_emb):
    rows, embed = image_emb.shape
    columns = text_emb.shape[0]
    width, step = 512, 256

    def body(scale_ref, image_ref, text_ref, logits_ref, rows_ref, cols_ref, peak_ref, mass_ref):
        j = pl.program_id(0)

        @pl.when(j == 0)
        def _():
            peak_ref[...] = jnp.full(peak_ref.shape, LOW, F32)
            mass_ref[...] = jnp.zeros(mass_ref.shape, F32)

        col_peak = jnp.full((1, width), LOW, F32)
        col_mass = jnp.zeros((1, width), F32)
        for r in range(rows // step):
            at = slice(r * step, (r + 1) * step)
            value = scale_ref[0] * lax.dot_general(
                image_ref[at], text_ref[...], (((1,), (1,)), ((), ())), preferred_element_type=F32
            )
            logits_ref[at] = value
            tiles = [value[:, t : t + LANES] for t in range(0, width, LANES)]
            old = peak_ref[at]
            peak = old
            for tile in tiles:
                peak = jnp.maximum(peak, tile)
            mass = mass_ref[at] * jnp.exp(old - peak)
            for tile in tiles:
                mass = mass + jnp.exp(tile - peak)
            peak_ref[at] = peak
            mass_ref[at] = mass
            top = jnp.maximum(col_peak, jnp.max(value, axis=0, keepdims=True))
            col_mass = col_mass * jnp.exp(col_peak - top) + jnp.sum(
                jnp.exp(value - top), axis=0, keepdims=True
            )
            col_peak = top
        cols_ref[0:1] = col_peak
        cols_ref[1:2] = col_mass

        @pl.when(j == pl.num_programs(0) - 1)
        def _():
            for r in range(rows // LANES):
                at = slice(r * LANES, (r + 1) * LANES)
                peak = jnp.max(peak_ref[at], axis=1, keepdims=True)
                mass = jnp.sum(
                    mass_ref[at] * jnp.exp(peak_ref[at] - peak), axis=1, keepdims=True
                )
                rows_ref[r : r + 1] = as_row(peak)
                rows_ref[8 + r : 9 + r] = as_row(mass)

    return kernel_call(
        body,
        "half_logits",
        (shaped((rows, columns), F32), shaped((16, LANES), F32), shaped((2, columns), F32)),
        grid=(columns // width,),
        in_specs=[
            pl.BlockSpec(memory_space=pltpu.SMEM),
            whole(image_emb.shape),
            pl.BlockSpec((width, embed), lambda j: (j, 0)),
        ],
        out_specs=[
            pl.BlockSpec((rows, width), lambda j: (0, j)),
            whole((16, LANES)),
            pl.BlockSpec((2, width), lambda j: (0, j)),
        ],
        scratch=[pltpu.VMEM((rows, LANES), F32)] * 2,
        flops=2 * rows * columns * embed,
        moved_bytes=8 * 2**20,
    )(scale, image_emb, text_emb)


def weigh(logits, row_lse, col_lse, partner, first_id):
    rows, columns = logits.shape
    lane = lax.broadcasted_iota(jnp.int32, (1, LANES), 1)
    weights = []
    for t in range(columns // LANES):
        at = slice(t * LANES, (t + 1) * LANES)
        value = logits[:, at]
        matched = partner == lane + first_id(t)
        weight = jnp.exp(value - row_lse) + jnp.exp(value - col_lse[:, at])
        weight = (weight - jnp.where(matched, 2.0, 0.0)) * (1.0 / DENOMINATOR)
        scale_term = jnp.sum(weight * value, axis=0, keepdims=True)
        positive = jnp.sum(jnp.where(matched, value, 0.0), axis=0, keepdims=True)
        weights.append((weight.astype(BF), scale_term, positive))
    return weights


def columns_of(rows_ref, first, count):
    return jnp.concatenate(
        [as_column(rows_ref[first + r : first + r + 1]) for r in range(count)], axis=0
    )


def far_weights(place, scale, logits, row_lse, col_lse, partner, image_turned):
    rows, columns = logits.shape
    embed = image_turned.shape[0]
    width = 256

    def body(place_ref, scale_ref, logits_ref, row_ref, col_ref, partner_ref, turned_ref, low_ref, text_ref, terms_ref):
        j = pl.program_id(0)
        sums = [jnp.zeros((1, LANES), F32)] * 2
        for r in range(0, rows, 256):
            at = slice(r, r + 256)
            row = columns_of(row_ref, r // LANES, 2)
            part = columns_of(partner_ref, r // LANES, 2).astype(jnp.int32)
            made = weigh(
                logits_ref[at], row, col_ref[...], part, lambda t: place_ref[0] + (2 * j + t) * RUN
            )
            for t, (low, scale_term, positive) in enumerate(made):
                low_ref[at, t * LANES : (t + 1) * LANES] = low
                sums = [sums[0] + scale_term, sums[1] + positive]
        text_ref[...] = scale_ref[0] * jnp.dot(
            turned_ref[...], low_ref[...], preferred_element_type=F32
        )

        @pl.when(j == 0)
        def _():
            terms_ref[...] = jnp.zeros(terms_ref.shape, F32)

        terms_ref[0:1] += sums[0]
        terms_ref[1:2] += sums[1]

    return kernel_call(
        body,
        "far_weights",
        (
            shaped((rows, columns), BF),
            shaped((embed, columns), F32),
            shaped((8, LANES), F32),
        ),
        grid=(columns // width,),
        in_specs=[
            pl.BlockSpec(memory_space=pltpu.SMEM),
            pl.BlockSpec((rows, width), lambda j, *_: (0, j)),
            whole(row_lse.shape),
            pl.BlockSpec((1, width), lambda j, *_: (0, j)),
            whole(partner.shape),
            whole(image_turned.shape),
        ],
        out_specs=[
            pl.BlockSpec((rows, width), lambda j, *_: (0, j)),
            pl.BlockSpec((embed, width), lambda j, *_: (0, j)),
            whole((8, LANES)),
        ],
        prefetch=1,
        flops=2 * rows * columns * embed,
        moved_bytes=8 * 2**20,
    )(place, scale, logits, row_lse, col_lse, partner, image_turned)


def near_weights(place, scale, logits, row_lse, col_lse, partner, far_low, near_emb, far_emb):
    rows, columns = logits.shape
    embed = near_emb.shape[1]
    step = 256

    def body(place_ref, scale_ref, logits_ref, row_ref, col_ref, partner_ref, far_ref, near_emb_ref, far_emb_ref, *outs):
        low_ref, terms_ref, *coded_refs = outs
        k = pl.program_id(0)
        row = columns_of(row_ref, 0, 2)
        part = columns_of(partner_ref, 0, 2).astype(jnp.int32)
        made = weigh(logits_ref[...], row, col_ref[...], part, lambda t: place_ref[1] + t * RUN)
        sums = [jnp.zeros((1, LANES), F32)] * 2
        for t, (low, scale_term, positive) in enumerate(made):
            low_ref[:, t * LANES : (t + 1) * LANES] = low
            sums = [sums[0] + scale_term, sums[1] + positive]

        @pl.when(k == 0)
        def _():
            terms_ref[...] = jnp.zeros(terms_ref.shape, F32)

        terms_ref[0:1] += sums[0]
        terms_ref[1:2] += sums[1]
        image = jnp.dot(low_ref[...], near_emb_ref[...], preferred_element_type=F32)
        image = image + jnp.dot(far_ref[...], far_emb_ref[...], preferred_element_type=F32)
        image = scale_ref[0] * image
        coded = [code_rows(image[:LANES]), code_rows(image[LANES:])]
        for i in range(4):

            @pl.when(k == i)
            def _():
                for h in range(2):
                    fixed, exponents = coded[h]
                    coded_refs[i][h, :LANES] = fixed
                    coded_refs[i][h, LANES:] = jnp.zeros((TAIL, embed), jnp.int16)
                    coded_refs[i][h, LANES:, :LANES] = exponents

    def rows_at(k, place_ref):
        return lax.rem(place_ref[2] + k, 4)

    piece = (2, LANES + TAIL, embed)
    return kernel_call(
        body,
        "near_weights",
        (
            shaped((rows, columns), BF),
            shaped((8, LANES), F32),
            *[shaped(piece, jnp.int16)] * 4,
        ),
        grid=(4,),
        in_specs=[
            pl.BlockSpec(memory_space=pltpu.SMEM),
            pl.BlockSpec((step, columns), lambda k, p: (rows_at(k, p), 0)),
            pl.BlockSpec((None, 2, LANES), lambda k, p: (rows_at(k, p), 0, 0)),
            whole(col_lse.shape),
            pl.BlockSpec((None, 2, LANES), lambda k, p: (rows_at(k, p), 0, 0)),
            pl.BlockSpec((step, columns), lambda k, p: (rows_at(k, p), 0)),
            whole(near_emb.shape),
            whole(far_emb.shape),
        ],
        out_specs=[
            pl.BlockSpec((step, columns), lambda k, p: (rows_at(k, p), 0)),
            whole((8, LANES)),
            *[whole(piece)] * 4,
        ],
        prefetch=1,
        flops=4 * rows * columns * embed,
        moved_bytes=10 * 2**20,
    )(place, scale, logits, row_lse.reshape(4, 2, LANES), col_lse, partner.reshape(4, 2, LANES), far_low, near_emb, far_emb)


def near_text_sum(scale, low, image_turned, arrived):
    embed, columns = arrived.shape
    rows = low.shape[0]
    width = 256

    def body(scale_ref, low_ref, turned_ref, arrived_ref, out_ref):
        text = scale_ref[0] * jnp.dot(turned_ref[...], low_ref[...], preferred_element_type=F32)
        text = text + arrived_ref[...]
        exponent = exponent_of(jnp.max(jnp.abs(text), axis=0, keepdims=True))
        fixed = to_fixed(text, exponent)
        last = tail(exponent)
        for h in range(width // LANES):
            at = slice(h * LANES, (h + 1) * LANES)
            out_ref[h, :embed] = fixed[:, at]
            out_ref[h, embed:] = last[:, at]

    return kernel_call(
        body,
        "near_text_sum",
        shaped((columns // LANES, embed + TAIL, LANES), jnp.int16),
        grid=(columns // width,),
        in_specs=[
            pl.BlockSpec(memory_space=pltpu.SMEM),
            pl.BlockSpec((rows, width), lambda j: (0, j)),
            whole(image_turned.shape),
            pl.BlockSpec((embed, width), lambda j: (0, j)),
        ],
        out_specs=pl.BlockSpec((width // LANES, embed + TAIL, LANES), lambda j: (j, 0, 0)),
        flops=2 * 10**10,
        moved_bytes=8 * 2**20,
    )(scale, low, image_turned, arrived)


def pair_sums(place, pieces):
    embed = pieces[0].shape[-1]

    def body(place_ref, a, b, c, d, own_ref, other_ref):
        def total(h):
            parts = [decode_rows(p[h, :LANES], p[h, LANES:, :LANES]) for p in (a, b, c, d)]
            return (parts[0] + parts[1]) + (parts[2] + parts[3])

        own_ref[...] = total(place_ref[3])
        fixed, exponents = code_rows(total(1 - place_ref[3]))
        other_ref[:LANES] = fixed
        other_ref[LANES:] = jnp.zeros((TAIL, embed), jnp.int16)
        other_ref[LANES:, :LANES] = exponents

    return kernel_call(
        body,
        "pair_sums",
        (shaped((LANES, embed), F32), shaped((LANES + TAIL, embed), jnp.int16)),
        grid=(1,),
        in_specs=[whole(pieces[0].shape)] * 4,
        out_specs=[whole((LANES, embed)), whole((LANES + TAIL, embed))],
        prefetch=1,
        flops=4 * 10**10,
        moved_bytes=3 * 2**20,
    )(place, *pieces)


def transposed_downs(image_own, image_other, image_unit, image_length, text_pieces, text_unit, text_length):
    embed = image_unit.shape[1]
    run = embed // 8

    def body(own_ref, other_ref, image_unit_ref, image_length_ref, pieces_ref, text_unit_ref, text_length_ref, *outs):
        image_ref, text_ref, downs_ref = outs
        up = own_ref[...] + decode_rows(other_ref[:LANES], other_ref[LANES:, :LANES])
        unit = image_unit_ref[...]
        radial = jnp.sum(up * unit, axis=1, keepdims=True)
        image = ((up - unit * radial) / image_length_ref[:, :1]).T.astype(BF)
        up = jnp.zeros((embed, LANES), F32)
        for n in range(8):
            row = pieces_ref[n, embed:].astype(jnp.int32).astype(F32)[:1]
            up = up + from_fixed(pieces_ref[n, :embed], row)
        unit = text_unit_ref[...].T
        radial = jnp.sum(up * unit, axis=0, keepdims=True)
        text = ((up - unit * radial) / text_length_ref[...]).astype(BF)
        image_ref[...] = image
        text_ref[...] = text
        for k in range(8):
            downs_ref[k, :run] = image[k * run : (k + 1) * run]
            downs_ref[k, run:] = text[k * run : (k + 1) * run]

    args = (image_own, image_other, image_unit, image_length, text_pieces, text_unit, text_length)
    return kernel_call(
        body,
        "transposed_downs",
        (shaped((embed, LANES), BF), shaped((embed, LANES), BF), shaped((8, 2 * run, LANES), BF)),
        grid=(1,),
        in_specs=[whole(a.shape) for a in args],
        out_specs=[whole((embed, LANES)), whole((embed, LANES)), whole((8, 2 * run, LANES))],
        flops=10**7,
        moved_bytes=4 * 2**20,
    )(*args)


def hidden_grads(image_proj, image_turned, text_proj, text_turned):
    image_run, text_run = image_proj.shape[0] // 8, text_proj.shape[0] // 8

    def body(image_proj_ref, image_ref, text_proj_ref, text_ref, out_ref):
        for k in range(8):
            for proj, down, run, first in (
                (image_proj_ref, image_ref, image_run, 0),
                (text_proj_ref, text_ref, text_run, image_run),
            ):
                value = jnp.dot(
                    proj[k * run : (k + 1) * run], down[...], preferred_element_type=F32
                )
                out_ref[k, first : first + run] = value.astype(BF)

    shape = (8, image_run + text_run, LANES)
    args = (image_proj, image_turned, text_proj, text_turned)
    return kernel_call(
        body,
        "hidden_grads",
        shaped(shape, BF),
        grid=(1,),
        in_specs=[whole(a.shape) for a in args],
        out_specs=whole(shape),
        flops=5 * 10**8,
        moved_bytes=4 * 2**20,
    )(*args)


def turned_back(grads, image_run):
    text_run = grads.shape[1] - image_run

    def body(grads_ref, image_ref, text_ref):
        for n in range(8):
            at = slice(n * LANES, (n + 1) * LANES)
            image_ref[at] = grads_ref[n, :image_run].astype(F32).T.astype(BF)
            text_ref[at] = grads_ref[n, image_run:].astype(F32).T.astype(BF)

    rows = 8 * LANES
    return kernel_call(
        body,
        "turned_back",
        (shaped((rows, image_run), BF), shaped((rows, text_run), BF)),
        grid=(1,),
        in_specs=[whole(grads.shape)],
        out_specs=[whole((rows, image_run)), whole((rows, text_run))],
        flops=10**6,
        moved_bytes=2**20,
    )(grads)


def weight_sums(place, hidden, text_parts, downs, scalars):
    width = downs.shape[1] // 2
    image_run, text_run = hidden.shape[1] // 16, text_parts[0].shape[1] // 4
    both = image_run + text_run

    def body(place_ref, hidden_ref, *refs):
        text_refs, (downs_ref, scalars_ref, kept_ref, sent_ref) = refs[:4], refs[4:]
        even = place_ref[6] == 0
        downs_all = jnp.concatenate([downs_ref[n] for n in range(8)], axis=1)
        for ref in (kept_ref, sent_ref):
            ref[:, :, both:] = jnp.broadcast_to(scalars_ref[:, both:][None], (8, width, LANES - both))
        for k in range(4):
            first = 2 * lax.rem(place_ref[2] + k, 4)
            image = jnp.dot(
                downs_all[:width],
                hidden_ref[:, k * 4 * image_run : (k + 1) * 4 * image_run],
                preferred_element_type=F32,
            )
            text = jnp.dot(downs_all[width:], text_refs[k][...], preferred_element_type=F32)
            for value, run, at in ((image, image_run, 0), (text, text_run, image_run)):
                for j in range(2):
                    low = value[:, 2 * j * run : (2 * j + 1) * run]
                    high = value[:, (2 * j + 1) * run : (2 * j + 2) * run]
                    kept_ref[first + j, :, at : at + run] = jnp.where(even, low, high)
                    sent_ref[first + j, :, at : at + run] = jnp.where(even, high, low)

    shape = (8, width, LANES)
    args = (hidden, *text_parts, downs, scalars)
    return kernel_call(
        body,
        "weight_sums",
        (shaped(shape, F32),) * 2,
        grid=(1,),
        in_specs=[whole(a.shape) for a in args],
        out_specs=[whole(shape)] * 2,
        prefetch=1,
        flops=10**9,
        moved_bytes=6 * 2**20,
    )(place, *args)


def slabs(place, lines, other_lines, image_run, text_run):
    width = lines.shape[2]
    embed = 8 * width
    both = image_run + text_run

    def body(place_ref, lines_ref, other_ref, image_ref, text_ref, scalars_ref):
        for part, core in ((lines_ref, place_ref[6]), (other_ref, 1 - place_ref[6])):
            def at(i):
                return part[lax.rem(i + 4 - place_ref[4], 4)]

            turned = jnp.concatenate([at(i).reshape(2 * width, LANES) for i in range(4)]).T

            for side in range(2):

                @pl.when(core == side)
                def _():
                    image_ref[side * image_run : (side + 1) * image_run] = turned[:image_run]
                    text_ref[side * text_run : (side + 1) * text_run] = turned[image_run:both]
                    if side == 0:
                        scalars_ref[...] = turned[both : both + 8]

    return kernel_call(
        body,
        "slabs",
        (
            shaped((2 * image_run, embed), F32),
            shaped((2 * text_run, embed), F32),
            shaped((8, embed), F32),
        ),
        grid=(1,),
        in_specs=[whole(lines.shape)] * 2,
        out_specs=[whole((2 * image_run, embed)), whole((2 * text_run, embed)), whole((8, embed))],
        prefetch=1,
        flops=10**6,
        moved_bytes=2**21,
    )(place, lines, other_lines)


def per_device(image_hidden, text_hidden, image_proj, text_proj, log_inverse_sharpness, partner):
    y, zl, c, x, zh = (lax.axis_index(a) for a in AXES)
    branch_pos = x * 2 + zh
    data_pos = (y * 2 + zl) * 2 + c
    group_rows, image_slab = image_hidden.shape
    text_slab = text_hidden.shape[1]
    own_rows = group_rows // 8
    embed = image_proj.shape[1]
    scale = jnp.exp(log_inverse_sharpness)
    first = branch_pos * own_rows
    place = jnp.stack([(1 - c) * group_rows + first, c * group_rows + first, x, zh, y, zl, c])

    image_other, text_local = lax.optimization_barrier(
        (
            swapped(image_hidden, "zh"),
            lax.all_to_all(text_hidden, BRANCH, split_axis=0, concat_axis=1, tiled=True),
        )
    )
    image_pair = paired(image_hidden, image_other, zh)

    def from_x(send):
        return [send(0)] + [moved(send(k), ("x",), lambda i, k=k: ((i + k) % 4,)) for k in (3, 2, 1)]

    text_raw = jnp.dot(text_local, text_proj, preferred_element_type=F32)
    text_unit, text_length, text_emb = normalize(text_raw)
    near_text = lax.all_to_all(
        jnp.broadcast_to(text_emb[None], (8, own_rows, embed)), PLANE, 0, 0, tiled=True
    ).reshape(8 * own_rows, embed)
    text_own, _ = lax.optimization_barrier((text_hidden, text_local))
    image_parts, text_other = lax.optimization_barrier(
        (from_x(lambda k: image_pair), swapped(text_own, "zh"))
    )
    far_text = swapped(near_text, "c")
    group_emb, image_turned, hidden, image_unit, image_length = project_group(
        jnp.stack([x, branch_pos]), image_parts, image_proj
    )

    text_pair = paired(text_hidden, text_other, zh)
    near_logits, near_rows, near_cols = half_logits(scale, group_emb, near_text)
    far_logits, far_rows, far_cols = half_logits(scale, group_emb, far_text)

    def joined(mine, theirs):
        peak = jnp.maximum(mine[0], theirs[0])
        mass = mine[1] * jnp.exp(mine[0] - peak) + theirs[1] * jnp.exp(theirs[0] - peak)
        return jnp.stack([peak, mass])

    row_stats = joined(near_rows.reshape(2, 8, LANES), far_rows.reshape(2, 8, LANES))
    col_stats = jnp.concatenate([near_cols, far_cols], axis=1)
    col_in = swapped(jnp.concatenate([far_cols, near_cols], axis=1), "c")
    col_stats = joined(col_stats, col_in)

    def along(stats, axis):
        return [moved(stats, (axis,), lambda i, k=k: ((i + k) % 4,)) for k in (1, 3, 2)]

    def joined_four(own, others):
        return joined(joined(own, others[2]), joined(others[0], others[1]))

    row_in, col_in = along(row_stats, "x"), along(col_stats, "y")
    row_stats, col_stats = joined_four(row_stats, row_in), joined_four(col_stats, col_in)
    row_in, col_in = swapped(row_stats, "zh"), swapped(col_stats, "zl")
    row_stats, col_stats = joined(row_stats, row_in), joined(col_stats, col_in)
    row_stats, col_stats, text_pair = lax.optimization_barrier((row_stats, col_stats, text_pair))
    text_parts = from_x(lambda k: text_pair)
    row_lse = row_stats[0] + jnp.log(row_stats[1])
    col_lse = col_stats[0] + jnp.log(col_stats[1])

    row_partner = lax.dynamic_slice_in_dim(partner, data_pos * group_rows, group_rows, 0)
    row_partner = row_partner.astype(F32).reshape(8, LANES)
    near_lse, far_lse = col_lse[None, :group_rows], col_lse[None, group_rows:]
    far_low, far_part, far_terms = far_weights(
        place, scale, far_logits, row_lse, far_lse, row_partner, image_turned
    )
    text_arrived = swapped(far_part, "c")
    near_low, near_terms, *image_coded = near_weights(
        place, scale, near_logits, row_lse, near_lse, row_partner, far_low, near_text, far_text
    )
    image_coded, text_parts = lax.optimization_barrier((image_coded, text_parts))
    image_ring = from_x(lambda k: image_coded[k])
    text_coded = near_text_sum(scale, near_low, image_turned, text_arrived)
    text_pieces = lax.all_to_all(text_coded, PLANE, 0, 0, tiled=True)
    image_own, image_other = pair_sums(place, image_ring)
    image_down, text_down, downs = transposed_downs(
        image_own,
        swapped(image_other, "zh"),
        image_unit,
        image_length,
        text_pieces,
        text_unit,
        text_length.reshape(1, own_rows),
    )
    downs, grads = lax.optimization_barrier(
        (
            lax.all_to_all(downs, BRANCH, 0, 0, tiled=True),
            hidden_grads(image_proj, image_down, text_proj, text_down),
        )
    )
    grads = lax.all_to_all(grads, BRANCH, 0, 0, tiled=True)
    grad_image_hidden, grad_text_hidden = turned_back(grads, image_slab)

    terms = jnp.sum(far_terms + near_terms, axis=1)
    own_row_terms = lax.dynamic_index_in_dim(row_lse, branch_pos, 0)
    own_col_terms = lax.dynamic_slice_in_dim(col_lse, (y * 2 + zl) * own_rows, own_rows, 0)
    loss_part = jnp.sum(own_row_terms) + jnp.sum(own_col_terms) - 2.0 * terms[1]
    width = embed // 8
    scalars = jnp.stack([loss_part / DENOMINATOR, terms[0]])
    image_rows, text_rows = image_slab // 2, text_slab // 2
    both = image_rows + text_rows
    scalars = jnp.pad(scalars[None], ((0, width - 1), (both, LANES - both - 2)))
    kept, sent = weight_sums(place, hidden, text_parts, downs, scalars)
    partial = kept + swapped(sent, "c")
    summed = jnp.sum(lax.all_to_all(partial, PLANE, 0, 0, tiled=True), axis=0)
    own, other = (
        moved(summed, AXES, lambda a, b, core, d, e, h=h: (d, e ^ h, core, a, b)) for h in (0, 1)
    )
    line = stacked(own[None], other[None], zl)
    lines = jnp.stack(
        [line] + [moved(line, ("y",), lambda i, k=k: ((i + k) % 4,)) for k in (3, 2, 1)]
    )
    grad_image_proj, grad_text_proj, totals = slabs(
        place, lines, swapped(lines, "c"), image_rows, text_rows
    )
    totals = jnp.sum(totals.reshape(8, 8, width)[:, :, 0], axis=1)
    return (
        totals[0].reshape(1),
        totals[1].reshape(1),
        grad_image_hidden,
        grad_text_hidden,
        grad_image_proj,
        grad_text_proj,
    )


def solution(mesh):
    torus = Mesh(mesh.devices.reshape(tuple(SIZES.values())), AXES)
    placed = (P(DP, BRANCH), P(DP, BRANCH), P(), P(), P(), P())
    return jax.shard_map(
        per_device,
        mesh=torus,
        in_specs=placed,
        out_specs=(P(), P(), P(DP, BRANCH), P(DP, BRANCH), P(BRANCH, None), P(BRANCH, None)),
        check_vma=False,
    )
```

```python
import jax
import jax.numpy as jnp
import numpy as np
from jax import lax
from jax.experimental import pallas as pl
from jax.experimental.pallas import tpu as pltpu
from jax.sharding import Mesh
from jax.sharding import PartitionSpec as P

SIZES = {"y": 4, "zl": 2, "c": 2, "x": 4, "zh": 2}
AXES = tuple(SIZES)
DP = ("y", "zl", "c")
PLANE = ("y", "zl")
BRANCH = ("x", "zh")

NORM_EPSILON = 1e-06
FULL_SCALE = 32000.0
DENOMINATOR = 32768.0
LOW = -1e30
LANES = 128
TAIL = 16
RUN = 2048
BF = jnp.bfloat16
F32 = jnp.float32


def moved(value, axes, target):
    sizes = [SIZES[a] for a in axes]
    pairs = []
    for i in range(int(np.prod(sizes))):
        at = tuple(int(v) for v in np.unravel_index(i, sizes))
        pairs.append((i, int(np.ravel_multi_index(target(*at), sizes))))
    return lax.ppermute(value, axes, pairs)


def swapped(value, axis, mask=1):
    return moved(value, (axis,), lambda i: (i ^ mask,))


def paired(own, other, side):
    return jnp.where(
        side == 0,
        jnp.concatenate([own, other], axis=1),
        jnp.concatenate([other, own], axis=1),
    )


def stacked(own, other, side):
    return jnp.where(side == 0, jnp.concatenate([own, other]), jnp.concatenate([other, own]))


def normalize(raw_rows):
    lengths = jnp.sqrt(jnp.sum(raw_rows * raw_rows, axis=1, keepdims=True) + NORM_EPSILON)
    unit_rows = raw_rows / lengths
    return (unit_rows, lengths, unit_rows.astype(BF))


def eye():
    row = lax.broadcasted_iota(jnp.int32, (LANES, LANES), 0)
    return row == lax.broadcasted_iota(jnp.int32, (LANES, LANES), 1)


def as_row(column):
    return jnp.sum(jnp.where(eye(), column, 0.0), axis=0, keepdims=True)


def as_column(row):
    return jnp.sum(jnp.where(eye(), row, 0.0), axis=1, keepdims=True)


def exponent_of(top):
    return jnp.maximum(jnp.ceil(jnp.log2(top)), -80.0)


def to_fixed(values, exponent):
    return jnp.round(values * (FULL_SCALE * jnp.exp2(-exponent))).astype(jnp.int32).astype(jnp.int16)


def from_fixed(fixed, exponent):
    return fixed.astype(jnp.int32).astype(F32) * (jnp.exp2(exponent) / FULL_SCALE)


def tail(row):
    return jnp.broadcast_to(row, (TAIL, row.shape[1])).astype(jnp.int32).astype(jnp.int16)


def code_rows(values):
    exponent = exponent_of(jnp.max(jnp.abs(values), axis=1, keepdims=True))
    return to_fixed(values, exponent), tail(as_row(exponent))


def decode_rows(fixed, exponents):
    row = exponents.astype(jnp.int32).astype(F32)[:1]
    return from_fixed(fixed, as_column(row))


def kernel_call(body, name, out_shape, grid=(), in_specs=None, out_specs=None, scratch=(), prefetch=0, flops=0, moved_bytes=0):
    spec = pltpu.PrefetchScalarGridSpec(
        num_scalar_prefetch=prefetch,
        grid=grid,
        in_specs=in_specs,
        out_specs=out_specs,
        scratch_shapes=scratch,
    )
    return pl.pallas_call(
        body,
        out_shape=out_shape,
        grid_spec=spec,
        name=name,
        compiler_params=pltpu.CompilerParams(vmem_limit_bytes=18 * 2**20),
        cost_estimate=pl.CostEstimate(flops=flops, bytes_accessed=moved_bytes, transcendentals=0),
    )


def in_hbm(*arrays):
    return [pltpu.with_memory_space_constraint(a, pltpu.HBM) for a in arrays]


def whole(shape):
    return pl.BlockSpec(shape, lambda *_: (0,) * len(shape))


def shaped(shape, dtype):
    return jax.ShapeDtypeStruct(shape, dtype)


def project_group(place, parts, proj):
    rows, width = parts[0].shape
    embed = proj.shape[1]
    step = 256

    def body(place_ref, a, b, c, d, proj_ref, emb_ref, turned_ref, hidden_ref, unit_ref, length_ref):
        i = pl.program_id(0)
        raw = None
        for k, part in enumerate((a, b, c, d)):
            first = pl.multiple_of(lax.rem(place_ref[0] + k, 4) * width, width)
            term = jnp.dot(
                part[...], proj_ref[pl.ds(first, width), :], preferred_element_type=F32
            )
            raw = term if raw is None else raw + term
            hidden_ref[:, k * width : (k + 1) * width] = part[...]
        length = jnp.sqrt(jnp.sum(raw * raw, axis=1, keepdims=True) + NORM_EPSILON)
        unit = raw / length
        emb_ref[...] = unit.astype(BF)
        turned_ref[...] = unit.T.astype(BF)
        for h in range(step // LANES):

            @pl.when(place_ref[1] == i * (step // LANES) + h)
            def _():
                unit_ref[...] = unit[h * LANES : (h + 1) * LANES]
                length_ref[...] = jnp.broadcast_to(
                    length[h * LANES : (h + 1) * LANES], (LANES, LANES)
                )

    return kernel_call(
        body,
        "project_group",
        (
            shaped((rows, embed), BF),
            shaped((embed, rows), BF),
            pltpu.HBM((rows, 4 * width), BF),
            pltpu.HBM((LANES, embed), F32),
            pltpu.HBM((LANES, LANES), F32),
        ),
        grid=(rows // step,),
        in_specs=[pl.BlockSpec((step, width), lambda i, *_: (i, 0))] * 4 + [whole(proj.shape)],
        out_specs=[
            pl.BlockSpec((step, embed), lambda i, *_: (i, 0)),
            pl.BlockSpec((embed, step), lambda i, *_: (0, i)),
            pl.BlockSpec((step, 4 * width), lambda i, *_: (i, 0)),
            whole((LANES, embed)),
            whole((LANES, LANES)),
        ],
        prefetch=1,
        flops=4 * 10**10,
        moved_bytes=6 * 2**20,
    )(place, *parts, proj)


def half_logits(scale, image_emb, text_emb):
    rows, embed = image_emb.shape
    columns = text_emb.shape[0]
    width, step = 512, 256

    def body(scale_ref, image_ref, text_ref, logits_ref, rows_ref, cols_ref, peak_ref, mass_ref):
        j = pl.program_id(0)

        @pl.when(j == 0)
        def _():
            peak_ref[...] = jnp.full(peak_ref.shape, LOW, F32)
            mass_ref[...] = jnp.zeros(mass_ref.shape, F32)

        col_peak = jnp.full((1, width), LOW, F32)
        col_mass = jnp.zeros((1, width), F32)
        for r in range(rows // step):
            at = slice(r * step, (r + 1) * step)
            value = scale_ref[0] * lax.dot_general(
                image_ref[at], text_ref[...], (((1,), (1,)), ((), ())), preferred_element_type=F32
            )
            logits_ref[at] = value
            tiles = [value[:, t : t + LANES] for t in range(0, width, LANES)]
            old = peak_ref[at]
            peak = old
            for tile in tiles:
                peak = jnp.maximum(peak, tile)
            mass = mass_ref[at] * jnp.exp(old - peak)
            for tile in tiles:
                mass = mass + jnp.exp(tile - peak)
            peak_ref[at] = peak
            mass_ref[at] = mass
            top = jnp.maximum(col_peak, jnp.max(value, axis=0, keepdims=True))
            col_mass = col_mass * jnp.exp(col_peak - top) + jnp.sum(
                jnp.exp(value - top), axis=0, keepdims=True
            )
            col_peak = top
        cols_ref[0:1] = col_peak
        cols_ref[1:2] = col_mass

        @pl.when(j == pl.num_programs(0) - 1)
        def _():
            for r in range(rows // LANES):
                at = slice(r * LANES, (r + 1) * LANES)
                peak = jnp.max(peak_ref[at], axis=1, keepdims=True)
                mass = jnp.sum(
                    mass_ref[at] * jnp.exp(peak_ref[at] - peak), axis=1, keepdims=True
                )
                rows_ref[r : r + 1] = as_row(peak)
                rows_ref[8 + r : 9 + r] = as_row(mass)

    return kernel_call(
        body,
        "half_logits",
        (shaped((rows, columns), F32), shaped((16, LANES), F32), shaped((2, columns), F32)),
        grid=(columns // width,),
        in_specs=[
            pl.BlockSpec(memory_space=pltpu.SMEM),
            whole(image_emb.shape),
            pl.BlockSpec((width, embed), lambda j: (j, 0)),
        ],
        out_specs=[
            pl.BlockSpec((rows, width), lambda j: (0, j)),
            whole((16, LANES)),
            pl.BlockSpec((2, width), lambda j: (0, j)),
        ],
        scratch=[pltpu.VMEM((rows, LANES), F32)] * 2,
        flops=2 * rows * columns * embed,
        moved_bytes=8 * 2**20,
    )(scale, image_emb, text_emb)


def weigh(logits, row_lse, col_lse, partner, first_id):
    rows, columns = logits.shape
    lane = lax.broadcasted_iota(jnp.int32, (1, LANES), 1)
    weights = []
    for t in range(columns // LANES):
        at = slice(t * LANES, (t + 1) * LANES)
        value = logits[:, at]
        matched = partner == lane + first_id(t)
        weight = jnp.exp(value - row_lse) + jnp.exp(value - col_lse[:, at])
        weight = (weight - jnp.where(matched, 2.0, 0.0)) * (1.0 / DENOMINATOR)
        scale_term = jnp.sum(weight * value, axis=0, keepdims=True)
        positive = jnp.sum(jnp.where(matched, value, 0.0), axis=0, keepdims=True)
        weights.append((weight.astype(BF), scale_term, positive))
    return weights


def columns_of(rows_ref, first, count):
    return jnp.concatenate(
        [as_column(rows_ref[first + r : first + r + 1]) for r in range(count)], axis=0
    )


def far_weights(place, scale, logits, row_lse, col_lse, partner, image_turned):
    rows, columns = logits.shape
    embed = image_turned.shape[0]
    width = 256

    def body(place_ref, scale_ref, logits_ref, row_ref, col_ref, partner_ref, turned_ref, low_ref, text_ref, terms_ref):
        j = pl.program_id(0)
        sums = [jnp.zeros((1, LANES), F32)] * 2
        for r in range(0, rows, 256):
            at = slice(r, r + 256)
            row = columns_of(row_ref, r // LANES, 2)
            part = columns_of(partner_ref, r // LANES, 2).astype(jnp.int32)
            made = weigh(
                logits_ref[at], row, col_ref[...], part, lambda t: place_ref[0] + (2 * j + t) * RUN
            )
            for t, (low, scale_term, positive) in enumerate(made):
                low_ref[at, t * LANES : (t + 1) * LANES] = low
                sums = [sums[0] + scale_term, sums[1] + positive]
        text_ref[...] = scale_ref[0] * jnp.dot(
            turned_ref[...], low_ref[...], preferred_element_type=F32
        )

        @pl.when(j == 0)
        def _():
            terms_ref[...] = jnp.zeros(terms_ref.shape, F32)

        terms_ref[0:1] += sums[0]
        terms_ref[1:2] += sums[1]

    return kernel_call(
        body,
        "far_weights",
        (
            shaped((rows, columns), BF),
            shaped((embed, columns), F32),
            shaped((8, LANES), F32),
        ),
        grid=(columns // width,),
        in_specs=[
            pl.BlockSpec(memory_space=pltpu.SMEM),
            pl.BlockSpec((rows, width), lambda j, *_: (0, j)),
            whole(row_lse.shape),
            pl.BlockSpec((1, width), lambda j, *_: (0, j)),
            whole(partner.shape),
            whole(image_turned.shape),
        ],
        out_specs=[
            pl.BlockSpec((rows, width), lambda j, *_: (0, j)),
            pl.BlockSpec((embed, width), lambda j, *_: (0, j)),
            whole((8, LANES)),
        ],
        prefetch=1,
        flops=10**8,
        moved_bytes=8 * 2**20,
    )(place, scale, logits, row_lse, col_lse, partner, image_turned)


def near_weights(place, scale, logits, row_lse, col_lse, partner, far_low, near_emb, far_emb):
    rows, columns = logits.shape
    embed = near_emb.shape[1]
    step = 256

    def body(place_ref, scale_ref, logits_ref, row_ref, col_ref, partner_ref, far_ref, near_emb_ref, far_emb_ref, *outs):
        low_ref, terms_ref, *coded_refs = outs
        k = pl.program_id(0)
        row = columns_of(row_ref, 0, 2)
        part = columns_of(partner_ref, 0, 2).astype(jnp.int32)
        made = weigh(logits_ref[...], row, col_ref[...], part, lambda t: place_ref[1] + t * RUN)
        sums = [jnp.zeros((1, LANES), F32)] * 2
        for t, (low, scale_term, positive) in enumerate(made):
            low_ref[:, t * LANES : (t + 1) * LANES] = low
            sums = [sums[0] + scale_term, sums[1] + positive]

        @pl.when(k == 0)
        def _():
            terms_ref[...] = jnp.zeros(terms_ref.shape, F32)

        terms_ref[0:1] += sums[0]
        terms_ref[1:2] += sums[1]
        image = jnp.dot(low_ref[...], near_emb_ref[...], preferred_element_type=F32)
        image = image + jnp.dot(far_ref[...], far_emb_ref[...], preferred_element_type=F32)
        image = scale_ref[0] * image
        coded = [code_rows(image[:LANES]), code_rows(image[LANES:])]
        for i in range(4):

            @pl.when(k == i)
            def _():
                for h in range(2):
                    fixed, exponents = coded[h]
                    coded_refs[i][h, :LANES] = fixed
                    coded_refs[i][h, LANES:] = jnp.zeros((TAIL, embed), jnp.int16)
                    coded_refs[i][h, LANES:, :LANES] = exponents

    def rows_at(k, place_ref):
        return lax.rem(place_ref[2] + k, 4)

    piece = (2, LANES + TAIL, embed)
    return kernel_call(
        body,
        "near_weights",
        (
            shaped((rows, columns), BF),
            shaped((8, LANES), F32),
            *[pltpu.HBM(piece, jnp.int16)] * 4,
        ),
        grid=(4,),
        in_specs=[
            pl.BlockSpec(memory_space=pltpu.SMEM),
            pl.BlockSpec((step, columns), lambda k, p: (rows_at(k, p), 0)),
            pl.BlockSpec((None, 2, LANES), lambda k, p: (rows_at(k, p), 0, 0)),
            whole(col_lse.shape),
            pl.BlockSpec((None, 2, LANES), lambda k, p: (rows_at(k, p), 0, 0)),
            pl.BlockSpec((step, columns), lambda k, p: (rows_at(k, p), 0)),
            whole(near_emb.shape),
            whole(far_emb.shape),
        ],
        out_specs=[
            pl.BlockSpec((step, columns), lambda k, p: (rows_at(k, p), 0)),
            whole((8, LANES)),
            *[whole(piece)] * 4,
        ],
        prefetch=1,
        flops=10**8,
        moved_bytes=10 * 2**20,
    )(place, scale, logits, row_lse.reshape(4, 2, LANES), col_lse, partner.reshape(4, 2, LANES), far_low, near_emb, far_emb)


def near_text_sum(scale, low, image_turned, arrived):
    embed, columns = arrived.shape
    rows = low.shape[0]
    width = 256

    def body(scale_ref, low_ref, turned_ref, arrived_ref, out_ref):
        text = scale_ref[0] * jnp.dot(turned_ref[...], low_ref[...], preferred_element_type=F32)
        text = text + arrived_ref[...]
        exponent = exponent_of(jnp.max(jnp.abs(text), axis=0, keepdims=True))
        fixed = to_fixed(text, exponent)
        last = tail(exponent)
        for h in range(width // LANES):
            at = slice(h * LANES, (h + 1) * LANES)
            out_ref[h, :embed] = fixed[:, at]
            out_ref[h, embed:] = last[:, at]

    return kernel_call(
        body,
        "near_text_sum",
        pltpu.HBM((columns // LANES, embed + TAIL, LANES), jnp.int16),
        grid=(columns // width,),
        in_specs=[
            pl.BlockSpec(memory_space=pltpu.SMEM),
            pl.BlockSpec((rows, width), lambda j: (0, j)),
            whole(image_turned.shape),
            pl.BlockSpec((embed, width), lambda j: (0, j)),
        ],
        out_specs=pl.BlockSpec((width // LANES, embed + TAIL, LANES), lambda j: (j, 0, 0)),
        flops=2 * 10**10,
        moved_bytes=8 * 2**20,
    )(scale, low, image_turned, arrived)


def pair_sums(place, pieces):
    embed = pieces[0].shape[-1]

    def body(place_ref, a, b, c, d, own_ref, other_ref):
        def total(h):
            parts = [decode_rows(p[h, :LANES], p[h, LANES:, :LANES]) for p in (a, b, c, d)]
            return (parts[0] + parts[1]) + (parts[2] + parts[3])

        own_ref[...] = total(place_ref[3])
        fixed, exponents = code_rows(total(1 - place_ref[3]))
        other_ref[:LANES] = fixed
        other_ref[LANES:] = jnp.zeros((TAIL, embed), jnp.int16)
        other_ref[LANES:, :LANES] = exponents

    return kernel_call(
        body,
        "pair_sums",
        (pltpu.HBM((LANES, embed), F32), pltpu.HBM((LANES + TAIL, embed), jnp.int16)),
        grid=(1,),
        in_specs=[whole(pieces[0].shape)] * 4,
        out_specs=[whole((LANES, embed)), whole((LANES + TAIL, embed))],
        prefetch=1,
        flops=4 * 10**10,
        moved_bytes=3 * 2**20,
    )(place, *pieces)


def transposed_downs(image_own, image_other, image_unit, image_length, text_pieces, text_unit, text_length):
    embed = image_unit.shape[1]
    run = embed // 8

    def body(own_ref, other_ref, image_unit_ref, image_length_ref, pieces_ref, text_unit_ref, text_length_ref, *outs):
        image_ref, text_ref, downs_ref = outs
        up = own_ref[...] + decode_rows(other_ref[:LANES], other_ref[LANES:, :LANES])
        unit = image_unit_ref[...]
        radial = jnp.sum(up * unit, axis=1, keepdims=True)
        image = ((up - unit * radial) / image_length_ref[:, :1]).T.astype(BF)
        up = jnp.zeros((embed, LANES), F32)
        for n in range(8):
            row = pieces_ref[n, embed:].astype(jnp.int32).astype(F32)[:1]
            up = up + from_fixed(pieces_ref[n, :embed], row)
        unit = text_unit_ref[...].T
        radial = jnp.sum(up * unit, axis=0, keepdims=True)
        text = ((up - unit * radial) / text_length_ref[...]).astype(BF)
        image_ref[...] = image
        text_ref[...] = text
        for k in range(8):
            downs_ref[k, :run] = image[k * run : (k + 1) * run]
            downs_ref[k, run:] = text[k * run : (k + 1) * run]

    late = in_hbm(image_own, image_unit, image_length, text_unit)
    image_own, image_unit, image_length, text_unit = late
    args = (image_own, image_other, image_unit, image_length, text_pieces, text_unit, text_length)
    return kernel_call(
        body,
        "transposed_downs",
        (
            pltpu.HBM((embed, LANES), BF),
            pltpu.HBM((embed, LANES), BF),
            pltpu.HBM((8, 2 * run, LANES), BF),
        ),
        grid=(1,),
        in_specs=[whole(a.shape) for a in args],
        out_specs=[whole((embed, LANES)), whole((embed, LANES)), whole((8, 2 * run, LANES))],
        flops=10**7,
        moved_bytes=4 * 2**20,
    )(*args)


def hidden_grads(image_proj, image_turned, text_proj, text_turned):
    image_run, text_run = image_proj.shape[0] // 8, text_proj.shape[0] // 8

    def body(image_proj_ref, image_ref, text_proj_ref, text_ref, out_ref):
        for k in range(8):
            for proj, down, run, first in (
                (image_proj_ref, image_ref, image_run, 0),
                (text_proj_ref, text_ref, text_run, image_run),
            ):
                value = jnp.dot(
                    proj[k * run : (k + 1) * run], down[...], preferred_element_type=F32
                )
                out_ref[k, first : first + run] = value.astype(BF)

    shape = (8, image_run + text_run, LANES)
    args = in_hbm(image_proj, image_turned, text_proj, text_turned)
    return kernel_call(
        body,
        "hidden_grads",
        shaped(shape, BF),
        grid=(1,),
        in_specs=[whole(a.shape) for a in args],
        out_specs=whole(shape),
        flops=5 * 10**8,
        moved_bytes=4 * 2**20,
    )(*args)


def turned_back(grads, image_run):
    text_run = grads.shape[1] - image_run

    def body(grads_ref, image_ref, text_ref):
        for n in range(8):
            at = slice(n * LANES, (n + 1) * LANES)
            image_ref[at] = grads_ref[n, :image_run].astype(F32).T.astype(BF)
            text_ref[at] = grads_ref[n, image_run:].astype(F32).T.astype(BF)

    rows = 8 * LANES
    return kernel_call(
        body,
        "turned_back",
        (shaped((rows, image_run), BF), shaped((rows, text_run), BF)),
        grid=(1,),
        in_specs=[whole(grads.shape)],
        out_specs=[whole((rows, image_run)), whole((rows, text_run))],
        flops=10**6,
        moved_bytes=2**20,
    )(grads)


def weight_sums(place, hidden, text_parts, downs, scalars):
    width = downs.shape[1] // 2
    image_run, text_run = hidden.shape[1] // 16, text_parts[0].shape[1] // 4
    both = image_run + text_run

    def body(place_ref, hidden_ref, *refs):
        text_refs, (downs_ref, scalars_ref, kept_ref, sent_ref) = refs[:4], refs[4:]
        even = place_ref[6] == 0
        downs_all = jnp.concatenate([downs_ref[n] for n in range(8)], axis=1)
        for ref in (kept_ref, sent_ref):
            ref[:, :, both:] = jnp.broadcast_to(scalars_ref[:, both:][None], (8, width, LANES - both))
        for k in range(4):
            first = 2 * lax.rem(place_ref[2] + k, 4)
            image = jnp.dot(
                downs_all[:width],
                hidden_ref[:, k * 4 * image_run : (k + 1) * 4 * image_run],
                preferred_element_type=F32,
            )
            text = jnp.dot(downs_all[width:], text_refs[k][...], preferred_element_type=F32)
            for value, run, at in ((image, image_run, 0), (text, text_run, image_run)):
                for j in range(2):
                    low = value[:, 2 * j * run : (2 * j + 1) * run]
                    high = value[:, (2 * j + 1) * run : (2 * j + 2) * run]
                    kept_ref[first + j, :, at : at + run] = jnp.where(even, low, high)
                    sent_ref[first + j, :, at : at + run] = jnp.where(even, high, low)

    shape = (8, width, LANES)
    args = (*in_hbm(hidden, *text_parts), downs, scalars)
    return kernel_call(
        body,
        "weight_sums",
        (shaped(shape, F32),) * 2,
        grid=(1,),
        in_specs=[whole(a.shape) for a in args],
        out_specs=[whole(shape)] * 2,
        prefetch=1,
        flops=10**9,
        moved_bytes=6 * 2**20,
    )(place, *args)


def slabs(place, lines, other_lines, image_run, text_run):
    width = lines.shape[2]
    embed = 8 * width
    both = image_run + text_run

    def body(place_ref, lines_ref, other_ref, image_ref, text_ref, scalars_ref):
        for part, core in ((lines_ref, place_ref[6]), (other_ref, 1 - place_ref[6])):
            def at(i):
                return part[lax.rem(i + 4 - place_ref[4], 4)]

            turned = jnp.concatenate([at(i).reshape(2 * width, LANES) for i in range(4)]).T

            for side in range(2):

                @pl.when(core == side)
                def _():
                    image_ref[side * image_run : (side + 1) * image_run] = turned[:image_run]
                    text_ref[side * text_run : (side + 1) * text_run] = turned[image_run:both]
                    if side == 0:
                        scalars_ref[...] = turned[both : both + 8]

    return kernel_call(
        body,
        "slabs",
        (
            shaped((2 * image_run, embed), F32),
            shaped((2 * text_run, embed), F32),
            shaped((8, embed), F32),
        ),
        grid=(1,),
        in_specs=[whole(lines.shape)] * 2,
        out_specs=[whole((2 * image_run, embed)), whole((2 * text_run, embed)), whole((8, embed))],
        prefetch=1,
        flops=10**6,
        moved_bytes=2**21,
    )(place, lines, other_lines)


def per_device(image_hidden, text_hidden, image_proj, text_proj, log_inverse_sharpness, partner):
    y, zl, c, x, zh = (lax.axis_index(a) for a in AXES)
    branch_pos = x * 2 + zh
    data_pos = (y * 2 + zl) * 2 + c
    group_rows, image_slab = image_hidden.shape
    text_slab = text_hidden.shape[1]
    own_rows = group_rows // 8
    embed = image_proj.shape[1]
    scale = jnp.exp(log_inverse_sharpness)
    first = branch_pos * own_rows
    place = jnp.stack([(1 - c) * group_rows + first, c * group_rows + first, x, zh, y, zl, c])

    image_other, text_local = lax.optimization_barrier(
        (
            swapped(image_hidden, "zh"),
            lax.all_to_all(text_hidden, BRANCH, split_axis=0, concat_axis=1, tiled=True),
        )
    )
    image_pair = paired(image_hidden, image_other, zh)

    def from_x(send):
        return [send(0)] + [moved(send(k), ("x",), lambda i, k=k: ((i + k) % 4,)) for k in (3, 2, 1)]

    text_raw = jnp.dot(text_local, text_proj, preferred_element_type=F32)
    text_unit, text_length, text_emb = normalize(text_raw)
    near_text = lax.all_to_all(
        jnp.broadcast_to(text_emb[None], (8, own_rows, embed)), PLANE, 0, 0, tiled=True
    ).reshape(8 * own_rows, embed)
    text_own, _ = lax.optimization_barrier((text_hidden, text_local))
    image_parts, text_other = lax.optimization_barrier(
        (from_x(lambda k: image_pair), swapped(text_own, "zh"))
    )
    group_emb, image_turned, hidden, image_unit, image_length = project_group(
        jnp.stack([x, branch_pos]), image_parts, image_proj
    )

    text_pair = paired(text_hidden, text_other, zh)
    near_text, group_emb = lax.optimization_barrier((near_text, group_emb))
    far_text = swapped(near_text, "c")
    near_logits, near_rows, near_cols = half_logits(scale, group_emb, near_text)
    far_logits, far_rows, far_cols = half_logits(scale, group_emb, far_text)

    def joined(mine, theirs):
        peak = jnp.maximum(mine[0], theirs[0])
        mass = mine[1] * jnp.exp(mine[0] - peak) + theirs[1] * jnp.exp(theirs[0] - peak)
        return jnp.stack([peak, mass])

    row_stats = joined(near_rows.reshape(2, 8, LANES), far_rows.reshape(2, 8, LANES))
    col_stats = jnp.concatenate([near_cols, far_cols], axis=1)
    col_in = swapped(jnp.concatenate([far_cols, near_cols], axis=1), "c")
    col_stats = joined(col_stats, col_in)

    def along(stats, axis):
        return [moved(stats, (axis,), lambda i, k=k: ((i + k) % 4,)) for k in (1, 3, 2)]

    def joined_four(own, others):
        return joined(joined(own, others[2]), joined(others[0], others[1]))

    row_in, col_in = along(row_stats, "x"), along(col_stats, "y")
    row_stats, col_stats = joined_four(row_stats, row_in), joined_four(col_stats, col_in)
    row_in, col_in = swapped(row_stats, "zh"), swapped(col_stats, "zl")
    row_stats, col_stats = joined(row_stats, row_in), joined(col_stats, col_in)
    row_stats, col_stats, text_pair = lax.optimization_barrier((row_stats, col_stats, text_pair))
    text_parts = from_x(lambda k: text_pair)
    row_lse = row_stats[0] + jnp.log(row_stats[1])
    col_lse = col_stats[0] + jnp.log(col_stats[1])

    row_partner = lax.dynamic_slice_in_dim(partner, data_pos * group_rows, group_rows, 0)
    row_partner = row_partner.astype(F32).reshape(8, LANES)
    near_lse, far_lse = col_lse[None, :group_rows], col_lse[None, group_rows:]
    far_low, far_part, far_terms = far_weights(
        place, scale, far_logits, row_lse, far_lse, row_partner, image_turned
    )
    text_arrived = swapped(far_part, "c")
    far_low, text_parts[1], text_parts[3] = lax.optimization_barrier(
        (far_low, text_parts[1], text_parts[3])
    )
    near_low, near_terms, *image_coded = near_weights(
        place, scale, near_logits, row_lse, near_lse, row_partner, far_low, near_text, far_text
    )
    image_coded, text_parts = lax.optimization_barrier((image_coded, text_parts))
    image_ring = from_x(lambda k: image_coded[k])
    text_coded = near_text_sum(scale, near_low, image_turned, text_arrived)
    text_pieces = lax.all_to_all(text_coded, PLANE, 0, 0, tiled=True)
    image_own, image_other = pair_sums(place, image_ring)
    image_down, text_down, downs = transposed_downs(
        image_own,
        swapped(image_other, "zh"),
        image_unit,
        image_length,
        text_pieces,
        text_unit,
        text_length.reshape(1, own_rows),
    )
    downs, grads = lax.optimization_barrier(
        (
            lax.all_to_all(downs, BRANCH, 0, 0, tiled=True),
            hidden_grads(image_proj, image_down, text_proj, text_down),
        )
    )
    grads = lax.all_to_all(grads, BRANCH, 0, 0, tiled=True)
    grad_image_hidden, grad_text_hidden = turned_back(grads, image_slab)

    terms = jnp.sum(far_terms + near_terms, axis=1)
    own_row_terms = lax.dynamic_index_in_dim(row_lse, branch_pos, 0)
    own_col_terms = lax.dynamic_slice_in_dim(col_lse, (y * 2 + zl) * own_rows, own_rows, 0)
    loss_part = jnp.sum(own_row_terms) + jnp.sum(own_col_terms) - 2.0 * terms[1]
    width = embed // 8
    scalars = jnp.stack([loss_part / DENOMINATOR, terms[0]])
    image_rows, text_rows = image_slab // 2, text_slab // 2
    both = image_rows + text_rows
    scalars = jnp.pad(scalars[None], ((0, width - 1), (both, LANES - both - 2)))
    kept, sent = weight_sums(place, hidden, text_parts, downs, scalars)
    partial = kept + swapped(sent, "c")
    summed = jnp.sum(lax.all_to_all(partial, PLANE, 0, 0, tiled=True), axis=0)
    own, other = (
        moved(summed, AXES, lambda a, b, core, d, e, h=h: (d, e ^ h, core, a, b)) for h in (0, 1)
    )
    line = stacked(own[None], other[None], zl)
    lines = jnp.stack(
        [line] + [moved(line, ("y",), lambda i, k=k: ((i + k) % 4,)) for k in (3, 2, 1)]
    )
    grad_image_proj, grad_text_proj, totals = slabs(
        place, lines, swapped(lines, "c"), image_rows, text_rows
    )
    totals = jnp.sum(totals.reshape(8, 8, width)[:, :, 0], axis=1)
    return (
        totals[0].reshape(1),
        totals[1].reshape(1),
        grad_image_hidden,
        grad_text_hidden,
        grad_image_proj,
        grad_text_proj,
    )


def solution(mesh):
    torus = Mesh(mesh.devices.reshape(tuple(SIZES.values())), AXES)
    placed = (P(DP, BRANCH), P(DP, BRANCH), P(), P(), P(), P())
    return jax.shard_map(
        per_device,
        mesh=torus,
        in_specs=placed,
        out_specs=(P(), P(), P(DP, BRANCH), P(DP, BRANCH), P(BRANCH, None), P(BRANCH, None)),
        check_vma=False,
    )
```

```python
import jax
import jax.numpy as jnp
import numpy as np
from jax import lax
from jax.experimental import pallas as pl
from jax.experimental.pallas import tpu as pltpu
from jax.sharding import Mesh
from jax.sharding import PartitionSpec as P

SIZES = {"y": 4, "zl": 2, "c": 2, "x": 4, "zh": 2}
AXES = tuple(SIZES)
DP = ("y", "zl", "c")
PLANE = ("y", "zl")
BRANCH = ("x", "zh")

NORM_EPSILON = 1e-06
FULL_SCALE = 32000.0
DENOMINATOR = 32768.0
LOW = -1e30
LANES = 128
TAIL = 16
RUN = 2048
BF = jnp.bfloat16
F32 = jnp.float32


def moved(value, axes, target):
    sizes = [SIZES[a] for a in axes]
    pairs = []
    for i in range(int(np.prod(sizes))):
        at = tuple(int(v) for v in np.unravel_index(i, sizes))
        pairs.append((i, int(np.ravel_multi_index(target(*at), sizes))))
    return lax.ppermute(value, axes, pairs)


def swapped(value, axis, mask=1):
    return moved(value, (axis,), lambda i: (i ^ mask,))


def paired(own, other, side):
    return jnp.where(
        side == 0,
        jnp.concatenate([own, other], axis=1),
        jnp.concatenate([other, own], axis=1),
    )


def stacked(own, other, side):
    return jnp.where(side == 0, jnp.concatenate([own, other]), jnp.concatenate([other, own]))


def normalize(raw_rows):
    lengths = jnp.sqrt(jnp.sum(raw_rows * raw_rows, axis=1, keepdims=True) + NORM_EPSILON)
    unit_rows = raw_rows / lengths
    return (unit_rows, lengths, unit_rows.astype(BF))


def eye():
    row = lax.broadcasted_iota(jnp.int32, (LANES, LANES), 0)
    return row == lax.broadcasted_iota(jnp.int32, (LANES, LANES), 1)


def as_row(column):
    return jnp.sum(jnp.where(eye(), column, 0.0), axis=0, keepdims=True)


def as_column(row):
    return jnp.sum(jnp.where(eye(), row, 0.0), axis=1, keepdims=True)


def exponent_of(top):
    return jnp.maximum(jnp.ceil(jnp.log2(top)), -80.0)


def to_fixed(values, exponent):
    return jnp.round(values * (FULL_SCALE * jnp.exp2(-exponent))).astype(jnp.int32).astype(jnp.int16)


def from_fixed(fixed, exponent):
    return fixed.astype(jnp.int32).astype(F32) * (jnp.exp2(exponent) / FULL_SCALE)


def tail(row):
    return jnp.broadcast_to(row, (TAIL, row.shape[1])).astype(jnp.int32).astype(jnp.int16)


def code_rows(values):
    exponent = exponent_of(jnp.max(jnp.abs(values), axis=1, keepdims=True))
    return to_fixed(values, exponent), tail(as_row(exponent))


def decode_rows(fixed, exponents):
    row = exponents.astype(jnp.int32).astype(F32)[:1]
    return from_fixed(fixed, as_column(row))


def kernel_call(body, name, out_shape, grid=(), in_specs=None, out_specs=None, scratch=(), prefetch=0, flops=0, moved_bytes=0):
    spec = pltpu.PrefetchScalarGridSpec(
        num_scalar_prefetch=prefetch,
        grid=grid,
        in_specs=in_specs,
        out_specs=out_specs,
        scratch_shapes=scratch,
    )
    return pl.pallas_call(
        body,
        out_shape=out_shape,
        grid_spec=spec,
        name=name,
        compiler_params=pltpu.CompilerParams(vmem_limit_bytes=18 * 2**20),
        cost_estimate=pl.CostEstimate(flops=flops, bytes_accessed=moved_bytes, transcendentals=0),
    )


def in_hbm(*arrays):
    return [pltpu.with_memory_space_constraint(a, pltpu.HBM) for a in arrays]


def whole(shape):
    return pl.BlockSpec(shape, lambda *_: (0,) * len(shape))


def shaped(shape, dtype):
    return jax.ShapeDtypeStruct(shape, dtype)


def project_group(place, parts, proj):
    rows, width = parts[0].shape
    embed = proj.shape[1]
    step = 256

    def body(place_ref, a, b, c, d, proj_ref, emb_ref, turned_ref, hidden_ref, unit_ref, length_ref):
        i = pl.program_id(0)
        raw = None
        for k, part in enumerate((a, b, c, d)):
            first = pl.multiple_of(lax.rem(place_ref[0] + k, 4) * width, width)
            term = jnp.dot(
                part[...], proj_ref[pl.ds(first, width), :], preferred_element_type=F32
            )
            raw = term if raw is None else raw + term
            hidden_ref[:, k * width : (k + 1) * width] = part[...]
        length = jnp.sqrt(jnp.sum(raw * raw, axis=1, keepdims=True) + NORM_EPSILON)
        unit = raw / length
        emb_ref[...] = unit.astype(BF)
        turned_ref[...] = unit.T.astype(BF)
        for h in range(step // LANES):

            @pl.when(place_ref[1] == i * (step // LANES) + h)
            def _():
                unit_ref[...] = unit[h * LANES : (h + 1) * LANES]
                length_ref[...] = jnp.broadcast_to(
                    length[h * LANES : (h + 1) * LANES], (LANES, LANES)
                )

    return kernel_call(
        body,
        "project_group",
        (
            shaped((rows, embed), BF),
            shaped((embed, rows), BF),
            pltpu.HBM((rows, 4 * width), BF),
            pltpu.HBM((LANES, embed), F32),
            pltpu.HBM((LANES, LANES), F32),
        ),
        grid=(rows // step,),
        in_specs=[pl.BlockSpec((step, width), lambda i, *_: (i, 0))] * 4 + [whole(proj.shape)],
        out_specs=[
            pl.BlockSpec((step, embed), lambda i, *_: (i, 0)),
            pl.BlockSpec((embed, step), lambda i, *_: (0, i)),
            pl.BlockSpec((step, 4 * width), lambda i, *_: (i, 0)),
            whole((LANES, embed)),
            whole((LANES, LANES)),
        ],
        prefetch=1,
        flops=4 * 10**10,
        moved_bytes=6 * 2**20,
    )(place, *parts, proj)


def half_logits(scale, image_emb, text_emb):
    rows, embed = image_emb.shape
    columns = text_emb.shape[0]
    width, step = 512, 256

    def body(scale_ref, image_ref, text_ref, logits_ref, rows_ref, cols_ref, peak_ref, mass_ref):
        j = pl.program_id(0)

        @pl.when(j == 0)
        def _():
            peak_ref[...] = jnp.full(peak_ref.shape, LOW, F32)
            mass_ref[...] = jnp.zeros(mass_ref.shape, F32)

        col_peak = jnp.full((1, width), LOW, F32)
        col_mass = jnp.zeros((1, width), F32)
        for r in range(rows // step):
            at = slice(r * step, (r + 1) * step)
            value = scale_ref[0] * lax.dot_general(
                image_ref[at], text_ref[...], (((1,), (1,)), ((), ())), preferred_element_type=F32
            )
            logits_ref[at] = value
            tiles = [value[:, t : t + LANES] for t in range(0, width, LANES)]
            old = peak_ref[at]
            peak = old
            for tile in tiles:
                peak = jnp.maximum(peak, tile)
            mass = mass_ref[at] * jnp.exp(old - peak)
            for tile in tiles:
                mass = mass + jnp.exp(tile - peak)
            peak_ref[at] = peak
            mass_ref[at] = mass
            top = jnp.maximum(col_peak, jnp.max(value, axis=0, keepdims=True))
            col_mass = col_mass * jnp.exp(col_peak - top) + jnp.sum(
                jnp.exp(value - top), axis=0, keepdims=True
            )
            col_peak = top
        cols_ref[0:1] = col_peak
        cols_ref[1:2] = col_mass

        @pl.when(j == pl.num_programs(0) - 1)
        def _():
            for r in range(rows // LANES):
                at = slice(r * LANES, (r + 1) * LANES)
                peak = jnp.max(peak_ref[at], axis=1, keepdims=True)
                mass = jnp.sum(
                    mass_ref[at] * jnp.exp(peak_ref[at] - peak), axis=1, keepdims=True
                )
                rows_ref[r : r + 1] = as_row(peak)
                rows_ref[8 + r : 9 + r] = as_row(mass)

    return kernel_call(
        body,
        "half_logits",
        (shaped((rows, columns), F32), shaped((16, LANES), F32), shaped((2, columns), F32)),
        grid=(columns // width,),
        in_specs=[
            pl.BlockSpec(memory_space=pltpu.SMEM),
            whole(image_emb.shape),
            pl.BlockSpec((width, embed), lambda j: (j, 0)),
        ],
        out_specs=[
            pl.BlockSpec((rows, width), lambda j: (0, j)),
            whole((16, LANES)),
            pl.BlockSpec((2, width), lambda j: (0, j)),
        ],
        scratch=[pltpu.VMEM((rows, LANES), F32)] * 2,
        flops=2 * rows * columns * embed,
        moved_bytes=8 * 2**20,
    )(scale, image_emb, text_emb)


def weigh(logits, row_lse, col_lse, partner, first_id):
    rows, columns = logits.shape
    lane = lax.broadcasted_iota(jnp.int32, (1, LANES), 1)
    weights = []
    for t in range(columns // LANES):
        at = slice(t * LANES, (t + 1) * LANES)
        value = logits[:, at]
        matched = partner == lane + first_id(t)
        weight = jnp.exp(value - row_lse) + jnp.exp(value - col_lse[:, at])
        weight = (weight - jnp.where(matched, 2.0, 0.0)) * (1.0 / DENOMINATOR)
        scale_term = jnp.sum(weight * value, axis=0, keepdims=True)
        positive = jnp.sum(jnp.where(matched, value, 0.0), axis=0, keepdims=True)
        weights.append((weight.astype(BF), scale_term, positive))
    return weights


def columns_of(rows_ref, first, count):
    return jnp.concatenate(
        [as_column(rows_ref[first + r : first + r + 1]) for r in range(count)], axis=0
    )


def far_weights(place, scale, logits, row_lse, col_lse, partner, image_turned):
    rows, columns = logits.shape
    embed = image_turned.shape[0]
    width = 256

    def body(place_ref, scale_ref, logits_ref, row_ref, col_ref, partner_ref, turned_ref, low_ref, text_ref, terms_ref):
        j = pl.program_id(0)
        sums = [jnp.zeros((1, LANES), F32)] * 2
        for r in range(0, rows, 256):
            at = slice(r, r + 256)
            row = columns_of(row_ref, r // LANES, 2)
            part = columns_of(partner_ref, r // LANES, 2).astype(jnp.int32)
            made = weigh(
                logits_ref[at], row, col_ref[...], part, lambda t: place_ref[0] + (2 * j + t) * RUN
            )
            for t, (low, scale_term, positive) in enumerate(made):
                low_ref[at, t * LANES : (t + 1) * LANES] = low
                sums = [sums[0] + scale_term, sums[1] + positive]
        text_ref[...] = scale_ref[0] * jnp.dot(
            turned_ref[...], low_ref[...], preferred_element_type=F32
        )

        @pl.when(j == 0)
        def _():
            terms_ref[...] = jnp.zeros(terms_ref.shape, F32)

        terms_ref[0:1] += sums[0]
        terms_ref[1:2] += sums[1]

    return kernel_call(
        body,
        "far_weights",
        (
            shaped((rows, columns), BF),
            shaped((embed, columns), F32),
            shaped((8, LANES), F32),
        ),
        grid=(columns // width,),
        in_specs=[
            pl.BlockSpec(memory_space=pltpu.SMEM),
            pl.BlockSpec((rows, width), lambda j, *_: (0, j)),
            whole(row_lse.shape),
            pl.BlockSpec((1, width), lambda j, *_: (0, j)),
            whole(partner.shape),
            whole(image_turned.shape),
        ],
        out_specs=[
            pl.BlockSpec((rows, width), lambda j, *_: (0, j)),
            pl.BlockSpec((embed, width), lambda j, *_: (0, j)),
            whole((8, LANES)),
        ],
        prefetch=1,
        flops=10**8,
        moved_bytes=8 * 2**20,
    )(place, scale, logits, row_lse, col_lse, partner, image_turned)


def near_weights(place, scale, logits, row_lse, col_lse, partner, far_low, near_emb, far_emb):
    rows, columns = logits.shape
    embed = near_emb.shape[1]
    step = 256

    def body(place_ref, scale_ref, logits_ref, row_ref, col_ref, partner_ref, far_ref, near_emb_ref, far_emb_ref, *outs):
        low_ref, terms_ref, *coded_refs = outs
        k = pl.program_id(0)
        row = columns_of(row_ref, 0, 2)
        part = columns_of(partner_ref, 0, 2).astype(jnp.int32)
        made = weigh(logits_ref[...], row, col_ref[...], part, lambda t: place_ref[1] + t * RUN)
        sums = [jnp.zeros((1, LANES), F32)] * 2
        for t, (low, scale_term, positive) in enumerate(made):
            low_ref[:, t * LANES : (t + 1) * LANES] = low
            sums = [sums[0] + scale_term, sums[1] + positive]

        @pl.when(k == 0)
        def _():
            terms_ref[...] = jnp.zeros(terms_ref.shape, F32)

        terms_ref[0:1] += sums[0]
        terms_ref[1:2] += sums[1]
        image = jnp.dot(low_ref[...], near_emb_ref[...], preferred_element_type=F32)
        image = image + jnp.dot(far_ref[...], far_emb_ref[...], preferred_element_type=F32)
        image = scale_ref[0] * image
        coded = [code_rows(image[:LANES]), code_rows(image[LANES:])]
        for i in range(4):

            @pl.when(k == i)
            def _():
                for h in range(2):
                    fixed, exponents = coded[h]
                    coded_refs[i][h, :LANES] = fixed
                    coded_refs[i][h, LANES:] = jnp.zeros((TAIL, embed), jnp.int16)
                    coded_refs[i][h, LANES:, :LANES] = exponents

    def rows_at(k, place_ref):
        return lax.rem(place_ref[2] + k, 4)

    piece = (2, LANES + TAIL, embed)
    return kernel_call(
        body,
        "near_weights",
        (
            shaped((rows, columns), BF),
            shaped((8, LANES), F32),
            *[pltpu.HBM(piece, jnp.int16)] * 4,
        ),
        grid=(4,),
        in_specs=[
            pl.BlockSpec(memory_space=pltpu.SMEM),
            pl.BlockSpec((step, columns), lambda k, p: (rows_at(k, p), 0)),
            pl.BlockSpec((None, 2, LANES), lambda k, p: (rows_at(k, p), 0, 0)),
            whole(col_lse.shape),
            pl.BlockSpec((None, 2, LANES), lambda k, p: (rows_at(k, p), 0, 0)),
            pl.BlockSpec((step, columns), lambda k, p: (rows_at(k, p), 0)),
            whole(near_emb.shape),
            whole(far_emb.shape),
        ],
        out_specs=[
            pl.BlockSpec((step, columns), lambda k, p: (rows_at(k, p), 0)),
            whole((8, LANES)),
            *[whole(piece)] * 4,
        ],
        prefetch=1,
        flops=10**8,
        moved_bytes=10 * 2**20,
    )(place, scale, logits, row_lse.reshape(4, 2, LANES), col_lse, partner.reshape(4, 2, LANES), far_low, near_emb, far_emb)


def near_text_sum(scale, low, image_turned, arrived):
    embed, columns = arrived.shape
    rows = low.shape[0]
    width = 256

    def body(scale_ref, low_ref, turned_ref, arrived_ref, out_ref):
        text = scale_ref[0] * jnp.dot(turned_ref[...], low_ref[...], preferred_element_type=F32)
        text = text + arrived_ref[...]
        exponent = exponent_of(jnp.max(jnp.abs(text), axis=0, keepdims=True))
        fixed = to_fixed(text, exponent)
        last = tail(exponent)
        for h in range(width // LANES):
            at = slice(h * LANES, (h + 1) * LANES)
            out_ref[h, :embed] = fixed[:, at]
            out_ref[h, embed:] = last[:, at]

    return kernel_call(
        body,
        "near_text_sum",
        pltpu.HBM((columns // LANES, embed + TAIL, LANES), jnp.int16),
        grid=(columns // width,),
        in_specs=[
            pl.BlockSpec(memory_space=pltpu.SMEM),
            pl.BlockSpec((rows, width), lambda j: (0, j)),
            whole(image_turned.shape),
            pl.BlockSpec((embed, width), lambda j: (0, j)),
        ],
        out_specs=pl.BlockSpec((width // LANES, embed + TAIL, LANES), lambda j: (j, 0, 0)),
        flops=2 * 10**10,
        moved_bytes=8 * 2**20,
    )(scale, low, image_turned, arrived)


def pair_sums(place, pieces):
    embed = pieces[0].shape[-1]

    def body(place_ref, a, b, c, d, own_ref, other_ref):
        def total(h):
            parts = [decode_rows(p[h, :LANES], p[h, LANES:, :LANES]) for p in (a, b, c, d)]
            return (parts[0] + parts[1]) + (parts[2] + parts[3])

        own_ref[...] = total(place_ref[3])
        fixed, exponents = code_rows(total(1 - place_ref[3]))
        other_ref[:LANES] = fixed
        other_ref[LANES:] = jnp.zeros((TAIL, embed), jnp.int16)
        other_ref[LANES:, :LANES] = exponents

    return kernel_call(
        body,
        "pair_sums",
        (pltpu.HBM((LANES, embed), F32), pltpu.HBM((LANES + TAIL, embed), jnp.int16)),
        grid=(1,),
        in_specs=[whole(pieces[0].shape)] * 4,
        out_specs=[whole((LANES, embed)), whole((LANES + TAIL, embed))],
        prefetch=1,
        flops=4 * 10**10,
        moved_bytes=3 * 2**20,
    )(place, *pieces)


def transposed_downs(image_own, image_other, image_unit, image_length, text_pieces, text_unit, text_length):
    embed = image_unit.shape[1]
    run = embed // 8

    def body(own_ref, other_ref, image_unit_ref, image_length_ref, pieces_ref, text_unit_ref, text_length_ref, *outs):
        image_ref, text_ref, downs_ref = outs
        up = own_ref[...] + decode_rows(other_ref[:LANES], other_ref[LANES:, :LANES])
        unit = image_unit_ref[...]
        radial = jnp.sum(up * unit, axis=1, keepdims=True)
        image = ((up - unit * radial) / image_length_ref[:, :1]).T.astype(BF)
        up = jnp.zeros((embed, LANES), F32)
        for n in range(8):
            row = pieces_ref[n, embed:].astype(jnp.int32).astype(F32)[:1]
            up = up + from_fixed(pieces_ref[n, :embed], row)
        unit = text_unit_ref[...].T
        radial = jnp.sum(up * unit, axis=0, keepdims=True)
        text = ((up - unit * radial) / text_length_ref[...]).astype(BF)
        image_ref[...] = image
        text_ref[...] = text
        for k in range(8):
            downs_ref[k, :run] = image[k * run : (k + 1) * run]
            downs_ref[k, run:] = text[k * run : (k + 1) * run]

    late = in_hbm(image_own, image_unit, image_length, text_unit)
    image_own, image_unit, image_length, text_unit = late
    args = (image_own, image_other, image_unit, image_length, text_pieces, text_unit, text_length)
    return kernel_call(
        body,
        "transposed_downs",
        (
            pltpu.HBM((embed, LANES), BF),
            pltpu.HBM((embed, LANES), BF),
            pltpu.HBM((8, 2 * run, LANES), BF),
        ),
        grid=(1,),
        in_specs=[whole(a.shape) for a in args],
        out_specs=[whole((embed, LANES)), whole((embed, LANES)), whole((8, 2 * run, LANES))],
        flops=10**7,
        moved_bytes=4 * 2**20,
    )(*args)


def hidden_grads(image_proj, image_turned, text_proj, text_turned):
    image_run, text_run = image_proj.shape[0] // 8, text_proj.shape[0] // 8

    def body(image_proj_ref, image_ref, text_proj_ref, text_ref, out_ref):
        for k in range(8):
            for proj, down, run, first in (
                (image_proj_ref, image_ref, image_run, 0),
                (text_proj_ref, text_ref, text_run, image_run),
            ):
                value = jnp.dot(
                    proj[k * run : (k + 1) * run], down[...], preferred_element_type=F32
                )
                out_ref[k, first : first + run] = value.astype(BF)

    shape = (8, image_run + text_run, LANES)
    args = in_hbm(image_proj, image_turned, text_proj, text_turned)
    return kernel_call(
        body,
        "hidden_grads",
        shaped(shape, BF),
        grid=(1,),
        in_specs=[whole(a.shape) for a in args],
        out_specs=whole(shape),
        flops=5 * 10**8,
        moved_bytes=4 * 2**20,
    )(*args)


def turned_back(grads, image_run):
    text_run = grads.shape[1] - image_run

    def body(grads_ref, image_ref, text_ref):
        for n in range(8):
            at = slice(n * LANES, (n + 1) * LANES)
            image_ref[at] = grads_ref[n, :image_run].astype(F32).T.astype(BF)
            text_ref[at] = grads_ref[n, image_run:].astype(F32).T.astype(BF)

    rows = 8 * LANES
    return kernel_call(
        body,
        "turned_back",
        (shaped((rows, image_run), BF), shaped((rows, text_run), BF)),
        grid=(1,),
        in_specs=[whole(grads.shape)],
        out_specs=[whole((rows, image_run)), whole((rows, text_run))],
        flops=10**6,
        moved_bytes=2**20,
    )(grads)


def weight_sums(place, hidden, text_parts, downs, scalars):
    width = downs.shape[1] // 2
    image_run, text_run = hidden.shape[1] // 16, text_parts[0].shape[0] // 4
    both = image_run + text_run

    def body(place_ref, hidden_ref, *refs):
        text_refs, (downs_ref, scalars_ref, kept_ref, sent_ref) = refs[:4], refs[4:]
        even = place_ref[6] == 0
        downs_all = jnp.concatenate([downs_ref[n] for n in range(8)], axis=1)
        for ref in (kept_ref, sent_ref):
            ref[:, :, both:] = jnp.broadcast_to(scalars_ref[:, both:][None], (8, width, LANES - both))
        for k in range(4):
            first = 2 * lax.rem(place_ref[2] + k, 4)
            image = jnp.dot(
                downs_all[:width],
                hidden_ref[:, k * 4 * image_run : (k + 1) * 4 * image_run],
                preferred_element_type=F32,
            )
            text = lax.dot_general(
                downs_all[width:],
                text_refs[k][...],
                (((1,), (1,)), ((), ())),
                preferred_element_type=F32,
            )
            for value, run, at in ((image, image_run, 0), (text, text_run, image_run)):
                for j in range(2):
                    low = value[:, 2 * j * run : (2 * j + 1) * run]
                    high = value[:, (2 * j + 1) * run : (2 * j + 2) * run]
                    kept_ref[first + j, :, at : at + run] = jnp.where(even, low, high)
                    sent_ref[first + j, :, at : at + run] = jnp.where(even, high, low)

    shape = (8, width, LANES)
    args = (*in_hbm(hidden, *text_parts), downs, scalars)
    return kernel_call(
        body,
        "weight_sums",
        (shaped(shape, F32),) * 2,
        grid=(1,),
        in_specs=[whole(a.shape) for a in args],
        out_specs=[whole(shape)] * 2,
        prefetch=1,
        flops=10**9,
        moved_bytes=6 * 2**20,
    )(place, *args)


def slabs(place, lines, other_lines, image_run, text_run):
    width = lines.shape[2]
    embed = 8 * width
    both = image_run + text_run

    def body(place_ref, lines_ref, other_ref, image_ref, text_ref, scalars_ref):
        for part, core in ((lines_ref, place_ref[6]), (other_ref, 1 - place_ref[6])):
            def at(i):
                return part[lax.rem(i + 4 - place_ref[4], 4)]

            turned = jnp.concatenate([at(i).reshape(2 * width, LANES) for i in range(4)]).T

            for side in range(2):

                @pl.when(core == side)
                def _():
                    image_ref[side * image_run : (side + 1) * image_run] = turned[:image_run]
                    text_ref[side * text_run : (side + 1) * text_run] = turned[image_run:both]
                    if side == 0:
                        scalars_ref[...] = turned[both : both + 8]

    return kernel_call(
        body,
        "slabs",
        (
            shaped((2 * image_run, embed), F32),
            shaped((2 * text_run, embed), F32),
            shaped((8, embed), F32),
        ),
        grid=(1,),
        in_specs=[whole(lines.shape)] * 2,
        out_specs=[whole((2 * image_run, embed)), whole((2 * text_run, embed)), whole((8, embed))],
        prefetch=1,
        flops=10**6,
        moved_bytes=2**21,
    )(place, lines, other_lines)


def per_device(image_hidden, text_hidden, image_proj, text_proj, log_inverse_sharpness, partner):
    y, zl, c, x, zh = (lax.axis_index(a) for a in AXES)
    branch_pos = x * 2 + zh
    data_pos = (y * 2 + zl) * 2 + c
    group_rows, image_slab = image_hidden.shape
    text_slab = text_hidden.shape[1]
    own_rows = group_rows // 8
    embed = image_proj.shape[1]
    scale = jnp.exp(log_inverse_sharpness)
    first = branch_pos * own_rows
    place = jnp.stack([(1 - c) * group_rows + first, c * group_rows + first, x, zh, y, zl, c])

    image_other, text_local = lax.optimization_barrier(
        (
            swapped(image_hidden, "zh"),
            lax.all_to_all(text_hidden, BRANCH, split_axis=0, concat_axis=1, tiled=True),
        )
    )
    image_pair = paired(image_hidden, image_other, zh)

    def from_x(send):
        return [send(0)] + [moved(send(k), ("x",), lambda i, k=k: ((i + k) % 4,)) for k in (3, 2, 1)]

    text_raw = jnp.dot(text_local, text_proj, preferred_element_type=F32)
    text_unit, text_length, text_emb = normalize(text_raw)
    near_text = lax.all_to_all(
        jnp.broadcast_to(text_emb[None], (8, own_rows, embed)), PLANE, 0, 0, tiled=True
    ).reshape(8 * own_rows, embed)
    text_own, _ = lax.optimization_barrier((text_hidden.T, text_local))
    image_parts, text_other = lax.optimization_barrier(
        (from_x(lambda k: image_pair), swapped(text_own, "zh"))
    )
    group_emb, image_turned, hidden, image_unit, image_length = project_group(
        jnp.stack([x, branch_pos]), image_parts, image_proj
    )

    text_pair = stacked(text_own, text_other, zh)
    text_parts = from_x(lambda k: text_pair)
    near_text, group_emb, text_parts[1], text_parts[3] = lax.optimization_barrier(
        (near_text, group_emb, text_parts[1], text_parts[3])
    )
    far_text = swapped(near_text, "c")
    near_logits, near_rows, near_cols = half_logits(scale, group_emb, near_text)
    far_logits, far_rows, far_cols = half_logits(scale, group_emb, far_text)

    def joined(mine, theirs):
        peak = jnp.maximum(mine[0], theirs[0])
        mass = mine[1] * jnp.exp(mine[0] - peak) + theirs[1] * jnp.exp(theirs[0] - peak)
        return jnp.stack([peak, mass])

    far_rows, far_cols, text_parts[2] = lax.optimization_barrier((far_rows, far_cols, text_parts[2]))
    row_stats = joined(near_rows.reshape(2, 8, LANES), far_rows.reshape(2, 8, LANES))
    col_stats = jnp.concatenate([near_cols, far_cols], axis=1)
    col_in = swapped(jnp.concatenate([far_cols, near_cols], axis=1), "c")
    row_stats, col_in = lax.optimization_barrier((row_stats, col_in))
    col_stats = joined(col_stats, col_in)

    def along(stats, axis):
        return [moved(stats, (axis,), lambda i, k=k: ((i + k) % 4,)) for k in (1, 3, 2)]

    def joined_four(own, others):
        return joined(joined(own, others[2]), joined(others[0], others[1]))

    row_in, col_in = along(row_stats, "x"), along(col_stats, "y")
    row_stats, col_stats = joined_four(row_stats, row_in), joined_four(col_stats, col_in)
    row_in, col_in = swapped(row_stats, "zh"), swapped(col_stats, "zl")
    row_stats, col_stats = joined(row_stats, row_in), joined(col_stats, col_in)
    row_lse = row_stats[0] + jnp.log(row_stats[1])
    col_lse = col_stats[0] + jnp.log(col_stats[1])

    row_partner = lax.dynamic_slice_in_dim(partner, data_pos * group_rows, group_rows, 0)
    row_partner = row_partner.astype(F32).reshape(8, LANES)
    near_lse, far_lse = col_lse[None, :group_rows], col_lse[None, group_rows:]
    far_low, far_part, far_terms = far_weights(
        place, scale, far_logits, row_lse, far_lse, row_partner, image_turned
    )
    text_arrived = swapped(far_part, "c")
    near_low, near_terms, *image_coded = near_weights(
        place, scale, near_logits, row_lse, near_lse, row_partner, far_low, near_text, far_text
    )
    image_ring = from_x(lambda k: image_coded[k])
    text_coded = near_text_sum(scale, near_low, image_turned, text_arrived)
    text_pieces = lax.all_to_all(text_coded, PLANE, 0, 0, tiled=True)
    image_own, image_other = pair_sums(place, image_ring)
    image_down, text_down, downs = transposed_downs(
        image_own,
        swapped(image_other, "zh"),
        image_unit,
        image_length,
        text_pieces,
        text_unit,
        text_length.reshape(1, own_rows),
    )
    downs, grads = lax.optimization_barrier(
        (
            lax.all_to_all(downs, BRANCH, 0, 0, tiled=True),
            hidden_grads(image_proj, image_down, text_proj, text_down),
        )
    )
    grads = lax.all_to_all(grads, BRANCH, 0, 0, tiled=True)
    grad_image_hidden, grad_text_hidden = turned_back(grads, image_slab)

    terms = jnp.sum(far_terms + near_terms, axis=1)
    own_row_terms = lax.dynamic_index_in_dim(row_lse, branch_pos, 0)
    own_col_terms = lax.dynamic_slice_in_dim(col_lse, (y * 2 + zl) * own_rows, own_rows, 0)
    loss_part = jnp.sum(own_row_terms) + jnp.sum(own_col_terms) - 2.0 * terms[1]
    width = embed // 8
    scalars = jnp.stack([loss_part / DENOMINATOR, terms[0]])
    image_rows, text_rows = image_slab // 2, text_slab // 2
    both = image_rows + text_rows
    scalars = jnp.pad(scalars[None], ((0, width - 1), (both, LANES - both - 2)))
    kept, sent = weight_sums(place, hidden, text_parts, downs, scalars)
    partial = kept + swapped(sent, "c")
    summed = jnp.sum(lax.all_to_all(partial, PLANE, 0, 0, tiled=True), axis=0)
    own, other = (
        moved(summed, AXES, lambda a, b, core, d, e, h=h: (d, e ^ h, core, a, b)) for h in (0, 1)
    )
    line = stacked(own[None], other[None], zl)
    lines = jnp.stack(
        [line] + [moved(line, ("y",), lambda i, k=k: ((i + k) % 4,)) for k in (3, 2, 1)]
    )
    grad_image_proj, grad_text_proj, totals = slabs(
        place, lines, swapped(lines, "c"), image_rows, text_rows
    )
    totals = jnp.sum(totals.reshape(8, 8, width)[:, :, 0], axis=1)
    return (
        totals[0].reshape(1),
        totals[1].reshape(1),
        grad_image_hidden,
        grad_text_hidden,
        grad_image_proj,
        grad_text_proj,
    )


def solution(mesh):
    torus = Mesh(mesh.devices.reshape(tuple(SIZES.values())), AXES)
    placed = (P(DP, BRANCH), P(DP, BRANCH), P(), P(), P(), P())
    return jax.shard_map(
        per_device,
        mesh=torus,
        in_specs=placed,
        out_specs=(P(), P(), P(DP, BRANCH), P(DP, BRANCH), P(BRANCH, None), P(BRANCH, None)),
        check_vma=False,
    )
```

```python
import jax
import jax.numpy as jnp
import numpy as np
from jax import lax
from jax.experimental import pallas as pl
from jax.experimental.pallas import tpu as pltpu
from jax.sharding import Mesh
from jax.sharding import PartitionSpec as P

SIZES = {"y": 4, "zl": 2, "c": 2, "x": 4, "zh": 2}
AXES = tuple(SIZES)
DP = ("y", "zl", "c")
PLANE = ("y", "zl")
BRANCH = ("x", "zh")

NORM_EPSILON = 1e-06
FULL_SCALE = 32000.0
DENOMINATOR = 32768.0
LOW = -1e30
LANES = 128
TAIL = 16
RUN = 2048
BF = jnp.bfloat16
F32 = jnp.float32


def moved(value, axes, target):
    sizes = [SIZES[a] for a in axes]
    pairs = []
    for i in range(int(np.prod(sizes))):
        at = tuple(int(v) for v in np.unravel_index(i, sizes))
        pairs.append((i, int(np.ravel_multi_index(target(*at), sizes))))
    return lax.ppermute(value, axes, pairs)


def swapped(value, axis, mask=1):
    return moved(value, (axis,), lambda i: (i ^ mask,))


def paired(own, other, side):
    return jnp.where(
        side == 0,
        jnp.concatenate([own, other], axis=1),
        jnp.concatenate([other, own], axis=1),
    )


def stacked(own, other, side):
    return jnp.where(side == 0, jnp.concatenate([own, other]), jnp.concatenate([other, own]))


def normalize(raw_rows):
    lengths = jnp.sqrt(jnp.sum(raw_rows * raw_rows, axis=1, keepdims=True) + NORM_EPSILON)
    unit_rows = raw_rows / lengths
    return (unit_rows, lengths, unit_rows.astype(BF))


def eye():
    row = lax.broadcasted_iota(jnp.int32, (LANES, LANES), 0)
    return row == lax.broadcasted_iota(jnp.int32, (LANES, LANES), 1)


def as_row(column):
    return jnp.sum(jnp.where(eye(), column, 0.0), axis=0, keepdims=True)


def as_column(row):
    return jnp.sum(jnp.where(eye(), row, 0.0), axis=1, keepdims=True)


def exponent_of(top):
    return jnp.maximum(jnp.ceil(jnp.log2(top)), -80.0)


def to_fixed(values, exponent):
    return jnp.round(values * (FULL_SCALE * jnp.exp2(-exponent))).astype(jnp.int32).astype(jnp.int16)


def from_fixed(fixed, exponent):
    return fixed.astype(jnp.int32).astype(F32) * (jnp.exp2(exponent) / FULL_SCALE)


def tail(row):
    return jnp.broadcast_to(row, (TAIL, row.shape[1])).astype(jnp.int32).astype(jnp.int16)


def code_rows(values):
    exponent = exponent_of(jnp.max(jnp.abs(values), axis=1, keepdims=True))
    return to_fixed(values, exponent), tail(as_row(exponent))


def decode_rows(fixed, exponents):
    row = exponents.astype(jnp.int32).astype(F32)[:1]
    return from_fixed(fixed, as_column(row))


def kernel_call(body, name, out_shape, grid=(), in_specs=None, out_specs=None, scratch=(), prefetch=0, flops=0, moved_bytes=0):
    spec = pltpu.PrefetchScalarGridSpec(
        num_scalar_prefetch=prefetch,
        grid=grid,
        in_specs=in_specs,
        out_specs=out_specs,
        scratch_shapes=scratch,
    )
    return pl.pallas_call(
        body,
        out_shape=out_shape,
        grid_spec=spec,
        name=name,
        compiler_params=pltpu.CompilerParams(vmem_limit_bytes=18 * 2**20),
        cost_estimate=pl.CostEstimate(flops=flops, bytes_accessed=moved_bytes, transcendentals=0),
    )


def in_hbm(*arrays):
    return [pltpu.with_memory_space_constraint(a, pltpu.HBM) for a in arrays]


def whole(shape):
    return pl.BlockSpec(shape, lambda *_: (0,) * len(shape))


def shaped(shape, dtype):
    return jax.ShapeDtypeStruct(shape, dtype)


def project_group(place, parts, proj):
    rows, width = parts[0].shape
    embed = proj.shape[1]
    step = 256

    def body(place_ref, a, b, c, d, proj_ref, emb_ref, turned_ref, hidden_ref, unit_ref, length_ref):
        i = pl.program_id(0)
        raw = None
        for k, part in enumerate((a, b, c, d)):
            first = pl.multiple_of(lax.rem(place_ref[0] + k, 4) * width, width)
            term = jnp.dot(
                part[...], proj_ref[pl.ds(first, width), :], preferred_element_type=F32
            )
            raw = term if raw is None else raw + term
            hidden_ref[:, k * width : (k + 1) * width] = part[...]
        length = jnp.sqrt(jnp.sum(raw * raw, axis=1, keepdims=True) + NORM_EPSILON)
        unit = raw / length
        emb_ref[...] = unit.astype(BF)
        turned_ref[...] = unit.T.astype(BF)
        for h in range(step // LANES):

            @pl.when(place_ref[1] == i * (step // LANES) + h)
            def _():
                unit_ref[...] = unit[h * LANES : (h + 1) * LANES]
                length_ref[...] = jnp.broadcast_to(
                    length[h * LANES : (h + 1) * LANES], (LANES, LANES)
                )

    return kernel_call(
        body,
        "project_group",
        (
            pltpu.HBM((rows, embed), BF),
            pltpu.HBM((embed, rows), BF),
            pltpu.HBM((rows, 4 * width), BF),
            pltpu.HBM((LANES, embed), F32),
            pltpu.HBM((LANES, LANES), F32),
        ),
        grid=(rows // step,),
        in_specs=[pl.BlockSpec((step, width), lambda i, *_: (i, 0))] * 4 + [whole(proj.shape)],
        out_specs=[
            pl.BlockSpec((step, embed), lambda i, *_: (i, 0)),
            pl.BlockSpec((embed, step), lambda i, *_: (0, i)),
            pl.BlockSpec((step, 4 * width), lambda i, *_: (i, 0)),
            whole((LANES, embed)),
            whole((LANES, LANES)),
        ],
        prefetch=1,
        flops=4 * 10**10,
        moved_bytes=6 * 2**20,
    )(place, *parts, proj)


def half_logits(scale, image_emb, text_emb):
    rows, embed = image_emb.shape
    columns = text_emb.shape[0]
    width, step = 512, 256

    def body(scale_ref, image_ref, text_ref, logits_ref, rows_ref, cols_ref, kept_ref, peak_ref, mass_ref):
        j = pl.program_id(0)
        kept_ref[...] = text_ref[...]

        @pl.when(j == 0)
        def _():
            peak_ref[...] = jnp.full(peak_ref.shape, LOW, F32)
            mass_ref[...] = jnp.zeros(mass_ref.shape, F32)

        col_peak = jnp.full((1, width), LOW, F32)
        col_mass = jnp.zeros((1, width), F32)
        for r in range(rows // step):
            at = slice(r * step, (r + 1) * step)
            value = scale_ref[0] * lax.dot_general(
                image_ref[at], text_ref[...], (((1,), (1,)), ((), ())), preferred_element_type=F32
            )
            logits_ref[at] = value
            tiles = [value[:, t : t + LANES] for t in range(0, width, LANES)]
            old = peak_ref[at]
            peak = old
            for tile in tiles:
                peak = jnp.maximum(peak, tile)
            mass = mass_ref[at] * jnp.exp(old - peak)
            for tile in tiles:
                mass = mass + jnp.exp(tile - peak)
            peak_ref[at] = peak
            mass_ref[at] = mass
            top = jnp.maximum(col_peak, jnp.max(value, axis=0, keepdims=True))
            col_mass = col_mass * jnp.exp(col_peak - top) + jnp.sum(
                jnp.exp(value - top), axis=0, keepdims=True
            )
            col_peak = top
        cols_ref[0:1] = col_peak
        cols_ref[1:2] = col_mass

        @pl.when(j == pl.num_programs(0) - 1)
        def _():
            for r in range(rows // LANES):
                at = slice(r * LANES, (r + 1) * LANES)
                peak = jnp.max(peak_ref[at], axis=1, keepdims=True)
                mass = jnp.sum(
                    mass_ref[at] * jnp.exp(peak_ref[at] - peak), axis=1, keepdims=True
                )
                rows_ref[r : r + 1] = as_row(peak)
                rows_ref[8 + r : 9 + r] = as_row(mass)

    return kernel_call(
        body,
        "half_logits",
        (
            shaped((rows, columns), F32),
            shaped((16, LANES), F32),
            shaped((2, columns), F32),
            pltpu.HBM((columns, embed), BF),
        ),
        grid=(columns // width,),
        in_specs=[
            pl.BlockSpec(memory_space=pltpu.SMEM),
            whole(image_emb.shape),
            pl.BlockSpec((width, embed), lambda j: (j, 0)),
        ],
        out_specs=[
            pl.BlockSpec((rows, width), lambda j: (0, j)),
            whole((16, LANES)),
            pl.BlockSpec((2, width), lambda j: (0, j)),
            pl.BlockSpec((width, embed), lambda j: (j, 0)),
        ],
        scratch=[pltpu.VMEM((rows, LANES), F32)] * 2,
        flops=2 * rows * columns * embed,
        moved_bytes=8 * 2**20,
    )(scale, image_emb, text_emb)


def weigh(logits, row_lse, col_lse, partner, first_id):
    rows, columns = logits.shape
    lane = lax.broadcasted_iota(jnp.int32, (1, LANES), 1)
    weights = []
    for t in range(columns // LANES):
        at = slice(t * LANES, (t + 1) * LANES)
        value = logits[:, at]
        matched = partner == lane + first_id(t)
        weight = jnp.exp(value - row_lse) + jnp.exp(value - col_lse[:, at])
        weight = (weight - jnp.where(matched, 2.0, 0.0)) * (1.0 / DENOMINATOR)
        scale_term = jnp.sum(weight * value, axis=0, keepdims=True)
        positive = jnp.sum(jnp.where(matched, value, 0.0), axis=0, keepdims=True)
        weights.append((weight.astype(BF), scale_term, positive))
    return weights


def columns_of(rows_ref, first, count):
    return jnp.concatenate(
        [as_column(rows_ref[first + r : first + r + 1]) for r in range(count)], axis=0
    )


def far_weights(place, scale, logits, row_lse, col_lse, partner, image_turned):
    rows, columns = logits.shape
    embed = image_turned.shape[0]
    width = 256

    def body(place_ref, scale_ref, logits_ref, row_ref, col_ref, partner_ref, turned_ref, low_ref, text_ref, terms_ref):
        j = pl.program_id(0)
        sums = [jnp.zeros((1, LANES), F32)] * 2
        for r in range(0, rows, 256):
            at = slice(r, r + 256)
            row = columns_of(row_ref, r // LANES, 2)
            part = columns_of(partner_ref, r // LANES, 2).astype(jnp.int32)
            made = weigh(
                logits_ref[at], row, col_ref[...], part, lambda t: place_ref[0] + (2 * j + t) * RUN
            )
            for t, (low, scale_term, positive) in enumerate(made):
                low_ref[at, t * LANES : (t + 1) * LANES] = low
                sums = [sums[0] + scale_term, sums[1] + positive]
        text_ref[...] = scale_ref[0] * jnp.dot(
            turned_ref[...], low_ref[...], preferred_element_type=F32
        )

        @pl.when(j == 0)
        def _():
            terms_ref[...] = jnp.zeros(terms_ref.shape, F32)

        terms_ref[0:1] += sums[0]
        terms_ref[1:2] += sums[1]

    return kernel_call(
        body,
        "far_weights",
        (
            shaped((rows, columns), BF),
            shaped((embed, columns), F32),
            shaped((8, LANES), F32),
        ),
        grid=(columns // width,),
        in_specs=[
            pl.BlockSpec(memory_space=pltpu.SMEM),
            pl.BlockSpec((rows, width), lambda j, *_: (0, j)),
            whole(row_lse.shape),
            pl.BlockSpec((1, width), lambda j, *_: (0, j)),
            whole(partner.shape),
            whole(image_turned.shape),
        ],
        out_specs=[
            pl.BlockSpec((rows, width), lambda j, *_: (0, j)),
            pl.BlockSpec((embed, width), lambda j, *_: (0, j)),
            whole((8, LANES)),
        ],
        prefetch=1,
        flops=10**8,
        moved_bytes=8 * 2**20,
    )(place, scale, logits, row_lse, col_lse, partner, image_turned)


def near_weights(place, scale, logits, row_lse, col_lse, partner, far_low, near_emb, far_emb):
    rows, columns = logits.shape
    embed = near_emb.shape[1]
    step = 256

    def body(place_ref, scale_ref, logits_ref, row_ref, col_ref, partner_ref, far_ref, near_emb_ref, far_emb_ref, *outs):
        low_ref, terms_ref, *coded_refs = outs
        k = pl.program_id(0)
        row = columns_of(row_ref, 0, 2)
        part = columns_of(partner_ref, 0, 2).astype(jnp.int32)
        made = weigh(logits_ref[...], row, col_ref[...], part, lambda t: place_ref[1] + t * RUN)
        sums = [jnp.zeros((1, LANES), F32)] * 2
        for t, (low, scale_term, positive) in enumerate(made):
            low_ref[:, t * LANES : (t + 1) * LANES] = low
            sums = [sums[0] + scale_term, sums[1] + positive]

        @pl.when(k == 0)
        def _():
            terms_ref[...] = jnp.zeros(terms_ref.shape, F32)

        terms_ref[0:1] += sums[0]
        terms_ref[1:2] += sums[1]
        image = jnp.dot(low_ref[...], near_emb_ref[...], preferred_element_type=F32)
        image = image + jnp.dot(far_ref[...], far_emb_ref[...], preferred_element_type=F32)
        image = scale_ref[0] * image
        coded = [code_rows(image[:LANES]), code_rows(image[LANES:])]
        for i in range(4):

            @pl.when(k == i)
            def _():
                for h in range(2):
                    fixed, exponents = coded[h]
                    coded_refs[i][h, :LANES] = fixed
                    coded_refs[i][h, LANES:] = jnp.zeros((TAIL, embed), jnp.int16)
                    coded_refs[i][h, LANES:, :LANES] = exponents

    def rows_at(k, place_ref):
        return lax.rem(place_ref[2] + k, 4)

    piece = (2, LANES + TAIL, embed)
    return kernel_call(
        body,
        "near_weights",
        (
            shaped((rows, columns), BF),
            shaped((8, LANES), F32),
            *[pltpu.HBM(piece, jnp.int16)] * 4,
        ),
        grid=(4,),
        in_specs=[
            pl.BlockSpec(memory_space=pltpu.SMEM),
            pl.BlockSpec((step, columns), lambda k, p: (rows_at(k, p), 0)),
            pl.BlockSpec((None, 2, LANES), lambda k, p: (rows_at(k, p), 0, 0)),
            whole(col_lse.shape),
            pl.BlockSpec((None, 2, LANES), lambda k, p: (rows_at(k, p), 0, 0)),
            pl.BlockSpec((step, columns), lambda k, p: (rows_at(k, p), 0)),
            whole(near_emb.shape),
            whole(far_emb.shape),
        ],
        out_specs=[
            pl.BlockSpec((step, columns), lambda k, p: (rows_at(k, p), 0)),
            whole((8, LANES)),
            *[whole(piece)] * 4,
        ],
        prefetch=1,
        flops=10**8,
        moved_bytes=10 * 2**20,
    )(place, scale, logits, row_lse.reshape(4, 2, LANES), col_lse, partner.reshape(4, 2, LANES), far_low, near_emb, far_emb)


def near_text_sum(scale, low, image_turned, arrived):
    embed, columns = arrived.shape
    rows = low.shape[0]
    width = 256

    def body(scale_ref, low_ref, turned_ref, arrived_ref, out_ref):
        text = scale_ref[0] * jnp.dot(turned_ref[...], low_ref[...], preferred_element_type=F32)
        text = text + arrived_ref[...]
        exponent = exponent_of(jnp.max(jnp.abs(text), axis=0, keepdims=True))
        fixed = to_fixed(text, exponent)
        last = tail(exponent)
        for h in range(width // LANES):
            at = slice(h * LANES, (h + 1) * LANES)
            out_ref[h, :embed] = fixed[:, at]
            out_ref[h, embed:] = last[:, at]

    return kernel_call(
        body,
        "near_text_sum",
        pltpu.HBM((columns // LANES, embed + TAIL, LANES), jnp.int16),
        grid=(columns // width,),
        in_specs=[
            pl.BlockSpec(memory_space=pltpu.SMEM),
            pl.BlockSpec((rows, width), lambda j: (0, j)),
            whole(image_turned.shape),
            pl.BlockSpec((embed, width), lambda j: (0, j)),
        ],
        out_specs=pl.BlockSpec((width // LANES, embed + TAIL, LANES), lambda j: (j, 0, 0)),
        flops=2 * 10**10,
        moved_bytes=8 * 2**20,
    )(scale, low, image_turned, arrived)


def pair_sum(place, pieces, own):
    embed = pieces[0].shape[-1]

    def body(place_ref, a, b, c, d, out_ref):
        h = place_ref[3] if own else 1 - place_ref[3]
        parts = [decode_rows(p[h, :LANES], p[h, LANES:, :LANES]) for p in (a, b, c, d)]
        total = (parts[0] + parts[1]) + (parts[2] + parts[3])
        if own:
            out_ref[...] = total
        else:
            fixed, exponents = code_rows(total)
            out_ref[:LANES] = fixed
            out_ref[LANES:] = jnp.zeros((TAIL, embed), jnp.int16)
            out_ref[LANES:, :LANES] = exponents

    shape, dtype = ((LANES, embed), F32) if own else ((LANES + TAIL, embed), jnp.int16)
    return kernel_call(
        body,
        "pair_sum",
        pltpu.HBM(shape, dtype),
        grid=(1,),
        in_specs=[whole(pieces[0].shape)] * 4,
        out_specs=whole(shape),
        prefetch=1,
        flops=10**7 if own else 4 * 10**10,
        moved_bytes=3 * 2**20,
    )(place, *pieces)


def downs_and_grads(image_own, image_other, image_unit, image_length, text_pieces, text_unit, text_length, image_proj, text_proj):
    embed = image_unit.shape[1]
    run = embed // 8
    image_run, text_run = image_proj.shape[0] // 8, text_proj.shape[0] // 8

    def body(own_ref, other_ref, image_unit_ref, image_length_ref, pieces_ref, text_unit_ref, text_length_ref, image_proj_ref, text_proj_ref, out_ref):
        up = own_ref[...] + decode_rows(other_ref[:LANES], other_ref[LANES:, :LANES])
        unit = image_unit_ref[...]
        radial = jnp.sum(up * unit, axis=1, keepdims=True)
        image = ((up - unit * radial) / image_length_ref[:, :1]).T.astype(BF)
        up = jnp.zeros((embed, LANES), F32)
        for n in range(8):
            row = pieces_ref[n, embed:].astype(jnp.int32).astype(F32)[:1]
            up = up + from_fixed(pieces_ref[n, :embed], row)
        unit = text_unit_ref[...].T
        radial = jnp.sum(up * unit, axis=0, keepdims=True)
        text = ((up - unit * radial) / text_length_ref[...]).astype(BF)
        image_grad = jnp.dot(image_proj_ref[...], image, preferred_element_type=F32).astype(BF)
        text_grad = jnp.dot(text_proj_ref[...], text, preferred_element_type=F32).astype(BF)
        for k in range(8):
            first = 0
            for part, size in (
                (image, run),
                (text, run),
                (image_grad, image_run),
                (text_grad, text_run),
            ):
                out_ref[k, first : first + size] = part[k * size : (k + 1) * size]
                first += size

    late = in_hbm(image_own, image_unit, image_length, text_unit, image_proj, text_proj)
    image_own, image_unit, image_length, text_unit, image_proj, text_proj = late
    args = (image_own, image_other, image_unit, image_length, text_pieces, text_unit, text_length, image_proj, text_proj)
    shape = (8, 2 * run + image_run + text_run, LANES)
    return kernel_call(
        body,
        "downs_and_grads",
        pltpu.HBM(shape, BF),
        grid=(1,),
        in_specs=[whole(a.shape) for a in args],
        out_specs=whole(shape),
        flops=5 * 10**8,
        moved_bytes=6 * 2**20,
    )(*args)


def weight_sums(place, hidden, text_parts, downs, scalars):
    image_run, text_run = hidden.shape[1] // 16, text_parts[0].shape[0] // 4
    both = image_run + text_run
    width = downs.shape[1] // 2 - both
    split = 2 * (width + image_run)

    def body(place_ref, hidden_ref, *refs):
        text_refs, (downs_ref, scalars_ref, kept_ref, sent_ref, image_ref, text_ref) = refs[:4], refs[4:]
        even = place_ref[6] == 0
        downs_all = jnp.concatenate([downs_ref[n, : 2 * width] for n in range(8)], axis=1)
        for n in range(8):
            at = slice(n * LANES, (n + 1) * LANES)
            image_ref[at] = downs_ref[n, 2 * width : split].astype(F32).T.astype(BF)
            text_ref[:, at] = downs_ref[n, split:]
        for ref in (kept_ref, sent_ref):
            ref[:, :, both:] = jnp.broadcast_to(scalars_ref[:, both:][None], (8, width, LANES - both))
        for k in range(4):
            first = 2 * lax.rem(place_ref[2] + k, 4)
            image = jnp.dot(
                downs_all[:width],
                hidden_ref[:, k * 4 * image_run : (k + 1) * 4 * image_run],
                preferred_element_type=F32,
            )
            text = lax.dot_general(
                downs_all[width : 2 * width],
                text_refs[k][...],
                (((1,), (1,)), ((), ())),
                preferred_element_type=F32,
            )
            for value, run, at in ((image, image_run, 0), (text, text_run, image_run)):
                for j in range(2):
                    low = value[:, 2 * j * run : (2 * j + 1) * run]
                    high = value[:, (2 * j + 1) * run : (2 * j + 2) * run]
                    kept_ref[first + j, :, at : at + run] = jnp.where(even, low, high)
                    sent_ref[first + j, :, at : at + run] = jnp.where(even, high, low)

    shape = (8, width, LANES)
    args = (*in_hbm(hidden, *text_parts), downs, scalars)
    return kernel_call(
        body,
        "weight_sums",
        (
            *[shaped(shape, F32)] * 2,
            pltpu.HBM((8 * LANES, 2 * image_run), BF),
            pltpu.HBM((2 * text_run, 8 * LANES), BF),
        ),
        grid=(1,),
        in_specs=[whole(a.shape) for a in args],
        out_specs=[whole(shape)] * 2
        + [whole((8 * LANES, 2 * image_run)), whole((2 * text_run, 8 * LANES))],
        prefetch=1,
        flops=10**9,
        moved_bytes=6 * 2**20,
    )(place, *args)


def slabs(place, lines, other_lines, image_run, text_run):
    width = lines.shape[2]
    embed = 8 * width
    both = image_run + text_run

    def body(place_ref, lines_ref, other_ref, image_ref, text_ref, scalars_ref):
        for part, core in ((lines_ref, place_ref[6]), (other_ref, 1 - place_ref[6])):
            def at(i):
                return part[lax.rem(i + 4 - place_ref[4], 4)]

            turned = jnp.concatenate([at(i).reshape(2 * width, LANES) for i in range(4)]).T

            for side in range(2):

                @pl.when(core == side)
                def _():
                    image_ref[side * image_run : (side + 1) * image_run] = turned[:image_run]
                    text_ref[side * text_run : (side + 1) * text_run] = turned[image_run:both]
                    if side == 0:
                        scalars_ref[...] = turned[both : both + 8]

    return kernel_call(
        body,
        "slabs",
        (
            shaped((2 * image_run, embed), F32),
            shaped((2 * text_run, embed), F32),
            shaped((8, embed), F32),
        ),
        grid=(1,),
        in_specs=[whole(lines.shape)] * 2,
        out_specs=[whole((2 * image_run, embed)), whole((2 * text_run, embed)), whole((8, embed))],
        prefetch=1,
        flops=10**6,
        moved_bytes=2**21,
    )(place, lines, other_lines)


def per_device(image_hidden, text_hidden, image_proj, text_proj, log_inverse_sharpness, partner):
    y, zl, c, x, zh = (lax.axis_index(a) for a in AXES)
    branch_pos = x * 2 + zh
    data_pos = (y * 2 + zl) * 2 + c
    group_rows, image_slab = image_hidden.shape
    text_slab = text_hidden.shape[1]
    own_rows = group_rows // 8
    embed = image_proj.shape[1]
    scale = jnp.exp(log_inverse_sharpness)
    first = branch_pos * own_rows
    place = jnp.stack([(1 - c) * group_rows + first, c * group_rows + first, x, zh, y, zl, c])

    image_other, text_local = lax.optimization_barrier(
        (
            swapped(image_hidden, "zh"),
            lax.all_to_all(text_hidden, BRANCH, split_axis=0, concat_axis=1, tiled=True),
        )
    )
    image_pair = paired(image_hidden, image_other, zh)

    def from_x(send):
        return [send(0)] + [moved(send(k), ("x",), lambda i, k=k: ((i + k) % 4,)) for k in (3, 2, 1)]

    text_raw = jnp.dot(text_local, text_proj, preferred_element_type=F32)
    text_unit, text_length, text_emb = normalize(text_raw)
    near_text = lax.all_to_all(
        jnp.broadcast_to(text_emb[None], (8, own_rows, embed)), PLANE, 0, 0, tiled=True
    ).reshape(8 * own_rows, embed)
    text_own, _ = lax.optimization_barrier((text_hidden.T, text_local))
    image_parts, text_pair = lax.optimization_barrier(
        (from_x(lambda k: image_pair), stacked(text_own, swapped(text_own, "zh"), zh))
    )
    group_emb, image_turned, hidden, image_unit, image_length = project_group(
        jnp.stack([x, branch_pos]), image_parts, image_proj
    )

    text_parts = from_x(lambda k: text_pair)
    near_text, group_emb, text_parts[1], text_parts[3] = lax.optimization_barrier(
        (near_text, group_emb, text_parts[1], text_parts[3])
    )
    far_text = swapped(near_text, "c")
    near_logits, near_rows, near_cols, near_kept = half_logits(scale, group_emb, near_text)
    far_logits, far_rows, far_cols, far_kept = half_logits(scale, group_emb, far_text)

    def joined(mine, theirs):
        peak = jnp.maximum(mine[0], theirs[0])
        mass = mine[1] * jnp.exp(mine[0] - peak) + theirs[1] * jnp.exp(theirs[0] - peak)
        return jnp.stack([peak, mass])

    far_rows, far_cols, text_parts[2] = lax.optimization_barrier((far_rows, far_cols, text_parts[2]))
    row_stats = joined(near_rows.reshape(2, 8, LANES), far_rows.reshape(2, 8, LANES))
    col_stats = jnp.concatenate([near_cols, far_cols], axis=1)
    col_in = swapped(jnp.concatenate([far_cols, near_cols], axis=1), "c")
    row_stats, col_in = lax.optimization_barrier((row_stats, col_in))
    col_stats = joined(col_stats, col_in)

    def along(stats, axis):
        return [moved(stats, (axis,), lambda i, k=k: ((i + k) % 4,)) for k in (1, 3, 2)]

    def joined_four(own, others):
        return joined(joined(own, others[2]), joined(others[0], others[1]))

    row_in, col_in = along(row_stats, "x"), along(col_stats, "y")
    row_stats, col_stats = joined_four(row_stats, row_in), joined_four(col_stats, col_in)
    row_in, col_in = swapped(row_stats, "zh"), swapped(col_stats, "zl")
    row_stats, col_stats = joined(row_stats, row_in), joined(col_stats, col_in)
    row_lse = row_stats[0] + jnp.log(row_stats[1])
    col_lse = col_stats[0] + jnp.log(col_stats[1])

    row_partner = lax.dynamic_slice_in_dim(partner, data_pos * group_rows, group_rows, 0)
    row_partner = row_partner.astype(F32).reshape(8, LANES)
    near_lse, far_lse = col_lse[None, :group_rows], col_lse[None, group_rows:]
    far_low, far_part, far_terms = far_weights(
        place, scale, far_logits, row_lse, far_lse, row_partner, image_turned
    )
    text_arrived = swapped(far_part, "c")
    near_low, near_terms, *image_coded = near_weights(
        place, scale, near_logits, row_lse, near_lse, row_partner, far_low, near_kept, far_kept
    )
    image_ring = from_x(lambda k: image_coded[k])
    text_coded = near_text_sum(scale, near_low, image_turned, text_arrived)
    text_pieces = lax.all_to_all(text_coded, PLANE, 0, 0, tiled=True)
    image_other = swapped(pair_sum(place, image_ring, False), "zh")
    image_own = pair_sum(place, image_ring, True)
    sent = downs_and_grads(
        image_own,
        image_other,
        image_unit,
        image_length,
        text_pieces,
        text_unit,
        text_length.reshape(1, own_rows),
        image_proj,
        text_proj,
    )
    downs = lax.all_to_all(sent, BRANCH, 0, 0, tiled=True)

    terms = jnp.sum(far_terms + near_terms, axis=1)
    own_row_terms = lax.dynamic_index_in_dim(row_lse, branch_pos, 0)
    own_col_terms = lax.dynamic_slice_in_dim(col_lse, (y * 2 + zl) * own_rows, own_rows, 0)
    loss_part = jnp.sum(own_row_terms) + jnp.sum(own_col_terms) - 2.0 * terms[1]
    width = embed // 8
    scalars = jnp.stack([loss_part / DENOMINATOR, terms[0]])
    image_rows, text_rows = image_slab // 2, text_slab // 2
    both = image_rows + text_rows
    scalars = jnp.pad(scalars[None], ((0, width - 1), (both, LANES - both - 2)))
    kept, sent, grad_image_hidden, text_grads = weight_sums(place, hidden, text_parts, downs, scalars)
    partial = kept + swapped(sent, "c")
    summed = jnp.sum(lax.all_to_all(partial, PLANE, 0, 0, tiled=True), axis=0)
    own, other = (
        moved(summed, AXES, lambda a, b, core, d, e, h=h: (d, e ^ h, core, a, b)) for h in (0, 1)
    )
    line = stacked(own[None], other[None], zl)
    lines = jnp.stack(
        [line] + [moved(line, ("y",), lambda i, k=k: ((i + k) % 4,)) for k in (3, 2, 1)]
    )
    grad_image_proj, grad_text_proj, totals = slabs(
        place, lines, swapped(lines, "c"), image_rows, text_rows
    )
    totals = jnp.sum(totals.reshape(8, 8, width)[:, :, 0], axis=1)
    return (
        totals[0].reshape(1),
        totals[1].reshape(1),
        grad_image_hidden,
        text_grads.T,
        grad_image_proj,
        grad_text_proj,
    )


def solution(mesh):
    torus = Mesh(mesh.devices.reshape(tuple(SIZES.values())), AXES)
    placed = (P(DP, BRANCH), P(DP, BRANCH), P(), P(), P(), P())
    return jax.shard_map(
        per_device,
        mesh=torus,
        in_specs=placed,
        out_specs=(P(), P(), P(DP, BRANCH), P(DP, BRANCH), P(BRANCH, None), P(BRANCH, None)),
        check_vma=False,
    )
```

```python
import jax
import jax.numpy as jnp
import numpy as np
from jax import lax
from jax.experimental import pallas as pl
from jax.experimental.pallas import tpu as pltpu
from jax.sharding import Mesh
from jax.sharding import PartitionSpec as P

SIZES = {"y": 4, "zl": 2, "c": 2, "x": 4, "zh": 2}
AXES = tuple(SIZES)
DP = ("y", "zl", "c")
PLANE = ("y", "zl")
BRANCH = ("x", "zh")

NORM_EPSILON = 1e-06
FULL_SCALE = 32000.0
DENOMINATOR = 32768.0
LOW = -1e30
LANES = 128
TAIL = 16
RUN = 2048
BF = jnp.bfloat16
F32 = jnp.float32


def moved(value, axes, target):
    sizes = [SIZES[a] for a in axes]
    pairs = []
    for i in range(int(np.prod(sizes))):
        at = tuple(int(v) for v in np.unravel_index(i, sizes))
        pairs.append((i, int(np.ravel_multi_index(target(*at), sizes))))
    return lax.ppermute(value, axes, pairs)


def swapped(value, axis, mask=1):
    return moved(value, (axis,), lambda i: (i ^ mask,))


def paired(own, other, side):
    return jnp.where(
        side == 0,
        jnp.concatenate([own, other], axis=1),
        jnp.concatenate([other, own], axis=1),
    )


def stacked(own, other, side):
    return jnp.where(side == 0, jnp.concatenate([own, other]), jnp.concatenate([other, own]))


def normalize(raw_rows):
    lengths = jnp.sqrt(jnp.sum(raw_rows * raw_rows, axis=1, keepdims=True) + NORM_EPSILON)
    unit_rows = raw_rows / lengths
    return (unit_rows, lengths, unit_rows.astype(BF))


def eye():
    row = lax.broadcasted_iota(jnp.int32, (LANES, LANES), 0)
    return row == lax.broadcasted_iota(jnp.int32, (LANES, LANES), 1)


def as_row(column):
    return jnp.sum(jnp.where(eye(), column, 0.0), axis=0, keepdims=True)


def as_column(row):
    return jnp.sum(jnp.where(eye(), row, 0.0), axis=1, keepdims=True)


def exponent_of(top):
    return jnp.maximum(jnp.ceil(jnp.log2(top)), -80.0)


def to_fixed(values, exponent):
    return jnp.round(values * (FULL_SCALE * jnp.exp2(-exponent))).astype(jnp.int32).astype(jnp.int16)


def from_fixed(fixed, exponent):
    return fixed.astype(jnp.int32).astype(F32) * (jnp.exp2(exponent) / FULL_SCALE)


def tail(row):
    return jnp.broadcast_to(row, (TAIL, row.shape[1])).astype(jnp.int32).astype(jnp.int16)


def code_rows(values):
    exponent = exponent_of(jnp.max(jnp.abs(values), axis=1, keepdims=True))
    return to_fixed(values, exponent), tail(as_row(exponent))


def decode_rows(fixed, exponents):
    row = exponents.astype(jnp.int32).astype(F32)[:1]
    return from_fixed(fixed, as_column(row))


def kernel_call(body, name, out_shape, grid=(), in_specs=None, out_specs=None, scratch=(), prefetch=0, flops=0, moved_bytes=0):
    spec = pltpu.PrefetchScalarGridSpec(
        num_scalar_prefetch=prefetch,
        grid=grid,
        in_specs=in_specs,
        out_specs=out_specs,
        scratch_shapes=scratch,
    )
    return pl.pallas_call(
        body,
        out_shape=out_shape,
        grid_spec=spec,
        name=name,
        compiler_params=pltpu.CompilerParams(vmem_limit_bytes=18 * 2**20),
        cost_estimate=pl.CostEstimate(flops=flops, bytes_accessed=moved_bytes, transcendentals=0),
    )


def in_hbm(*arrays):
    return [pltpu.with_memory_space_constraint(a, pltpu.HBM) for a in arrays]


def whole(shape):
    return pl.BlockSpec(shape, lambda *_: (0,) * len(shape))


def shaped(shape, dtype):
    return jax.ShapeDtypeStruct(shape, dtype)


def project_group(place, parts, proj):
    rows, width = parts[0].shape
    embed = proj.shape[1]
    step = 256

    def body(place_ref, a, b, c, d, proj_ref, emb_ref, turned_ref, hidden_ref, unit_ref, length_ref):
        i = pl.program_id(0)
        raw = None
        for k, part in enumerate((a, b, c, d)):
            first = pl.multiple_of(lax.rem(place_ref[0] + k, 4) * width, width)
            term = jnp.dot(
                part[...], proj_ref[pl.ds(first, width), :], preferred_element_type=F32
            )
            raw = term if raw is None else raw + term
            hidden_ref[:, k * width : (k + 1) * width] = part[...]
        length = jnp.sqrt(jnp.sum(raw * raw, axis=1, keepdims=True) + NORM_EPSILON)
        unit = raw / length
        emb_ref[...] = unit.astype(BF)
        turned_ref[...] = unit.T.astype(BF)
        for h in range(step // LANES):

            @pl.when(place_ref[1] == i * (step // LANES) + h)
            def _():
                unit_ref[...] = unit[h * LANES : (h + 1) * LANES]
                length_ref[...] = jnp.broadcast_to(
                    length[h * LANES : (h + 1) * LANES], (LANES, LANES)
                )

    return kernel_call(
        body,
        "project_group",
        (
            shaped((rows, embed), BF),
            shaped((embed, rows), BF),
            pltpu.HBM((rows, 4 * width), BF),
            pltpu.HBM((LANES, embed), F32),
            pltpu.HBM((LANES, LANES), F32),
        ),
        grid=(rows // step,),
        in_specs=[pl.BlockSpec((step, width), lambda i, *_: (i, 0))] * 4 + [whole(proj.shape)],
        out_specs=[
            pl.BlockSpec((step, embed), lambda i, *_: (i, 0)),
            pl.BlockSpec((embed, step), lambda i, *_: (0, i)),
            pl.BlockSpec((step, 4 * width), lambda i, *_: (i, 0)),
            whole((LANES, embed)),
            whole((LANES, LANES)),
        ],
        prefetch=1,
        flops=4 * 10**10,
        moved_bytes=6 * 2**20,
    )(place, *parts, proj)


def half_logits(scale, image_emb, text_emb):
    rows, embed = image_emb.shape
    columns = text_emb.shape[0]
    width, step = 512, 256

    def body(scale_ref, image_ref, text_ref, logits_ref, rows_ref, cols_ref, peak_ref, mass_ref):
        j = pl.program_id(0)

        @pl.when(j == 0)
        def _():
            peak_ref[...] = jnp.full(peak_ref.shape, LOW, F32)
            mass_ref[...] = jnp.zeros(mass_ref.shape, F32)

        col_peak = jnp.full((1, width), LOW, F32)
        col_mass = jnp.zeros((1, width), F32)
        for r in range(rows // step):
            at = slice(r * step, (r + 1) * step)
            value = scale_ref[0] * lax.dot_general(
                image_ref[at], text_ref[...], (((1,), (1,)), ((), ())), preferred_element_type=F32
            )
            logits_ref[at] = value
            tiles = [value[:, t : t + LANES] for t in range(0, width, LANES)]
            old = peak_ref[at]
            peak = old
            for tile in tiles:
                peak = jnp.maximum(peak, tile)
            mass = mass_ref[at] * jnp.exp(old - peak)
            for tile in tiles:
                mass = mass + jnp.exp(tile - peak)
            peak_ref[at] = peak
            mass_ref[at] = mass
            top = jnp.maximum(col_peak, jnp.max(value, axis=0, keepdims=True))
            col_mass = col_mass * jnp.exp(col_peak - top) + jnp.sum(
                jnp.exp(value - top), axis=0, keepdims=True
            )
            col_peak = top
        cols_ref[0:1] = col_peak
        cols_ref[1:2] = col_mass

        @pl.when(j == pl.num_programs(0) - 1)
        def _():
            for r in range(rows // LANES):
                at = slice(r * LANES, (r + 1) * LANES)
                peak = jnp.max(peak_ref[at], axis=1, keepdims=True)
                mass = jnp.sum(
                    mass_ref[at] * jnp.exp(peak_ref[at] - peak), axis=1, keepdims=True
                )
                rows_ref[r : r + 1] = as_row(peak)
                rows_ref[8 + r : 9 + r] = as_row(mass)

    return kernel_call(
        body,
        "half_logits",
        (shaped((rows, columns), F32), shaped((16, LANES), F32), shaped((2, columns), F32)),
        grid=(columns // width,),
        in_specs=[
            pl.BlockSpec(memory_space=pltpu.SMEM),
            whole(image_emb.shape),
            pl.BlockSpec((width, embed), lambda j: (j, 0)),
        ],
        out_specs=[
            pl.BlockSpec((rows, width), lambda j: (0, j)),
            whole((16, LANES)),
            pl.BlockSpec((2, width), lambda j: (0, j)),
        ],
        scratch=[pltpu.VMEM((rows, LANES), F32)] * 2,
        flops=2 * rows * columns * embed,
        moved_bytes=8 * 2**20,
    )(scale, image_emb, text_emb)


def weigh(logits, row_lse, col_lse, partner, first_id):
    rows, columns = logits.shape
    lane = lax.broadcasted_iota(jnp.int32, (1, LANES), 1)
    weights = []
    for t in range(columns // LANES):
        at = slice(t * LANES, (t + 1) * LANES)
        value = logits[:, at]
        matched = partner == lane + first_id(t)
        weight = jnp.exp(value - row_lse) + jnp.exp(value - col_lse[:, at])
        weight = (weight - jnp.where(matched, 2.0, 0.0)) * (1.0 / DENOMINATOR)
        scale_term = jnp.sum(weight * value, axis=0, keepdims=True)
        positive = jnp.sum(jnp.where(matched, value, 0.0), axis=0, keepdims=True)
        weights.append((weight.astype(BF), scale_term, positive))
    return weights


def columns_of(rows_ref, first, count):
    return jnp.concatenate(
        [as_column(rows_ref[first + r : first + r + 1]) for r in range(count)], axis=0
    )


def far_weights(place, scale, logits, row_lse, col_lse, partner, image_turned):
    rows, columns = logits.shape
    embed = image_turned.shape[0]
    width = 256

    def body(place_ref, scale_ref, logits_ref, row_ref, col_ref, partner_ref, turned_ref, low_ref, text_ref, terms_ref):
        j = pl.program_id(0)
        sums = [jnp.zeros((1, LANES), F32)] * 2
        for r in range(0, rows, 256):
            at = slice(r, r + 256)
            row = columns_of(row_ref, r // LANES, 2)
            part = columns_of(partner_ref, r // LANES, 2).astype(jnp.int32)
            made = weigh(
                logits_ref[at], row, col_ref[...], part, lambda t: place_ref[0] + (2 * j + t) * RUN
            )
            for t, (low, scale_term, positive) in enumerate(made):
                low_ref[at, t * LANES : (t + 1) * LANES] = low
                sums = [sums[0] + scale_term, sums[1] + positive]
        text_ref[...] = scale_ref[0] * jnp.dot(
            turned_ref[...], low_ref[...], preferred_element_type=F32
        )

        @pl.when(j == 0)
        def _():
            terms_ref[...] = jnp.zeros(terms_ref.shape, F32)

        terms_ref[0:1] += sums[0]
        terms_ref[1:2] += sums[1]

    return kernel_call(
        body,
        "far_weights",
        (
            shaped((rows, columns), BF),
            shaped((embed, columns), F32),
            shaped((8, LANES), F32),
        ),
        grid=(columns // width,),
        in_specs=[
            pl.BlockSpec(memory_space=pltpu.SMEM),
            pl.BlockSpec((rows, width), lambda j, *_: (0, j)),
            whole(row_lse.shape),
            pl.BlockSpec((1, width), lambda j, *_: (0, j)),
            whole(partner.shape),
            whole(image_turned.shape),
        ],
        out_specs=[
            pl.BlockSpec((rows, width), lambda j, *_: (0, j)),
            pl.BlockSpec((embed, width), lambda j, *_: (0, j)),
            whole((8, LANES)),
        ],
        prefetch=1,
        flops=10**8,
        moved_bytes=8 * 2**20,
    )(place, scale, logits, row_lse, col_lse, partner, image_turned)


def near_weights(place, scale, logits, row_lse, col_lse, partner, far_low, near_emb, far_emb):
    rows, columns = logits.shape
    embed = near_emb.shape[1]
    step = 256

    def body(place_ref, scale_ref, logits_ref, row_ref, col_ref, partner_ref, far_ref, near_emb_ref, far_emb_ref, *outs):
        low_ref, terms_ref, *coded_refs = outs
        k = pl.program_id(0)
        row = columns_of(row_ref, 0, 2)
        part = columns_of(partner_ref, 0, 2).astype(jnp.int32)
        made = weigh(logits_ref[...], row, col_ref[...], part, lambda t: place_ref[1] + t * RUN)
        sums = [jnp.zeros((1, LANES), F32)] * 2
        for t, (low, scale_term, positive) in enumerate(made):
            low_ref[:, t * LANES : (t + 1) * LANES] = low
            sums = [sums[0] + scale_term, sums[1] + positive]

        @pl.when(k == 0)
        def _():
            terms_ref[...] = jnp.zeros(terms_ref.shape, F32)

        terms_ref[0:1] += sums[0]
        terms_ref[1:2] += sums[1]
        image = jnp.dot(low_ref[...], near_emb_ref[...], preferred_element_type=F32)
        image = image + jnp.dot(far_ref[...], far_emb_ref[...], preferred_element_type=F32)
        image = scale_ref[0] * image
        coded = [code_rows(image[:LANES]), code_rows(image[LANES:])]
        for i in range(4):

            @pl.when(k == i)
            def _():
                for h in range(2):
                    fixed, exponents = coded[h]
                    coded_refs[i][h, :LANES] = fixed
                    coded_refs[i][h, LANES:] = jnp.zeros((TAIL, embed), jnp.int16)
                    coded_refs[i][h, LANES:, :LANES] = exponents

    def rows_at(k, place_ref):
        return lax.rem(place_ref[2] + k, 4)

    piece = (2, LANES + TAIL, embed)
    return kernel_call(
        body,
        "near_weights",
        (
            shaped((rows, columns), BF),
            shaped((8, LANES), F32),
            *[pltpu.HBM(piece, jnp.int16)] * 4,
        ),
        grid=(4,),
        in_specs=[
            pl.BlockSpec(memory_space=pltpu.SMEM),
            pl.BlockSpec((step, columns), lambda k, p: (rows_at(k, p), 0)),
            pl.BlockSpec((None, 2, LANES), lambda k, p: (rows_at(k, p), 0, 0)),
            whole(col_lse.shape),
            pl.BlockSpec((None, 2, LANES), lambda k, p: (rows_at(k, p), 0, 0)),
            pl.BlockSpec((step, columns), lambda k, p: (rows_at(k, p), 0)),
            whole(near_emb.shape),
            whole(far_emb.shape),
        ],
        out_specs=[
            pl.BlockSpec((step, columns), lambda k, p: (rows_at(k, p), 0)),
            whole((8, LANES)),
            *[whole(piece)] * 4,
        ],
        prefetch=1,
        flops=10**8,
        moved_bytes=10 * 2**20,
    )(place, scale, logits, row_lse.reshape(4, 2, LANES), col_lse, partner.reshape(4, 2, LANES), far_low, near_emb, far_emb)


def near_text_sum(scale, low, image_turned, arrived):
    embed, columns = arrived.shape
    rows = low.shape[0]
    width = 256

    def body(scale_ref, low_ref, turned_ref, arrived_ref, out_ref):
        text = scale_ref[0] * jnp.dot(turned_ref[...], low_ref[...], preferred_element_type=F32)
        text = text + arrived_ref[...]
        exponent = exponent_of(jnp.max(jnp.abs(text), axis=0, keepdims=True))
        fixed = to_fixed(text, exponent)
        last = tail(exponent)
        for h in range(width // LANES):
            at = slice(h * LANES, (h + 1) * LANES)
            out_ref[h, :embed] = fixed[:, at]
            out_ref[h, embed:] = last[:, at]

    return kernel_call(
        body,
        "near_text_sum",
        pltpu.HBM((columns // LANES, embed + TAIL, LANES), jnp.int16),
        grid=(columns // width,),
        in_specs=[
            pl.BlockSpec(memory_space=pltpu.SMEM),
            pl.BlockSpec((rows, width), lambda j: (0, j)),
            whole(image_turned.shape),
            pl.BlockSpec((embed, width), lambda j: (0, j)),
        ],
        out_specs=pl.BlockSpec((width // LANES, embed + TAIL, LANES), lambda j: (j, 0, 0)),
        flops=2 * 10**10,
        moved_bytes=8 * 2**20,
    )(scale, low, image_turned, arrived)


def pair_sums(place, pieces):
    embed = pieces[0].shape[-1]

    def body(place_ref, a, b, c, d, own_ref, other_ref):
        def total(h):
            parts = [decode_rows(p[h, :LANES], p[h, LANES:, :LANES]) for p in (a, b, c, d)]
            return (parts[0] + parts[1]) + (parts[2] + parts[3])

        own_ref[...] = total(place_ref[3])
        fixed, exponents = code_rows(total(1 - place_ref[3]))
        other_ref[:LANES] = fixed
        other_ref[LANES:] = jnp.zeros((TAIL, embed), jnp.int16)
        other_ref[LANES:, :LANES] = exponents

    return kernel_call(
        body,
        "pair_sums",
        (pltpu.HBM((LANES, embed), F32), pltpu.HBM((LANES + TAIL, embed), jnp.int16)),
        grid=(1,),
        in_specs=[whole(pieces[0].shape)] * 4,
        out_specs=[whole((LANES, embed)), whole((LANES + TAIL, embed))],
        prefetch=1,
        flops=4 * 10**10,
        moved_bytes=3 * 2**20,
    )(place, *pieces)


def transposed_downs(image_own, image_other, image_unit, image_length, text_pieces, text_unit, text_length):
    embed = image_unit.shape[1]
    run = embed // 8

    def body(own_ref, other_ref, image_unit_ref, image_length_ref, pieces_ref, text_unit_ref, text_length_ref, *outs):
        image_ref, text_ref, downs_ref = outs
        up = own_ref[...] + decode_rows(other_ref[:LANES], other_ref[LANES:, :LANES])
        unit = image_unit_ref[...]
        radial = jnp.sum(up * unit, axis=1, keepdims=True)
        image = ((up - unit * radial) / image_length_ref[:, :1]).T.astype(BF)
        up = jnp.zeros((embed, LANES), F32)
        for n in range(8):
            row = pieces_ref[n, embed:].astype(jnp.int32).astype(F32)[:1]
            up = up + from_fixed(pieces_ref[n, :embed], row)
        unit = text_unit_ref[...].T
        radial = jnp.sum(up * unit, axis=0, keepdims=True)
        text = ((up - unit * radial) / text_length_ref[...]).astype(BF)
        image_ref[...] = image
        text_ref[...] = text
        for k in range(8):
            downs_ref[k, :run] = image[k * run : (k + 1) * run]
            downs_ref[k, run:] = text[k * run : (k + 1) * run]

    late = in_hbm(image_own, image_unit, image_length, text_unit)
    image_own, image_unit, image_length, text_unit = late
    args = (image_own, image_other, image_unit, image_length, text_pieces, text_unit, text_length)
    return kernel_call(
        body,
        "transposed_downs",
        (
            pltpu.HBM((embed, LANES), BF),
            pltpu.HBM((embed, LANES), BF),
            pltpu.HBM((8, 2 * run, LANES), BF),
        ),
        grid=(1,),
        in_specs=[whole(a.shape) for a in args],
        out_specs=[whole((embed, LANES)), whole((embed, LANES)), whole((8, 2 * run, LANES))],
        flops=10**7,
        moved_bytes=4 * 2**20,
    )(*args)


def hidden_grads(image_proj, image_turned, text_proj, text_turned):
    image_run, text_run = image_proj.shape[0] // 8, text_proj.shape[0] // 8

    def body(image_proj_ref, image_ref, text_proj_ref, text_ref, out_ref):
        for k in range(8):
            for proj, down, run, first in (
                (image_proj_ref, image_ref, image_run, 0),
                (text_proj_ref, text_ref, text_run, image_run),
            ):
                value = jnp.dot(
                    proj[k * run : (k + 1) * run], down[...], preferred_element_type=F32
                )
                out_ref[k, first : first + run] = value.astype(BF)

    shape = (8, image_run + text_run, LANES)
    args = in_hbm(image_proj, image_turned, text_proj, text_turned)
    return kernel_call(
        body,
        "hidden_grads",
        shaped(shape, BF),
        grid=(1,),
        in_specs=[whole(a.shape) for a in args],
        out_specs=whole(shape),
        flops=5 * 10**8,
        moved_bytes=4 * 2**20,
    )(*args)


def turned_back(grads, image_run):
    text_run = grads.shape[1] - image_run

    def body(grads_ref, image_ref, text_ref):
        for n in range(8):
            at = slice(n * LANES, (n + 1) * LANES)
            image_ref[at] = grads_ref[n, :image_run].astype(F32).T.astype(BF)
            text_ref[at] = grads_ref[n, image_run:].astype(F32).T.astype(BF)

    rows = 8 * LANES
    return kernel_call(
        body,
        "turned_back",
        (shaped((rows, image_run), BF), shaped((rows, text_run), BF)),
        grid=(1,),
        in_specs=[whole(grads.shape)],
        out_specs=[whole((rows, image_run)), whole((rows, text_run))],
        flops=10**6,
        moved_bytes=2**20,
    )(grads)


def weight_sums(place, hidden, text_parts, downs, scalars):
    width = downs.shape[1] // 2
    image_run, text_run = hidden.shape[1] // 16, text_parts[0].shape[0] // 4
    both = image_run + text_run

    def body(place_ref, hidden_ref, *refs):
        text_refs, (downs_ref, scalars_ref, kept_ref, sent_ref) = refs[:4], refs[4:]
        even = place_ref[6] == 0
        downs_all = jnp.concatenate([downs_ref[n] for n in range(8)], axis=1)
        for ref in (kept_ref, sent_ref):
            ref[:, :, both:] = jnp.broadcast_to(scalars_ref[:, both:][None], (8, width, LANES - both))
        for k in range(4):
            first = 2 * k
            image = jnp.dot(
                downs_all[:width],
                hidden_ref[:, k * 4 * image_run : (k + 1) * 4 * image_run],
                preferred_element_type=F32,
            )
            text = lax.dot_general(
                downs_all[width:],
                text_refs[k][...],
                (((1,), (1,)), ((), ())),
                preferred_element_type=F32,
            )
            for value, run, at in ((image, image_run, 0), (text, text_run, image_run)):
                for j in range(2):
                    low = value[:, 2 * j * run : (2 * j + 1) * run]
                    high = value[:, (2 * j + 1) * run : (2 * j + 2) * run]
                    slab = first + jnp.bitwise_xor(place_ref[3], j)
                    kept_ref[slab, :, at : at + run] = jnp.where(even, low, high)
                    sent_ref[slab, :, at : at + run] = jnp.where(even, high, low)

    shape = (8, width, LANES)
    args = (*in_hbm(hidden, *text_parts), downs, scalars)
    return kernel_call(
        body,
        "weight_sums",
        (shaped(shape, F32),) * 2,
        grid=(1,),
        in_specs=[whole(a.shape) for a in args],
        out_specs=[whole(shape)] * 2,
        prefetch=1,
        flops=10**9,
        moved_bytes=6 * 2**20,
    )(place, *args)


def slabs(place, lines, other_lines, image_run, text_run):
    width = lines.shape[2]
    embed = 8 * width
    both = image_run + text_run

    def body(place_ref, lines_ref, other_ref, image_ref, text_ref, scalars_ref):
        for part, core in ((lines_ref, place_ref[6]), (other_ref, 1 - place_ref[6])):
            def at(i):
                return part[lax.rem(place_ref[2] + 8 - place_ref[4] - i, 4)]

            turned = jnp.concatenate([at(i).reshape(2 * width, LANES) for i in range(4)]).T

            for side in range(2):

                @pl.when(core == side)
                def _():
                    image_ref[side * image_run : (side + 1) * image_run] = turned[:image_run]
                    text_ref[side * text_run : (side + 1) * text_run] = turned[image_run:both]
                    if side == 0:
                        scalars_ref[...] = turned[both : both + 8]

    return kernel_call(
        body,
        "slabs",
        (
            shaped((2 * image_run, embed), F32),
            shaped((2 * text_run, embed), F32),
            shaped((8, embed), F32),
        ),
        grid=(1,),
        in_specs=[whole(lines.shape)] * 2,
        out_specs=[whole((2 * image_run, embed)), whole((2 * text_run, embed)), whole((8, embed))],
        prefetch=1,
        flops=10**6,
        moved_bytes=2**21,
    )(place, lines, other_lines)


def per_device(image_hidden, text_hidden, image_proj, text_proj, log_inverse_sharpness, partner):
    y, zl, c, x, zh = (lax.axis_index(a) for a in AXES)
    branch_pos = x * 2 + zh
    data_pos = (y * 2 + zl) * 2 + c
    group_rows, image_slab = image_hidden.shape
    text_slab = text_hidden.shape[1]
    own_rows = group_rows // 8
    embed = image_proj.shape[1]
    scale = jnp.exp(log_inverse_sharpness)
    first = branch_pos * own_rows
    place = jnp.stack([(1 - c) * group_rows + first, c * group_rows + first, x, zh, y, zl, c])

    image_other, text_local = lax.optimization_barrier(
        (
            swapped(image_hidden, "zh"),
            lax.all_to_all(text_hidden, BRANCH, split_axis=0, concat_axis=1, tiled=True),
        )
    )
    image_pair = paired(image_hidden, image_other, zh)

    def from_x(send):
        return [send(0)] + [moved(send(k), ("x",), lambda i, k=k: ((i + k) % 4,)) for k in (3, 2, 1)]

    text_raw = jnp.dot(text_local, text_proj, preferred_element_type=F32)
    text_unit, text_length, text_emb = normalize(text_raw)
    near_text = lax.all_to_all(
        jnp.broadcast_to(text_emb[None], (8, own_rows, embed)), PLANE, 0, 0, tiled=True
    ).reshape(8 * own_rows, embed)
    text_own, _ = lax.optimization_barrier((text_hidden.T, text_local))
    image_parts, text_pair = lax.optimization_barrier(
        (from_x(lambda k: image_pair), stacked(text_own, swapped(text_own, "zh"), zh))
    )
    group_emb, image_turned, hidden, image_unit, image_length = project_group(
        jnp.stack([x, branch_pos]), image_parts, image_proj
    )

    text_parts = from_x(lambda k: text_pair)
    near_text, group_emb, text_parts[1], text_parts[3] = lax.optimization_barrier(
        (near_text, group_emb, text_parts[1], text_parts[3])
    )
    far_text = swapped(near_text, "c")
    near_logits, near_rows, near_cols = half_logits(scale, group_emb, near_text)
    far_logits, far_rows, far_cols = half_logits(scale, group_emb, far_text)

    def joined(mine, theirs):
        peak = jnp.maximum(mine[0], theirs[0])
        mass = mine[1] * jnp.exp(mine[0] - peak) + theirs[1] * jnp.exp(theirs[0] - peak)
        return jnp.stack([peak, mass])

    far_rows, far_cols, text_parts[2] = lax.optimization_barrier((far_rows, far_cols, text_parts[2]))
    row_stats = joined(near_rows.reshape(2, 8, LANES), far_rows.reshape(2, 8, LANES))
    col_stats = jnp.concatenate([near_cols, far_cols], axis=1)
    col_in = swapped(jnp.concatenate([far_cols, near_cols], axis=1), "c")
    row_stats, col_in = lax.optimization_barrier((row_stats, col_in))
    col_stats = joined(col_stats, col_in)

    def along(stats, axis):
        return [moved(stats, (axis,), lambda i, k=k: ((i + k) % 4,)) for k in (1, 3, 2)]

    def joined_four(own, others):
        return joined(joined(own, others[2]), joined(others[0], others[1]))

    row_in, col_in = along(row_stats, "x"), along(col_stats, "y")
    row_stats, col_stats = joined_four(row_stats, row_in), joined_four(col_stats, col_in)
    row_in, col_in = swapped(row_stats, "zh"), swapped(col_stats, "zl")
    row_stats, col_stats = joined(row_stats, row_in), joined(col_stats, col_in)
    row_lse = row_stats[0] + jnp.log(row_stats[1])
    col_lse = col_stats[0] + jnp.log(col_stats[1])

    row_partner = lax.dynamic_slice_in_dim(partner, data_pos * group_rows, group_rows, 0)
    row_partner = row_partner.astype(F32).reshape(8, LANES)
    near_lse, far_lse = col_lse[None, :group_rows], col_lse[None, group_rows:]
    far_low, far_part, far_terms = far_weights(
        place, scale, far_logits, row_lse, far_lse, row_partner, image_turned
    )
    text_arrived = swapped(far_part, "c")
    near_low, near_terms, *image_coded = near_weights(
        place, scale, near_logits, row_lse, near_lse, row_partner, far_low, near_text, far_text
    )
    image_ring = from_x(lambda k: image_coded[k])
    text_coded = near_text_sum(scale, near_low, image_turned, text_arrived)
    text_pieces = lax.all_to_all(text_coded, PLANE, 0, 0, tiled=True)
    image_own, image_other = pair_sums(place, image_ring)
    image_down, text_down, downs = transposed_downs(
        image_own,
        swapped(image_other, "zh"),
        image_unit,
        image_length,
        text_pieces,
        text_unit,
        text_length.reshape(1, own_rows),
    )
    downs, grads = lax.optimization_barrier(
        (
            lax.all_to_all(downs, BRANCH, 0, 0, tiled=True),
            hidden_grads(image_proj, image_down, text_proj, text_down),
        )
    )
    grads = lax.all_to_all(grads, BRANCH, 0, 0, tiled=True)
    grad_image_hidden, grad_text_hidden = turned_back(grads, image_slab)

    terms = jnp.sum(far_terms + near_terms, axis=1)
    own_row_terms = lax.dynamic_index_in_dim(row_lse, branch_pos, 0)
    own_col_terms = lax.dynamic_slice_in_dim(col_lse, (y * 2 + zl) * own_rows, own_rows, 0)
    loss_part = jnp.sum(own_row_terms) + jnp.sum(own_col_terms) - 2.0 * terms[1]
    width = embed // 8
    scalars = jnp.stack([loss_part / DENOMINATOR, terms[0]])
    image_rows, text_rows = image_slab // 2, text_slab // 2
    both = image_rows + text_rows
    scalars = jnp.pad(scalars[None], ((0, width - 1), (both, LANES - both - 2)))
    kept, sent = weight_sums(place, hidden, text_parts, downs, scalars)
    partial = kept + swapped(sent, "c")
    summed = jnp.sum(lax.all_to_all(partial, PLANE, 0, 0, tiled=True), axis=0)
    own, other = (
        moved(summed, AXES, lambda a, b, core, d, e, h=h: (a, b ^ h, core, (d + a) % 4, e ^ b))
        for h in (0, 1)
    )
    line = stacked(own[None], other[None], jnp.bitwise_xor(zl, zh))
    lines = jnp.stack(
        [line] + [moved(line, ("y",), lambda i, k=k: ((i + k) % 4,)) for k in (3, 2, 1)]
    )
    grad_image_proj, grad_text_proj, totals = slabs(
        place, lines, swapped(lines, "c"), image_rows, text_rows
    )
    totals = jnp.sum(totals.reshape(8, 8, width)[:, :, 0], axis=1)
    return (
        totals[0].reshape(1),
        totals[1].reshape(1),
        grad_image_hidden,
        grad_text_hidden,
        grad_image_proj,
        grad_text_proj,
    )


def solution(mesh):
    torus = Mesh(mesh.devices.reshape(tuple(SIZES.values())), AXES)
    placed = (P(DP, BRANCH), P(DP, BRANCH), P(), P(), P(), P())
    return jax.shard_map(
        per_device,
        mesh=torus,
        in_specs=placed,
        out_specs=(P(), P(), P(DP, BRANCH), P(DP, BRANCH), P(BRANCH, None), P(BRANCH, None)),
        check_vma=False,
    )
```

```python
import jax
import jax.numpy as jnp
import numpy as np
from jax import lax
from jax.experimental import pallas as pl
from jax.experimental.pallas import tpu as pltpu
from jax.sharding import Mesh
from jax.sharding import PartitionSpec as P

SIZES = {"y": 4, "zl": 2, "c": 2, "x": 4, "zh": 2}
AXES = tuple(SIZES)
DP = ("y", "zl", "c")
PLANE = ("y", "zl")
BRANCH = ("x", "zh")

NORM_EPSILON = 1e-06
FULL_SCALE = 32000.0
DENOMINATOR = 32768.0
LOW = -1e30
LANES = 128
TAIL = 16
RUN = 2048
BF = jnp.bfloat16
F32 = jnp.float32


def moved(value, axes, target):
    sizes = [SIZES[a] for a in axes]
    pairs = []
    for i in range(int(np.prod(sizes))):
        at = tuple(int(v) for v in np.unravel_index(i, sizes))
        pairs.append((i, int(np.ravel_multi_index(target(*at), sizes))))
    return lax.ppermute(value, axes, pairs)


def swapped(value, axis, mask=1):
    return moved(value, (axis,), lambda i: (i ^ mask,))


def stacked(own, other, side):
    return jnp.where(side == 0, jnp.concatenate([own, other]), jnp.concatenate([other, own]))


def normalize(raw_rows):
    lengths = jnp.sqrt(jnp.sum(raw_rows * raw_rows, axis=1, keepdims=True) + NORM_EPSILON)
    unit_rows = raw_rows / lengths
    return (unit_rows, lengths, unit_rows.astype(BF))


def eye():
    row = lax.broadcasted_iota(jnp.int32, (LANES, LANES), 0)
    return row == lax.broadcasted_iota(jnp.int32, (LANES, LANES), 1)


def as_row(column):
    return jnp.sum(jnp.where(eye(), column, 0.0), axis=0, keepdims=True)


def as_column(row):
    return jnp.sum(jnp.where(eye(), row, 0.0), axis=1, keepdims=True)


def exponent_of(top):
    return jnp.maximum(jnp.ceil(jnp.log2(top)), -80.0)


def to_fixed(values, exponent):
    return jnp.round(values * (FULL_SCALE * jnp.exp2(-exponent))).astype(jnp.int32).astype(jnp.int16)


def from_fixed(fixed, exponent):
    return fixed.astype(jnp.int32).astype(F32) * (jnp.exp2(exponent) / FULL_SCALE)


def tail(row):
    return jnp.broadcast_to(row, (TAIL, row.shape[1])).astype(jnp.int32).astype(jnp.int16)


def code_rows(values):
    exponent = exponent_of(jnp.max(jnp.abs(values), axis=1, keepdims=True))
    return to_fixed(values, exponent), tail(as_row(exponent))


def decode_rows(fixed, exponents):
    row = exponents.astype(jnp.int32).astype(F32)[:1]
    return from_fixed(fixed, as_column(row))


def kernel_call(body, name, out_shape, grid=(), in_specs=None, out_specs=None, scratch=(), prefetch=0, flops=0, moved_bytes=0):
    spec = pltpu.PrefetchScalarGridSpec(
        num_scalar_prefetch=prefetch,
        grid=grid,
        in_specs=in_specs,
        out_specs=out_specs,
        scratch_shapes=scratch,
    )
    return pl.pallas_call(
        body,
        out_shape=out_shape,
        grid_spec=spec,
        name=name,
        compiler_params=pltpu.CompilerParams(vmem_limit_bytes=18 * 2**20),
        cost_estimate=pl.CostEstimate(flops=flops, bytes_accessed=moved_bytes, transcendentals=0),
    )


def in_hbm(*arrays):
    return [pltpu.with_memory_space_constraint(a, pltpu.HBM) for a in arrays]


def whole(shape):
    return pl.BlockSpec(shape, lambda *_: (0,) * len(shape))


def shaped(shape, dtype):
    return jax.ShapeDtypeStruct(shape, dtype)


def project_group(place, parts, proj):
    rows, width = parts[0].shape
    embed = proj.shape[1]
    step = 256

    def body(place_ref, a, b, c, d, proj_ref, emb_ref, turned_ref, hidden_ref, unit_ref, length_ref):
        i = pl.program_id(0)
        raw = None
        for k, part in enumerate((a, b, c, d)):
            slab = 2 * lax.rem(place_ref[0] + k, 4)
            rows_of = [
                proj_ref[pl.ds(pl.multiple_of((slab + z) * (width // 2), width // 2), width // 2), :]
                for z in (place_ref[2], 1 - place_ref[2])
            ]
            term = jnp.dot(
                part[...], jnp.concatenate(rows_of, axis=0), preferred_element_type=F32
            )
            raw = term if raw is None else raw + term
            hidden_ref[:, k * width : (k + 1) * width] = part[...]
        length = jnp.sqrt(jnp.sum(raw * raw, axis=1, keepdims=True) + NORM_EPSILON)
        unit = raw / length
        emb_ref[...] = unit.astype(BF)
        turned_ref[...] = unit.T.astype(BF)
        for h in range(step // LANES):

            @pl.when(place_ref[1] == i * (step // LANES) + h)
            def _():
                unit_ref[...] = unit[h * LANES : (h + 1) * LANES]
                length_ref[...] = jnp.broadcast_to(
                    length[h * LANES : (h + 1) * LANES], (LANES, LANES)
                )

    return kernel_call(
        body,
        "project_group",
        (
            shaped((rows, embed), BF),
            shaped((embed, rows), BF),
            pltpu.HBM((rows, 4 * width), BF),
            pltpu.HBM((LANES, embed), F32),
            pltpu.HBM((LANES, LANES), F32),
        ),
        grid=(rows // step,),
        in_specs=[pl.BlockSpec((step, width), lambda i, *_: (i, 0))] * 4 + [whole(proj.shape)],
        out_specs=[
            pl.BlockSpec((step, embed), lambda i, *_: (i, 0)),
            pl.BlockSpec((embed, step), lambda i, *_: (0, i)),
            pl.BlockSpec((step, 4 * width), lambda i, *_: (i, 0)),
            whole((LANES, embed)),
            whole((LANES, LANES)),
        ],
        prefetch=1,
        flops=4 * 10**10,
        moved_bytes=6 * 2**20,
    )(place, *parts, proj)


def half_logits(scale, image_emb, text_emb):
    rows, embed = image_emb.shape
    columns = text_emb.shape[0]
    width, step = 512, 256

    def body(scale_ref, image_ref, text_ref, logits_ref, rows_ref, cols_ref, peak_ref, mass_ref):
        j = pl.program_id(0)

        @pl.when(j == 0)
        def _():
            peak_ref[...] = jnp.full(peak_ref.shape, LOW, F32)
            mass_ref[...] = jnp.zeros(mass_ref.shape, F32)

        col_peak = jnp.full((1, width), LOW, F32)
        col_mass = jnp.zeros((1, width), F32)
        for r in range(rows // step):
            at = slice(r * step, (r + 1) * step)
            value = scale_ref[0] * lax.dot_general(
                image_ref[at], text_ref[...], (((1,), (1,)), ((), ())), preferred_element_type=F32
            )
            logits_ref[at] = value
            tiles = [value[:, t : t + LANES] for t in range(0, width, LANES)]
            old = peak_ref[at]
            peak = old
            for tile in tiles:
                peak = jnp.maximum(peak, tile)
            mass = mass_ref[at] * jnp.exp(old - peak)
            for tile in tiles:
                mass = mass + jnp.exp(tile - peak)
            peak_ref[at] = peak
            mass_ref[at] = mass
            top = jnp.maximum(col_peak, jnp.max(value, axis=0, keepdims=True))
            col_mass = col_mass * jnp.exp(col_peak - top) + jnp.sum(
                jnp.exp(value - top), axis=0, keepdims=True
            )
            col_peak = top
        cols_ref[0:1] = col_peak
        cols_ref[1:2] = col_mass

        @pl.when(j == pl.num_programs(0) - 1)
        def _():
            for r in range(rows // LANES):
                at = slice(r * LANES, (r + 1) * LANES)
                peak = jnp.max(peak_ref[at], axis=1, keepdims=True)
                mass = jnp.sum(
                    mass_ref[at] * jnp.exp(peak_ref[at] - peak), axis=1, keepdims=True
                )
                rows_ref[r : r + 1] = as_row(peak)
                rows_ref[8 + r : 9 + r] = as_row(mass)

    return kernel_call(
        body,
        "half_logits",
        (shaped((rows, columns), F32), shaped((16, LANES), F32), shaped((2, columns), F32)),
        grid=(columns // width,),
        in_specs=[
            pl.BlockSpec(memory_space=pltpu.SMEM),
            whole(image_emb.shape),
            pl.BlockSpec((width, embed), lambda j: (j, 0)),
        ],
        out_specs=[
            pl.BlockSpec((rows, width), lambda j: (0, j)),
            whole((16, LANES)),
            pl.BlockSpec((2, width), lambda j: (0, j)),
        ],
        scratch=[pltpu.VMEM((rows, LANES), F32)] * 2,
        flops=2 * rows * columns * embed,
        moved_bytes=8 * 2**20,
    )(scale, image_emb, text_emb)


def weigh(logits, row_lse, col_lse, partner, first_id):
    rows, columns = logits.shape
    lane = lax.broadcasted_iota(jnp.int32, (1, LANES), 1)
    weights = []
    for t in range(columns // LANES):
        at = slice(t * LANES, (t + 1) * LANES)
        value = logits[:, at]
        matched = partner == lane + first_id(t)
        weight = jnp.exp(value - row_lse) + jnp.exp(value - col_lse[:, at])
        weight = (weight - jnp.where(matched, 2.0, 0.0)) * (1.0 / DENOMINATOR)
        scale_term = jnp.sum(weight * value, axis=0, keepdims=True)
        positive = jnp.sum(jnp.where(matched, value, 0.0), axis=0, keepdims=True)
        weights.append((weight.astype(BF), scale_term, positive))
    return weights


def columns_of(rows_ref, first, count):
    return jnp.concatenate(
        [as_column(rows_ref[first + r : first + r + 1]) for r in range(count)], axis=0
    )


def far_weights(place, scale, logits, row_lse, col_lse, partner, image_turned):
    rows, columns = logits.shape
    embed = image_turned.shape[0]
    width = 256

    def body(place_ref, scale_ref, logits_ref, row_ref, col_ref, partner_ref, turned_ref, low_ref, text_ref, terms_ref):
        j = pl.program_id(0)
        sums = [jnp.zeros((1, LANES), F32)] * 2
        for r in range(0, rows, 256):
            at = slice(r, r + 256)
            row = columns_of(row_ref, r // LANES, 2)
            part = columns_of(partner_ref, r // LANES, 2).astype(jnp.int32)
            made = weigh(
                logits_ref[at], row, col_ref[...], part, lambda t: place_ref[0] + (2 * j + t) * RUN
            )
            for t, (low, scale_term, positive) in enumerate(made):
                low_ref[at, t * LANES : (t + 1) * LANES] = low
                sums = [sums[0] + scale_term, sums[1] + positive]
        text_ref[...] = scale_ref[0] * jnp.dot(
            turned_ref[...], low_ref[...], preferred_element_type=F32
        )

        @pl.when(j == 0)
        def _():
            terms_ref[...] = jnp.zeros(terms_ref.shape, F32)

        terms_ref[0:1] += sums[0]
        terms_ref[1:2] += sums[1]

    return kernel_call(
        body,
        "far_weights",
        (
            shaped((rows, columns), BF),
            shaped((embed, columns), F32),
            shaped((8, LANES), F32),
        ),
        grid=(columns // width,),
        in_specs=[
            pl.BlockSpec(memory_space=pltpu.SMEM),
            pl.BlockSpec((rows, width), lambda j, *_: (0, j)),
            whole(row_lse.shape),
            pl.BlockSpec((1, width), lambda j, *_: (0, j)),
            whole(partner.shape),
            whole(image_turned.shape),
        ],
        out_specs=[
            pl.BlockSpec((rows, width), lambda j, *_: (0, j)),
            pl.BlockSpec((embed, width), lambda j, *_: (0, j)),
            whole((8, LANES)),
        ],
        prefetch=1,
        flops=10**8,
        moved_bytes=8 * 2**20,
    )(place, scale, logits, row_lse, col_lse, partner, image_turned)


def near_weights(place, scale, logits, row_lse, col_lse, partner, far_low, near_emb, far_emb):
    rows, columns = logits.shape
    embed = near_emb.shape[1]
    step = 256

    def body(place_ref, scale_ref, logits_ref, row_ref, col_ref, partner_ref, far_ref, near_emb_ref, far_emb_ref, *outs):
        low_ref, terms_ref, *coded_refs = outs
        k = pl.program_id(0)
        row = columns_of(row_ref, 0, 2)
        part = columns_of(partner_ref, 0, 2).astype(jnp.int32)
        made = weigh(logits_ref[...], row, col_ref[...], part, lambda t: place_ref[1] + t * RUN)
        sums = [jnp.zeros((1, LANES), F32)] * 2
        for t, (low, scale_term, positive) in enumerate(made):
            low_ref[:, t * LANES : (t + 1) * LANES] = low
            sums = [sums[0] + scale_term, sums[1] + positive]

        @pl.when(k == 0)
        def _():
            terms_ref[...] = jnp.zeros(terms_ref.shape, F32)

        terms_ref[0:1] += sums[0]
        terms_ref[1:2] += sums[1]
        image = jnp.dot(low_ref[...], near_emb_ref[...], preferred_element_type=F32)
        image = image + jnp.dot(far_ref[...], far_emb_ref[...], preferred_element_type=F32)
        image = scale_ref[0] * image
        coded = [code_rows(image[:LANES]), code_rows(image[LANES:])]
        for i in range(4):

            @pl.when(k == i)
            def _():
                for h in range(2):
                    fixed, exponents = coded[h]
                    coded_refs[i][h, :LANES] = fixed
                    coded_refs[i][h, LANES:] = jnp.zeros((TAIL, embed), jnp.int16)
                    coded_refs[i][h, LANES:, :LANES] = exponents

    def rows_at(k, place_ref):
        return lax.rem(place_ref[2] + k, 4)

    piece = (2, LANES + TAIL, embed)
    return kernel_call(
        body,
        "near_weights",
        (
            shaped((rows, columns), BF),
            shaped((8, LANES), F32),
            *[pltpu.HBM(piece, jnp.int16)] * 4,
        ),
        grid=(4,),
        in_specs=[
            pl.BlockSpec(memory_space=pltpu.SMEM),
            pl.BlockSpec((step, columns), lambda k, p: (rows_at(k, p), 0)),
            pl.BlockSpec((None, 2, LANES), lambda k, p: (rows_at(k, p), 0, 0)),
            whole(col_lse.shape),
            pl.BlockSpec((None, 2, LANES), lambda k, p: (rows_at(k, p), 0, 0)),
            pl.BlockSpec((step, columns), lambda k, p: (rows_at(k, p), 0)),
            whole(near_emb.shape),
            whole(far_emb.shape),
        ],
        out_specs=[
            pl.BlockSpec((step, columns), lambda k, p: (rows_at(k, p), 0)),
            whole((8, LANES)),
            *[whole(piece)] * 4,
        ],
        prefetch=1,
        flops=10**8,
        moved_bytes=10 * 2**20,
    )(place, scale, logits, row_lse.reshape(4, 2, LANES), col_lse, partner.reshape(4, 2, LANES), far_low, near_emb, far_emb)


def near_text_sum(scale, low, image_turned, arrived):
    embed, columns = arrived.shape
    rows = low.shape[0]
    width = 256

    def body(scale_ref, low_ref, turned_ref, arrived_ref, out_ref):
        text = scale_ref[0] * jnp.dot(turned_ref[...], low_ref[...], preferred_element_type=F32)
        text = text + arrived_ref[...]
        exponent = exponent_of(jnp.max(jnp.abs(text), axis=0, keepdims=True))
        fixed = to_fixed(text, exponent)
        last = tail(exponent)
        for h in range(width // LANES):
            at = slice(h * LANES, (h + 1) * LANES)
            out_ref[h, :embed] = fixed[:, at]
            out_ref[h, embed:] = last[:, at]

    return kernel_call(
        body,
        "near_text_sum",
        pltpu.HBM((columns // LANES, embed + TAIL, LANES), jnp.int16),
        grid=(columns // width,),
        in_specs=[
            pl.BlockSpec(memory_space=pltpu.SMEM),
            pl.BlockSpec((rows, width), lambda j: (0, j)),
            whole(image_turned.shape),
            pl.BlockSpec((embed, width), lambda j: (0, j)),
        ],
        out_specs=pl.BlockSpec((width // LANES, embed + TAIL, LANES), lambda j: (j, 0, 0)),
        flops=2 * 10**10,
        moved_bytes=8 * 2**20,
    )(scale, low, image_turned, arrived)


def pair_sums(place, pieces):
    embed = pieces[0].shape[-1]

    def body(place_ref, a, b, c, d, own_ref, other_ref):
        def total(h):
            parts = [decode_rows(p[h, :LANES], p[h, LANES:, :LANES]) for p in (a, b, c, d)]
            return (parts[0] + parts[1]) + (parts[2] + parts[3])

        own_ref[...] = total(place_ref[3])
        fixed, exponents = code_rows(total(1 - place_ref[3]))
        other_ref[:LANES] = fixed
        other_ref[LANES:] = jnp.zeros((TAIL, embed), jnp.int16)
        other_ref[LANES:, :LANES] = exponents

    return kernel_call(
        body,
        "pair_sums",
        (pltpu.HBM((LANES, embed), F32), pltpu.HBM((LANES + TAIL, embed), jnp.int16)),
        grid=(1,),
        in_specs=[whole(pieces[0].shape)] * 4,
        out_specs=[whole((LANES, embed)), whole((LANES + TAIL, embed))],
        prefetch=1,
        flops=4 * 10**10,
        moved_bytes=3 * 2**20,
    )(place, *pieces)


def transposed_downs(image_own, image_other, image_unit, image_length, text_pieces, text_unit, text_length):
    embed = image_unit.shape[1]
    run = embed // 8

    def body(own_ref, other_ref, image_unit_ref, image_length_ref, pieces_ref, text_unit_ref, text_length_ref, *outs):
        image_ref, text_ref, downs_ref = outs
        up = own_ref[...] + decode_rows(other_ref[:LANES], other_ref[LANES:, :LANES])
        unit = image_unit_ref[...]
        radial = jnp.sum(up * unit, axis=1, keepdims=True)
        image = ((up - unit * radial) / image_length_ref[:, :1]).T.astype(BF)
        up = jnp.zeros((embed, LANES), F32)
        for n in range(8):
            row = pieces_ref[n, embed:].astype(jnp.int32).astype(F32)[:1]
            up = up + from_fixed(pieces_ref[n, :embed], row)
        unit = text_unit_ref[...].T
        radial = jnp.sum(up * unit, axis=0, keepdims=True)
        text = ((up - unit * radial) / text_length_ref[...]).astype(BF)
        image_ref[...] = image
        text_ref[...] = text
        for k in range(8):
            downs_ref[k, :run] = image[k * run : (k + 1) * run]
            downs_ref[k, run:] = text[k * run : (k + 1) * run]

    late = in_hbm(image_own, image_unit, image_length, text_unit)
    image_own, image_unit, image_length, text_unit = late
    args = (image_own, image_other, image_unit, image_length, text_pieces, text_unit, text_length)
    return kernel_call(
        body,
        "transposed_downs",
        (
            pltpu.HBM((embed, LANES), BF),
            pltpu.HBM((embed, LANES), BF),
            pltpu.HBM((8, 2 * run, LANES), BF),
        ),
        grid=(1,),
        in_specs=[whole(a.shape) for a in args],
        out_specs=[whole((embed, LANES)), whole((embed, LANES)), whole((8, 2 * run, LANES))],
        flops=10**7,
        moved_bytes=4 * 2**20,
    )(*args)


def hidden_grads(image_proj, image_turned, text_proj, text_turned):
    image_run, text_run = image_proj.shape[0] // 8, text_proj.shape[0] // 8

    def body(image_proj_ref, image_ref, text_proj_ref, text_ref, out_ref):
        for k in range(8):
            for proj, down, run, first in (
                (image_proj_ref, image_ref, image_run, 0),
                (text_proj_ref, text_ref, text_run, image_run),
            ):
                value = jnp.dot(
                    proj[k * run : (k + 1) * run], down[...], preferred_element_type=F32
                )
                out_ref[k, first : first + run] = value.astype(BF)

    shape = (8, image_run + text_run, LANES)
    args = in_hbm(image_proj, image_turned, text_proj, text_turned)
    return kernel_call(
        body,
        "hidden_grads",
        shaped(shape, BF),
        grid=(1,),
        in_specs=[whole(a.shape) for a in args],
        out_specs=whole(shape),
        flops=5 * 10**8,
        moved_bytes=4 * 2**20,
    )(*args)


def turned_back(grads, image_run):
    text_run = grads.shape[1] - image_run

    def body(grads_ref, image_ref, text_ref):
        for n in range(8):
            at = slice(n * LANES, (n + 1) * LANES)
            image_ref[at] = grads_ref[n, :image_run].astype(F32).T.astype(BF)
            text_ref[:, at] = grads_ref[n, image_run:]

    rows = 8 * LANES
    return kernel_call(
        body,
        "turned_back",
        (shaped((rows, image_run), BF), shaped((text_run, rows), BF)),
        grid=(1,),
        in_specs=[whole(grads.shape)],
        out_specs=[whole((rows, image_run)), whole((text_run, rows))],
        flops=10**6,
        moved_bytes=2**20,
    )(grads)


def weight_sums(place, hidden, text_parts, downs, scalars):
    width = downs.shape[1] // 2
    image_run, text_run = hidden.shape[1] // 16, text_parts[0].shape[0] // 4
    both = image_run + text_run

    def body(place_ref, hidden_ref, *refs):
        text_refs, (downs_ref, scalars_ref, kept_ref, sent_ref) = refs[:4], refs[4:]
        even = place_ref[6] == 0
        downs_all = jnp.concatenate([downs_ref[n] for n in range(8)], axis=1)
        for ref in (kept_ref, sent_ref):
            ref[:, :, both:] = jnp.broadcast_to(scalars_ref[:, both:][None], (8, width, LANES - both))
        for k in range(4):
            first = 2 * k
            image = jnp.dot(
                downs_all[:width],
                hidden_ref[:, k * 4 * image_run : (k + 1) * 4 * image_run],
                preferred_element_type=F32,
            )
            text = lax.dot_general(
                downs_all[width:],
                text_refs[k][...],
                (((1,), (1,)), ((), ())),
                preferred_element_type=F32,
            )
            for value, run, at in ((image, image_run, 0), (text, text_run, image_run)):
                for j in range(2):
                    low = value[:, 2 * j * run : (2 * j + 1) * run]
                    high = value[:, (2 * j + 1) * run : (2 * j + 2) * run]
                    slab = first + j
                    kept_ref[slab, :, at : at + run] = jnp.where(even, low, high)
                    sent_ref[slab, :, at : at + run] = jnp.where(even, high, low)

    shape = (8, width, LANES)
    args = (*in_hbm(hidden, *text_parts), downs, scalars)
    return kernel_call(
        body,
        "weight_sums",
        (shaped(shape, F32),) * 2,
        grid=(1,),
        in_specs=[whole(a.shape) for a in args],
        out_specs=[whole(shape)] * 2,
        prefetch=1,
        flops=10**9,
        moved_bytes=6 * 2**20,
    )(place, *args)


def slabs(place, lines, other_lines, image_run, text_run):
    width = lines.shape[2]
    embed = 8 * width
    both = image_run + text_run

    def body(place_ref, lines_ref, other_ref, image_ref, text_ref, scalars_ref):
        for part, core in ((lines_ref, place_ref[6]), (other_ref, 1 - place_ref[6])):
            def at(i):
                return part[lax.rem(place_ref[2] + 8 - place_ref[4] - i, 4)]

            turned = jnp.concatenate([at(i).reshape(2 * width, LANES) for i in range(4)]).T

            for side in range(2):

                @pl.when(core == side)
                def _():
                    image_ref[side * image_run : (side + 1) * image_run] = turned[:image_run]
                    text_ref[side * text_run : (side + 1) * text_run] = turned[image_run:both]
                    if side == 0:
                        scalars_ref[...] = turned[both : both + 8]

    return kernel_call(
        body,
        "slabs",
        (
            shaped((2 * image_run, embed), F32),
            shaped((2 * text_run, embed), F32),
            shaped((8, embed), F32),
        ),
        grid=(1,),
        in_specs=[whole(lines.shape)] * 2,
        out_specs=[whole((2 * image_run, embed)), whole((2 * text_run, embed)), whole((8, embed))],
        prefetch=1,
        flops=10**6,
        moved_bytes=2**21,
    )(place, lines, other_lines)


def per_device(image_hidden, text_hidden, image_proj, text_proj, log_inverse_sharpness, partner):
    y, zl, c, x, zh = (lax.axis_index(a) for a in AXES)
    branch_pos = x * 2 + zh
    data_pos = (y * 2 + zl) * 2 + c
    group_rows, image_slab = image_hidden.shape
    text_slab = text_hidden.shape[1]
    own_rows = group_rows // 8
    embed = image_proj.shape[1]
    scale = jnp.exp(log_inverse_sharpness)
    first = branch_pos * own_rows
    place = jnp.stack([(1 - c) * group_rows + first, c * group_rows + first, x, zh, y, zl, c])

    image_other, text_local = lax.optimization_barrier(
        (
            swapped(image_hidden, "zh"),
            lax.all_to_all(text_hidden, BRANCH, split_axis=0, concat_axis=1, tiled=True),
        )
    )
    image_pair = jnp.concatenate([image_hidden, image_other], axis=1)

    def from_x(send):
        return [send(0)] + [moved(send(k), ("x",), lambda i, k=k: ((i + k) % 4,)) for k in (3, 2, 1)]

    text_raw = jnp.dot(text_local, text_proj, preferred_element_type=F32)
    text_unit, text_length, text_emb = normalize(text_raw)
    near_text = lax.all_to_all(
        jnp.broadcast_to(text_emb[None], (8, own_rows, embed)), PLANE, 0, 0, tiled=True
    ).reshape(8 * own_rows, embed)
    text_own, _ = lax.optimization_barrier((text_hidden.T, text_local))
    image_parts, text_pair = lax.optimization_barrier(
        (from_x(lambda k: image_pair), jnp.concatenate([text_own, swapped(text_own, "zh")]))
    )
    group_emb, image_turned, hidden, image_unit, image_length = project_group(
        jnp.stack([x, branch_pos, zh]), image_parts, image_proj
    )

    text_parts = from_x(lambda k: text_pair)
    near_text, group_emb, text_parts[1], text_parts[3] = lax.optimization_barrier(
        (near_text, group_emb, text_parts[1], text_parts[3])
    )
    far_text = swapped(near_text, "c")
    near_logits, near_rows, near_cols = half_logits(scale, group_emb, near_text)
    far_logits, far_rows, far_cols = half_logits(scale, group_emb, far_text)

    def joined(mine, theirs):
        peak = jnp.maximum(mine[0], theirs[0])
        mass = mine[1] * jnp.exp(mine[0] - peak) + theirs[1] * jnp.exp(theirs[0] - peak)
        return jnp.stack([peak, mass])

    far_rows, far_cols, text_parts[2] = lax.optimization_barrier((far_rows, far_cols, text_parts[2]))
    row_stats = joined(near_rows.reshape(2, 8, LANES), far_rows.reshape(2, 8, LANES))
    col_stats = jnp.concatenate([near_cols, far_cols], axis=1)
    col_in = swapped(jnp.concatenate([far_cols, near_cols], axis=1), "c")
    row_stats, col_in = lax.optimization_barrier((row_stats, col_in))
    col_stats = joined(col_stats, col_in)

    def along(stats, axis):
        return [moved(stats, (axis,), lambda i, k=k: ((i + k) % 4,)) for k in (1, 3, 2)]

    def joined_four(own, others):
        return joined(joined(own, others[2]), joined(others[0], others[1]))

    row_in, col_in = along(row_stats, "x"), along(col_stats, "y")
    row_stats, col_stats = joined_four(row_stats, row_in), joined_four(col_stats, col_in)
    row_in, col_in = swapped(row_stats, "zh"), swapped(col_stats, "zl")
    row_stats, col_stats = joined(row_stats, row_in), joined(col_stats, col_in)
    row_lse = row_stats[0] + jnp.log(row_stats[1])
    col_lse = col_stats[0] + jnp.log(col_stats[1])

    row_partner = lax.dynamic_slice_in_dim(partner, data_pos * group_rows, group_rows, 0)
    row_partner = lax.optimization_barrier(row_partner.astype(F32).reshape(8, LANES))
    near_lse, far_lse = col_lse[None, :group_rows], col_lse[None, group_rows:]
    far_low, far_part, far_terms = far_weights(
        place, scale, far_logits, row_lse, far_lse, row_partner, image_turned
    )
    text_arrived = swapped(far_part, "c")
    near_low, near_terms, *image_coded = near_weights(
        place, scale, near_logits, row_lse, near_lse, row_partner, far_low, near_text, far_text
    )
    image_ring = from_x(lambda k: image_coded[k])
    text_coded = near_text_sum(scale, near_low, image_turned, text_arrived)
    text_pieces = lax.all_to_all(text_coded, PLANE, 0, 0, tiled=True)
    image_own, image_other = pair_sums(place, image_ring)
    image_down, text_down, downs = transposed_downs(
        image_own,
        swapped(image_other, "zh"),
        image_unit,
        image_length,
        text_pieces,
        text_unit,
        text_length.reshape(1, own_rows),
    )
    downs, grads = lax.optimization_barrier(
        (
            lax.all_to_all(downs, BRANCH, 0, 0, tiled=True),
            hidden_grads(image_proj, image_down, text_proj, text_down),
        )
    )
    grads = lax.all_to_all(grads, BRANCH, 0, 0, tiled=True)
    grad_image_hidden, grad_text_hidden = turned_back(grads, image_slab)

    terms = jnp.sum(far_terms + near_terms, axis=1)
    own_row_terms = lax.dynamic_index_in_dim(row_lse, branch_pos, 0)
    own_col_terms = lax.dynamic_slice_in_dim(col_lse, (y * 2 + zl) * own_rows, own_rows, 0)
    loss_part = jnp.sum(own_row_terms) + jnp.sum(own_col_terms) - 2.0 * terms[1]
    width = embed // 8
    scalars = jnp.stack([loss_part / DENOMINATOR, terms[0]])
    image_rows, text_rows = image_slab // 2, text_slab // 2
    both = image_rows + text_rows
    scalars = jnp.pad(scalars[None], ((0, width - 1), (both, LANES - both - 2)))
    kept, sent = weight_sums(place, hidden, text_parts, downs, scalars)
    partial = kept + swapped(sent, "c")
    summed = jnp.sum(lax.all_to_all(partial, PLANE, 0, 0, tiled=True), axis=0)
    own, other = (
        moved(summed, AXES, lambda a, b, core, d, e, h=h: (a, b ^ h, core, (d + a) % 4, e ^ b))
        for h in (0, 1)
    )
    line = stacked(own[None], other[None], jnp.bitwise_xor(zl, zh))
    lines = jnp.stack(
        [line] + [moved(line, ("y",), lambda i, k=k: ((i + k) % 4,)) for k in (3, 2, 1)]
    )
    grad_image_proj, grad_text_proj, totals = slabs(
        place, lines, swapped(lines, "c"), image_rows, text_rows
    )
    totals = jnp.sum(totals.reshape(8, 8, width)[:, :, 0], axis=1)
    return (
        totals[0].reshape(1),
        totals[1].reshape(1),
        grad_image_hidden,
        grad_text_hidden.T,
        grad_image_proj,
        grad_text_proj,
    )


def solution(mesh):
    torus = Mesh(mesh.devices.reshape(tuple(SIZES.values())), AXES)
    placed = (P(DP, BRANCH), P(DP, BRANCH), P(), P(), P(), P())
    return jax.shard_map(
        per_device,
        mesh=torus,
        in_specs=placed,
        out_specs=(P(), P(), P(DP, BRANCH), P(DP, BRANCH), P(BRANCH, None), P(BRANCH, None)),
        check_vma=False,
    )
```

```python
import jax
import jax.numpy as jnp
import numpy as np
from jax import lax
from jax.experimental import pallas as pl
from jax.experimental.pallas import tpu as pltpu
from jax.sharding import Mesh
from jax.sharding import PartitionSpec as P

SIZES = {"y": 4, "zl": 2, "c": 2, "x": 4, "zh": 2}
AXES = tuple(SIZES)
DP = ("y", "zl", "c")
PLANE = ("y", "zl")
BRANCH = ("x", "zh")

NORM_EPSILON = 1e-06
FULL_SCALE = 32000.0
DENOMINATOR = 32768.0
LOW = -1e30
LANES = 128
TAIL = 16
RUN = 2048
BF = jnp.bfloat16
F32 = jnp.float32


def moved(value, axes, target):
    sizes = [SIZES[a] for a in axes]
    pairs = []
    for i in range(int(np.prod(sizes))):
        at = tuple(int(v) for v in np.unravel_index(i, sizes))
        pairs.append((i, int(np.ravel_multi_index(target(*at), sizes))))
    return lax.ppermute(value, axes, pairs)


def swapped(value, axis, mask=1):
    return moved(value, (axis,), lambda i: (i ^ mask,))


def stacked(own, other, side):
    return jnp.where(side == 0, jnp.concatenate([own, other]), jnp.concatenate([other, own]))


def normalize(raw_rows):
    lengths = jnp.sqrt(jnp.sum(raw_rows * raw_rows, axis=1, keepdims=True) + NORM_EPSILON)
    unit_rows = raw_rows / lengths
    return (unit_rows, lengths, unit_rows.astype(BF))


def eye():
    row = lax.broadcasted_iota(jnp.int32, (LANES, LANES), 0)
    return row == lax.broadcasted_iota(jnp.int32, (LANES, LANES), 1)


def as_row(column):
    return jnp.sum(jnp.where(eye(), column, 0.0), axis=0, keepdims=True)


def as_column(row):
    return jnp.sum(jnp.where(eye(), row, 0.0), axis=1, keepdims=True)


def exponent_of(top):
    return jnp.maximum(jnp.ceil(jnp.log2(top)), -80.0)


def to_fixed(values, exponent):
    return jnp.round(values * (FULL_SCALE * jnp.exp2(-exponent))).astype(jnp.int32).astype(jnp.int16)


def from_fixed(fixed, exponent):
    return fixed.astype(jnp.int32).astype(F32) * (jnp.exp2(exponent) / FULL_SCALE)


def tail(row):
    return jnp.broadcast_to(row, (TAIL, row.shape[1])).astype(jnp.int32).astype(jnp.int16)


def code_rows(values):
    exponent = exponent_of(jnp.max(jnp.abs(values), axis=1, keepdims=True))
    return to_fixed(values, exponent), tail(as_row(exponent))


def decode_rows(fixed, exponents):
    row = exponents.astype(jnp.int32).astype(F32)[:1]
    return from_fixed(fixed, as_column(row))


def kernel_call(body, name, out_shape, grid=(), in_specs=None, out_specs=None, scratch=(), prefetch=0, flops=0, moved_bytes=0):
    spec = pltpu.PrefetchScalarGridSpec(
        num_scalar_prefetch=prefetch,
        grid=grid,
        in_specs=in_specs,
        out_specs=out_specs,
        scratch_shapes=scratch,
    )
    return pl.pallas_call(
        body,
        out_shape=out_shape,
        grid_spec=spec,
        name=name,
        compiler_params=pltpu.CompilerParams(vmem_limit_bytes=18 * 2**20),
        cost_estimate=pl.CostEstimate(flops=flops, bytes_accessed=moved_bytes, transcendentals=0),
    )


def in_hbm(*arrays):
    return [pltpu.with_memory_space_constraint(a, pltpu.HBM) for a in arrays]


def whole(shape):
    return pl.BlockSpec(shape, lambda *_: (0,) * len(shape))


def shaped(shape, dtype):
    return jax.ShapeDtypeStruct(shape, dtype)


def project_group(place, parts, proj):
    rows, width = parts[0].shape
    embed = proj.shape[1]
    step = 256

    def body(place_ref, a, b, c, d, proj_ref, emb_ref, turned_ref, hidden_ref, unit_ref, length_ref):
        i = pl.program_id(0)
        raw = None
        for k, part in enumerate((a, b, c, d)):
            slab = 2 * lax.rem(place_ref[0] + k, 4)
            rows_of = [
                proj_ref[pl.ds(pl.multiple_of((slab + z) * (width // 2), width // 2), width // 2), :]
                for z in (place_ref[2], 1 - place_ref[2])
            ]
            term = jnp.dot(
                part[...], jnp.concatenate(rows_of, axis=0), preferred_element_type=F32
            )
            raw = term if raw is None else raw + term
            hidden_ref[:, k * width : (k + 1) * width] = part[...]
        length = jnp.sqrt(jnp.sum(raw * raw, axis=1, keepdims=True) + NORM_EPSILON)
        unit = raw / length
        emb_ref[...] = unit.astype(BF)
        turned_ref[...] = unit.T.astype(BF)
        for h in range(step // LANES):

            @pl.when(place_ref[1] == i * (step // LANES) + h)
            def _():
                unit_ref[...] = unit[h * LANES : (h + 1) * LANES]
                length_ref[...] = jnp.broadcast_to(
                    length[h * LANES : (h + 1) * LANES], (LANES, LANES)
                )

    return kernel_call(
        body,
        "project_group",
        (
            pltpu.HBM((rows, embed), BF),
            pltpu.HBM((embed, rows), BF),
            pltpu.HBM((rows, 4 * width), BF),
            pltpu.HBM((LANES, embed), F32),
            pltpu.HBM((LANES, LANES), F32),
        ),
        grid=(rows // step,),
        in_specs=[pl.BlockSpec((step, width), lambda i, *_: (i, 0))] * 4 + [whole(proj.shape)],
        out_specs=[
            pl.BlockSpec((step, embed), lambda i, *_: (i, 0)),
            pl.BlockSpec((embed, step), lambda i, *_: (0, i)),
            pl.BlockSpec((step, 4 * width), lambda i, *_: (i, 0)),
            whole((LANES, embed)),
            whole((LANES, LANES)),
        ],
        prefetch=1,
        flops=4 * 10**10,
        moved_bytes=6 * 2**20,
    )(place, *parts, proj)


def half_logits(scale, image_emb, text_emb):
    rows, embed = image_emb.shape
    columns = text_emb.shape[0]
    width, step = 512, 256

    def body(scale_ref, image_ref, text_ref, logits_ref, rows_ref, cols_ref, peak_ref, mass_ref):
        j = pl.program_id(0)

        @pl.when(j == 0)
        def _():
            peak_ref[...] = jnp.full(peak_ref.shape, LOW, F32)
            mass_ref[...] = jnp.zeros(mass_ref.shape, F32)

        col_peak = jnp.full((1, width), LOW, F32)
        col_mass = jnp.zeros((1, width), F32)
        for r in range(rows // step):
            at = slice(r * step, (r + 1) * step)
            value = scale_ref[0] * lax.dot_general(
                image_ref[at], text_ref[...], (((1,), (1,)), ((), ())), preferred_element_type=F32
            )
            logits_ref[at] = value
            tiles = [value[:, t : t + LANES] for t in range(0, width, LANES)]
            old = peak_ref[at]
            peak = old
            for tile in tiles:
                peak = jnp.maximum(peak, tile)
            mass = mass_ref[at] * jnp.exp(old - peak)
            for tile in tiles:
                mass = mass + jnp.exp(tile - peak)
            peak_ref[at] = peak
            mass_ref[at] = mass
            top = jnp.maximum(col_peak, jnp.max(value, axis=0, keepdims=True))
            col_mass = col_mass * jnp.exp(col_peak - top) + jnp.sum(
                jnp.exp(value - top), axis=0, keepdims=True
            )
            col_peak = top
        cols_ref[0:1] = col_peak
        cols_ref[1:2] = col_mass

        @pl.when(j == pl.num_programs(0) - 1)
        def _():
            for r in range(rows // LANES):
                at = slice(r * LANES, (r + 1) * LANES)
                peak = jnp.max(peak_ref[at], axis=1, keepdims=True)
                mass = jnp.sum(
                    mass_ref[at] * jnp.exp(peak_ref[at] - peak), axis=1, keepdims=True
                )
                rows_ref[r : r + 1] = as_row(peak)
                rows_ref[8 + r : 9 + r] = as_row(mass)

    return kernel_call(
        body,
        "half_logits",
        (shaped((rows, columns), F32), shaped((16, LANES), F32), shaped((2, columns), F32)),
        grid=(columns // width,),
        in_specs=[
            pl.BlockSpec(memory_space=pltpu.SMEM),
            whole(image_emb.shape),
            pl.BlockSpec((width, embed), lambda j: (j, 0)),
        ],
        out_specs=[
            pl.BlockSpec((rows, width), lambda j: (0, j)),
            whole((16, LANES)),
            pl.BlockSpec((2, width), lambda j: (0, j)),
        ],
        scratch=[pltpu.VMEM((rows, LANES), F32)] * 2,
        flops=2 * rows * columns * embed,
        moved_bytes=8 * 2**20,
    )(scale, image_emb, text_emb)


def weigh(logits, row_lse, col_lse, partner, first_id):
    rows, columns = logits.shape
    lane = lax.broadcasted_iota(jnp.int32, (1, LANES), 1)
    weights = []
    for t in range(columns // LANES):
        at = slice(t * LANES, (t + 1) * LANES)
        value = logits[:, at]
        matched = partner == lane + first_id(t)
        weight = jnp.exp(value - row_lse) + jnp.exp(value - col_lse[:, at])
        weight = (weight - jnp.where(matched, 2.0, 0.0)) * (1.0 / DENOMINATOR)
        scale_term = jnp.sum(weight * value, axis=0, keepdims=True)
        positive = jnp.sum(jnp.where(matched, value, 0.0), axis=0, keepdims=True)
        weights.append((weight.astype(BF), scale_term, positive))
    return weights


def columns_of(rows_ref, first, count):
    return jnp.concatenate(
        [as_column(rows_ref[first + r : first + r + 1]) for r in range(count)], axis=0
    )


def far_weights(place, scale, logits, row_lse, col_lse, partner, image_turned):
    rows, columns = logits.shape
    embed = image_turned.shape[0]
    width = 256

    def body(place_ref, scale_ref, logits_ref, row_ref, col_ref, partner_ref, turned_ref, low_ref, text_ref, terms_ref):
        j = pl.program_id(0)
        sums = [jnp.zeros((1, LANES), F32)] * 2
        for r in range(0, rows, 256):
            at = slice(r, r + 256)
            row = columns_of(row_ref, r // LANES, 2)
            part = columns_of(partner_ref, r // LANES, 2).astype(jnp.int32)
            made = weigh(
                logits_ref[at], row, col_ref[...], part, lambda t: place_ref[0] + (2 * j + t) * RUN
            )
            for t, (low, scale_term, positive) in enumerate(made):
                low_ref[at, t * LANES : (t + 1) * LANES] = low
                sums = [sums[0] + scale_term, sums[1] + positive]
        text_ref[...] = scale_ref[0] * jnp.dot(
            turned_ref[...], low_ref[...], preferred_element_type=F32
        )

        @pl.when(j == 0)
        def _():
            terms_ref[...] = jnp.zeros(terms_ref.shape, F32)

        terms_ref[0:1] += sums[0]
        terms_ref[1:2] += sums[1]

    return kernel_call(
        body,
        "far_weights",
        (
            shaped((rows, columns), BF),
            shaped((embed, columns), F32),
            shaped((8, LANES), F32),
        ),
        grid=(columns // width,),
        in_specs=[
            pl.BlockSpec(memory_space=pltpu.SMEM),
            pl.BlockSpec((rows, width), lambda j, *_: (0, j)),
            whole(row_lse.shape),
            pl.BlockSpec((1, width), lambda j, *_: (0, j)),
            whole(partner.shape),
            whole(image_turned.shape),
        ],
        out_specs=[
            pl.BlockSpec((rows, width), lambda j, *_: (0, j)),
            pl.BlockSpec((embed, width), lambda j, *_: (0, j)),
            whole((8, LANES)),
        ],
        prefetch=1,
        flops=10**8,
        moved_bytes=8 * 2**20,
    )(place, scale, logits, row_lse, col_lse, partner, image_turned)


def near_weights(place, scale, logits, row_lse, col_lse, partner, far_low, near_emb, far_emb):
    rows, columns = logits.shape
    embed = near_emb.shape[1]
    step = 256

    def body(place_ref, scale_ref, logits_ref, row_ref, col_ref, partner_ref, far_ref, near_emb_ref, far_emb_ref, *outs):
        low_ref, terms_ref, *coded_refs = outs
        k = pl.program_id(0)
        row = columns_of(row_ref, 0, 2)
        part = columns_of(partner_ref, 0, 2).astype(jnp.int32)
        made = weigh(logits_ref[...], row, col_ref[...], part, lambda t: place_ref[1] + t * RUN)
        sums = [jnp.zeros((1, LANES), F32)] * 2
        for t, (low, scale_term, positive) in enumerate(made):
            low_ref[:, t * LANES : (t + 1) * LANES] = low
            sums = [sums[0] + scale_term, sums[1] + positive]

        @pl.when(k == 0)
        def _():
            terms_ref[...] = jnp.zeros(terms_ref.shape, F32)

        terms_ref[0:1] += sums[0]
        terms_ref[1:2] += sums[1]
        image = jnp.dot(low_ref[...], near_emb_ref[...], preferred_element_type=F32)
        image = image + jnp.dot(far_ref[...], far_emb_ref[...], preferred_element_type=F32)
        image = scale_ref[0] * image
        coded = [code_rows(image[:LANES]), code_rows(image[LANES:])]
        for i in range(4):

            @pl.when(k == i)
            def _():
                for h in range(2):
                    fixed, exponents = coded[h]
                    coded_refs[i][h, :LANES] = fixed
                    coded_refs[i][h, LANES:] = jnp.zeros((TAIL, embed), jnp.int16)
                    coded_refs[i][h, LANES:, :LANES] = exponents

    def rows_at(k, place_ref):
        return lax.rem(place_ref[2] + k, 4)

    piece = (2, LANES + TAIL, embed)
    return kernel_call(
        body,
        "near_weights",
        (
            shaped((rows, columns), BF),
            shaped((8, LANES), F32),
            *[pltpu.HBM(piece, jnp.int16)] * 4,
        ),
        grid=(4,),
        in_specs=[
            pl.BlockSpec(memory_space=pltpu.SMEM),
            pl.BlockSpec((step, columns), lambda k, p: (rows_at(k, p), 0)),
            pl.BlockSpec((None, 2, LANES), lambda k, p: (rows_at(k, p), 0, 0)),
            whole(col_lse.shape),
            pl.BlockSpec((None, 2, LANES), lambda k, p: (rows_at(k, p), 0, 0)),
            pl.BlockSpec((step, columns), lambda k, p: (rows_at(k, p), 0)),
            whole(near_emb.shape),
            whole(far_emb.shape),
        ],
        out_specs=[
            pl.BlockSpec((step, columns), lambda k, p: (rows_at(k, p), 0)),
            whole((8, LANES)),
            *[whole(piece)] * 4,
        ],
        prefetch=1,
        flops=10**8,
        moved_bytes=10 * 2**20,
    )(place, scale, logits, row_lse.reshape(4, 2, LANES), col_lse, partner.reshape(4, 2, LANES), far_low, near_emb, far_emb)


def near_text_sum(scale, low, image_turned, arrived):
    embed, columns = arrived.shape
    rows = low.shape[0]
    width = 256

    def body(scale_ref, low_ref, turned_ref, arrived_ref, out_ref):
        text = scale_ref[0] * jnp.dot(turned_ref[...], low_ref[...], preferred_element_type=F32)
        text = text + arrived_ref[...]
        exponent = exponent_of(jnp.max(jnp.abs(text), axis=0, keepdims=True))
        fixed = to_fixed(text, exponent)
        last = tail(exponent)
        for h in range(width // LANES):
            at = slice(h * LANES, (h + 1) * LANES)
            out_ref[h, :embed] = fixed[:, at]
            out_ref[h, embed:] = last[:, at]

    return kernel_call(
        body,
        "near_text_sum",
        pltpu.HBM((columns // LANES, embed + TAIL, LANES), jnp.int16),
        grid=(columns // width,),
        in_specs=[
            pl.BlockSpec(memory_space=pltpu.SMEM),
            pl.BlockSpec((rows, width), lambda j: (0, j)),
            whole(image_turned.shape),
            pl.BlockSpec((embed, width), lambda j: (0, j)),
        ],
        out_specs=pl.BlockSpec((width // LANES, embed + TAIL, LANES), lambda j: (j, 0, 0)),
        flops=2 * 10**10,
        moved_bytes=8 * 2**20,
    )(scale, low, image_turned, arrived)


def pair_sums(place, pieces):
    embed = pieces[0].shape[-1]

    def body(place_ref, a, b, c, d, own_ref, other_ref):
        def total(h):
            parts = [decode_rows(p[h, :LANES], p[h, LANES:, :LANES]) for p in (a, b, c, d)]
            return (parts[0] + parts[1]) + (parts[2] + parts[3])

        own_ref[...] = total(place_ref[3])
        fixed, exponents = code_rows(total(1 - place_ref[3]))
        other_ref[:LANES] = fixed
        other_ref[LANES:] = jnp.zeros((TAIL, embed), jnp.int16)
        other_ref[LANES:, :LANES] = exponents

    return kernel_call(
        body,
        "pair_sums",
        (pltpu.HBM((LANES, embed), F32), pltpu.HBM((LANES + TAIL, embed), jnp.int16)),
        grid=(1,),
        in_specs=[whole(pieces[0].shape)] * 4,
        out_specs=[whole((LANES, embed)), whole((LANES + TAIL, embed))],
        prefetch=1,
        flops=4 * 10**10,
        moved_bytes=3 * 2**20,
    )(place, *pieces)


def transposed_downs(image_own, image_other, image_unit, image_length, text_pieces, text_unit, text_length):
    embed = image_unit.shape[1]
    run = embed // 8

    def body(own_ref, other_ref, image_unit_ref, image_length_ref, pieces_ref, text_unit_ref, text_length_ref, *outs):
        image_ref, text_ref, downs_ref = outs
        up = own_ref[...] + decode_rows(other_ref[:LANES], other_ref[LANES:, :LANES])
        unit = image_unit_ref[...]
        radial = jnp.sum(up * unit, axis=1, keepdims=True)
        image = ((up - unit * radial) / image_length_ref[:, :1]).T.astype(BF)
        up = jnp.zeros((embed, LANES), F32)
        for n in range(8):
            row = pieces_ref[n, embed:].astype(jnp.int32).astype(F32)[:1]
            up = up + from_fixed(pieces_ref[n, :embed], row)
        unit = text_unit_ref[...].T
        radial = jnp.sum(up * unit, axis=0, keepdims=True)
        text = ((up - unit * radial) / text_length_ref[...]).astype(BF)
        image_ref[...] = image
        text_ref[...] = text
        for k in range(8):
            downs_ref[k, :run] = image[k * run : (k + 1) * run]
            downs_ref[k, run:] = text[k * run : (k + 1) * run]

    late = in_hbm(image_own, image_unit, image_length, text_unit)
    image_own, image_unit, image_length, text_unit = late
    args = (image_own, image_other, image_unit, image_length, text_pieces, text_unit, text_length)
    return kernel_call(
        body,
        "transposed_downs",
        (
            pltpu.HBM((embed, LANES), BF),
            pltpu.HBM((embed, LANES), BF),
            pltpu.HBM((8, 2 * run, LANES), BF),
        ),
        grid=(1,),
        in_specs=[whole(a.shape) for a in args],
        out_specs=[whole((embed, LANES)), whole((embed, LANES)), whole((8, 2 * run, LANES))],
        flops=10**7,
        moved_bytes=4 * 2**20,
    )(*args)


def hidden_grads(image_proj, image_turned, text_proj, text_turned):
    image_run, text_run = image_proj.shape[0] // 8, text_proj.shape[0] // 8

    def body(image_proj_ref, image_ref, text_proj_ref, text_ref, out_ref):
        for k in range(8):
            for proj, down, run, first in (
                (image_proj_ref, image_ref, image_run, 0),
                (text_proj_ref, text_ref, text_run, image_run),
            ):
                value = jnp.dot(
                    proj[k * run : (k + 1) * run], down[...], preferred_element_type=F32
                )
                out_ref[k, first : first + run] = value.astype(BF)

    shape = (8, image_run + text_run, LANES)
    args = in_hbm(image_proj, image_turned, text_proj, text_turned)
    return kernel_call(
        body,
        "hidden_grads",
        shaped(shape, BF),
        grid=(1,),
        in_specs=[whole(a.shape) for a in args],
        out_specs=whole(shape),
        flops=5 * 10**8,
        moved_bytes=4 * 2**20,
    )(*args)


def turned_back(grads, image_run):
    text_run = grads.shape[1] - image_run

    def body(grads_ref, image_ref, text_ref):
        for n in range(8):
            at = slice(n * LANES, (n + 1) * LANES)
            image_ref[at] = grads_ref[n, :image_run].astype(F32).T.astype(BF)
            text_ref[:, at] = grads_ref[n, image_run:]

    rows = 8 * LANES
    return kernel_call(
        body,
        "turned_back",
        (shaped((rows, image_run), BF), shaped((text_run, rows), BF)),
        grid=(1,),
        in_specs=[whole(grads.shape)],
        out_specs=[whole((rows, image_run)), whole((text_run, rows))],
        flops=10**6,
        moved_bytes=2**20,
    )(grads)


def weight_sums(place, hidden, text_parts, downs, scalars):
    width = downs.shape[1] // 2
    image_run, text_run = hidden.shape[1] // 16, text_parts[0].shape[0] // 4
    both = image_run + text_run

    def body(place_ref, hidden_ref, *refs):
        text_refs, (downs_ref, scalars_ref, kept_ref, sent_ref) = refs[:4], refs[4:]
        even = place_ref[6] == 0
        downs_all = jnp.concatenate([downs_ref[n] for n in range(8)], axis=1)
        for ref in (kept_ref, sent_ref):
            ref[:, :, both:] = jnp.broadcast_to(scalars_ref[:, both:][None], (8, width, LANES - both))
        for k in range(4):
            first = 2 * k
            image = jnp.dot(
                downs_all[:width],
                hidden_ref[:, k * 4 * image_run : (k + 1) * 4 * image_run],
                preferred_element_type=F32,
            )
            text = lax.dot_general(
                downs_all[width:],
                text_refs[k][...],
                (((1,), (1,)), ((), ())),
                preferred_element_type=F32,
            )
            for value, run, at in ((image, image_run, 0), (text, text_run, image_run)):
                for j in range(2):
                    low = value[:, 2 * j * run : (2 * j + 1) * run]
                    high = value[:, (2 * j + 1) * run : (2 * j + 2) * run]
                    slab = first + j
                    kept_ref[slab, :, at : at + run] = jnp.where(even, low, high)
                    sent_ref[slab, :, at : at + run] = jnp.where(even, high, low)

    shape = (8, width, LANES)
    args = (*in_hbm(hidden, *text_parts), downs, scalars)
    return kernel_call(
        body,
        "weight_sums",
        (shaped(shape, F32),) * 2,
        grid=(1,),
        in_specs=[whole(a.shape) for a in args],
        out_specs=[whole(shape)] * 2,
        prefetch=1,
        flops=10**9,
        moved_bytes=6 * 2**20,
    )(place, *args)


def slabs(place, lines, other_lines, image_run, text_run):
    width = lines.shape[2]
    embed = 8 * width
    both = image_run + text_run

    def body(place_ref, lines_ref, other_ref, image_ref, text_ref, scalars_ref):
        for part, core in ((lines_ref, place_ref[6]), (other_ref, 1 - place_ref[6])):
            def at(i):
                return part[lax.rem(place_ref[2] + 8 - place_ref[4] - i, 4)]

            turned = jnp.concatenate([at(i).reshape(2 * width, LANES) for i in range(4)]).T

            for side in range(2):

                @pl.when(core == side)
                def _():
                    image_ref[side * image_run : (side + 1) * image_run] = turned[:image_run]
                    text_ref[side * text_run : (side + 1) * text_run] = turned[image_run:both]
                    if side == 0:
                        scalars_ref[...] = turned[both : both + 8]

    return kernel_call(
        body,
        "slabs",
        (
            shaped((2 * image_run, embed), F32),
            shaped((2 * text_run, embed), F32),
            shaped((8, embed), F32),
        ),
        grid=(1,),
        in_specs=[whole(lines.shape)] * 2,
        out_specs=[whole((2 * image_run, embed)), whole((2 * text_run, embed)), whole((8, embed))],
        prefetch=1,
        flops=10**6,
        moved_bytes=2**21,
    )(place, lines, other_lines)


def per_device(image_hidden, text_hidden, image_proj, text_proj, log_inverse_sharpness, partner):
    y, zl, c, x, zh = (lax.axis_index(a) for a in AXES)
    branch_pos = x * 2 + zh
    data_pos = (y * 2 + zl) * 2 + c
    group_rows, image_slab = image_hidden.shape
    text_slab = text_hidden.shape[1]
    own_rows = group_rows // 8
    embed = image_proj.shape[1]
    scale = jnp.exp(log_inverse_sharpness)
    first = branch_pos * own_rows
    place = jnp.stack([(1 - c) * group_rows + first, c * group_rows + first, x, zh, y, zl, c])

    image_other, text_local = lax.optimization_barrier(
        (
            swapped(image_hidden, "zh"),
            lax.all_to_all(text_hidden, BRANCH, split_axis=0, concat_axis=1, tiled=True),
        )
    )
    image_pair = jnp.concatenate([image_hidden, image_other], axis=1)

    def from_x(send):
        return [send(0)] + [moved(send(k), ("x",), lambda i, k=k: ((i + k) % 4,)) for k in (3, 2, 1)]

    text_raw = jnp.dot(text_local, text_proj, preferred_element_type=F32)
    text_unit, text_length, text_emb = normalize(text_raw)
    near_text = lax.all_to_all(
        jnp.broadcast_to(text_emb[None], (8, own_rows, embed)), PLANE, 0, 0, tiled=True
    ).reshape(8 * own_rows, embed)
    text_own, _ = lax.optimization_barrier((text_hidden.T, text_local))
    image_parts, text_pair = lax.optimization_barrier(
        (from_x(lambda k: image_pair), jnp.concatenate([text_own, swapped(text_own, "zh")]))
    )
    group_emb, image_turned, hidden, image_unit, image_length = project_group(
        jnp.stack([x, branch_pos, zh]), image_parts, image_proj
    )

    text_parts = from_x(lambda k: text_pair)
    near_text, group_emb, text_parts[1], text_parts[3] = lax.optimization_barrier(
        (near_text, group_emb, text_parts[1], text_parts[3])
    )
    far_text = swapped(near_text, "c")
    near_logits, near_rows, near_cols = half_logits(scale, group_emb, near_text)
    far_logits, far_rows, far_cols = half_logits(scale, group_emb, far_text)

    def joined(mine, theirs):
        peak = jnp.maximum(mine[0], theirs[0])
        mass = mine[1] * jnp.exp(mine[0] - peak) + theirs[1] * jnp.exp(theirs[0] - peak)
        return jnp.stack([peak, mass])

    far_rows, far_cols, text_parts[2] = lax.optimization_barrier((far_rows, far_cols, text_parts[2]))
    row_stats = joined(near_rows.reshape(2, 8, LANES), far_rows.reshape(2, 8, LANES))
    col_stats = jnp.concatenate([near_cols, far_cols], axis=1)
    col_in = swapped(jnp.concatenate([far_cols, near_cols], axis=1), "c")
    row_stats, col_in = lax.optimization_barrier((row_stats, col_in))
    col_stats = joined(col_stats, col_in)

    def along(stats, axis):
        return [moved(stats, (axis,), lambda i, k=k: ((i + k) % 4,)) for k in (1, 3, 2)]

    def joined_four(own, others):
        return joined(joined(own, others[2]), joined(others[0], others[1]))

    row_in, col_in = along(row_stats, "x"), along(col_stats, "y")
    row_stats, col_stats = joined_four(row_stats, row_in), joined_four(col_stats, col_in)
    row_in, col_in = swapped(row_stats, "zh"), swapped(col_stats, "zl")
    row_stats, col_stats = joined(row_stats, row_in), joined(col_stats, col_in)
    row_lse = row_stats[0] + jnp.log(row_stats[1])
    col_lse = col_stats[0] + jnp.log(col_stats[1])

    row_partner = lax.dynamic_slice_in_dim(partner, data_pos * group_rows, group_rows, 0)
    row_partner = lax.optimization_barrier(row_partner.astype(F32).reshape(8, LANES))
    near_lse, far_lse = col_lse[None, :group_rows], col_lse[None, group_rows:]
    far_low, far_part, far_terms = far_weights(
        place, scale, far_logits, row_lse, far_lse, row_partner, image_turned
    )
    text_arrived = swapped(far_part, "c")
    near_low, near_terms, *image_coded = near_weights(
        place, scale, near_logits, row_lse, near_lse, row_partner, far_low, near_text, far_text
    )
    image_ring = from_x(lambda k: image_coded[k])
    text_coded = near_text_sum(scale, near_low, image_turned, text_arrived)
    text_pieces = lax.all_to_all(text_coded, PLANE, 0, 0, tiled=True)
    image_own, image_other = pair_sums(place, image_ring)
    image_down, text_down, downs = transposed_downs(
        image_own,
        swapped(image_other, "zh"),
        image_unit,
        image_length,
        text_pieces,
        text_unit,
        text_length.reshape(1, own_rows),
    )
    downs, grads = lax.optimization_barrier(
        (
            lax.all_to_all(downs, BRANCH, 0, 0, tiled=True),
            hidden_grads(image_proj, image_down, text_proj, text_down),
        )
    )
    grads = lax.all_to_all(grads, BRANCH, 0, 0, tiled=True)
    grad_image_hidden, grad_text_hidden = turned_back(grads, image_slab)

    terms = jnp.sum(far_terms + near_terms, axis=1)
    own_row_terms = lax.dynamic_index_in_dim(row_lse, branch_pos, 0)
    own_col_terms = lax.dynamic_slice_in_dim(col_lse, (y * 2 + zl) * own_rows, own_rows, 0)
    loss_part = jnp.sum(own_row_terms) + jnp.sum(own_col_terms) - 2.0 * terms[1]
    width = embed // 8
    scalars = jnp.stack([loss_part / DENOMINATOR, terms[0]])
    image_rows, text_rows = image_slab // 2, text_slab // 2
    both = image_rows + text_rows
    scalars = jnp.pad(scalars[None], ((0, width - 1), (both, LANES - both - 2)))
    kept, sent = weight_sums(place, hidden, text_parts, downs, scalars)
    partial = kept + swapped(sent, "c")
    summed = jnp.sum(lax.all_to_all(partial, PLANE, 0, 0, tiled=True), axis=0)
    own, other = (
        moved(summed, AXES, lambda a, b, core, d, e, h=h: (a, b ^ h, core, (d + a) % 4, e ^ b))
        for h in (0, 1)
    )
    line = stacked(own[None], other[None], jnp.bitwise_xor(zl, zh))
    lines = jnp.stack(
        [line] + [moved(line, ("y",), lambda i, k=k: ((i + k) % 4,)) for k in (3, 2, 1)]
    )
    grad_image_proj, grad_text_proj, totals = slabs(
        place, lines, swapped(lines, "c"), image_rows, text_rows
    )
    totals = jnp.sum(totals.reshape(8, 8, width)[:, :, 0], axis=1)
    return (
        totals[0].reshape(1),
        totals[1].reshape(1),
        grad_image_hidden,
        grad_text_hidden.T,
        grad_image_proj,
        grad_text_proj,
    )


def solution(mesh):
    torus = Mesh(mesh.devices.reshape(tuple(SIZES.values())), AXES)
    placed = (P(DP, BRANCH), P(DP, BRANCH), P(), P(), P(), P())
    return jax.shard_map(
        per_device,
        mesh=torus,
        in_specs=placed,
        out_specs=(P(), P(), P(DP, BRANCH), P(DP, BRANCH), P(BRANCH, None), P(BRANCH, None)),
        check_vma=False,
    )
```
